32 devices in a mesh: ctx: 16 (over z, y, core), exp: 2 (over x).
Axes of the slice: x: 2, y: 2, z: 4, core: 2. Of those that a mesh axis runs over, the one named last changes fastest.
Arguments:
- query: bfloat16 [2, 2048, 2048], P('exp', 'ctx'), may hold values from -12 to 12
- key: bfloat16 [2, 2048, 2048], P('exp', 'ctx'), may hold values from -6 to 6
- value: bfloat16 [2, 2048, 2048], P('exp', 'ctx'), may hold values from -12 to 12
- cotangent: bfloat16 [2, 2048, 2048], P('exp', 'ctx'), may hold values from -6 to 6
- route_ids: int32 [2, 2048, 1], P('exp', 'ctx'), may hold values from 0 to 1; in each aligned block of 128 rows (0 to 127, 128 to 255, ..., all dimensions but the last counted through in order) at most 128 rows name the same one
- route_weights: float32 [2, 2048, 1], P('exp', 'ctx'), may hold values from 0.2 to 1
- block_mask: int32 [2, 16, 3], P('exp', 'ctx'), may hold values 0 or 1
- w_gate: bfloat16 [2, 2048, 512], P('exp'), may hold values from -0.125 to 0.125
- w_up: bfloat16 [2, 2048, 512], P('exp'), may hold values from -0.125 to 0.125
- w_down: bfloat16 [2, 512, 2048], P('exp'), may hold values from -0.25 to 0.25
Outputs:
- layer_out: bfloat16 [2, 2048, 2048], P('exp', 'ctx')
- grad_query: bfloat16 [2, 2048, 2048], P('exp', 'ctx')
- grad_key: bfloat16 [2, 2048, 2048], P('exp', 'ctx')
- grad_value: bfloat16 [2, 2048, 2048], P('exp', 'ctx')
- tangent_out: bfloat16 [2, 2048, 2048], P('exp', 'ctx')
The draws below stay inside these ranges and needn't reach their ends.
Inputs may be any that keep to these rules, and one draw needn't show every extreme that they name: `route_ids`: among the 128 tokens of one block of a sequence, the routes of a token name distinct experts, no expert is named by more than 128 routes, and in every draw some block names some expert exactly 128 times.
All inputs are finite; a program needn't handle non-finite values. No bound on the sum of `block_mask` on one device may be relied on, other than what follows from the above.
Results may differ from the reference program's by a relative error of at most 0.035.
Values may be sent and summed in bfloat16 or wider, within the bound.
No kernel may reach another device: no remote copies, remote signals or barrier semaphores. Data moves between devices by JAX's collectives and lax.ppermute only.
A program may use at most 128 MiB of HBM per device.

```python
import math
import jax
import jax.numpy as jnp
import numpy as np
from jax import lax

D = 2048
HEADS = 16
FFH = 512
TOK_DEV = 128
WIN = 4
EXPERTS = 2
TOPK = 1
CAP = 128
LEN = 2048
SEQS = 2
N_CTX = 16


def plant_plan(key):
    base_key = jax.random.fold_in(key, 901)
    block_count = SEQS * (LEN // TOK_DEV)
    head_size = D // HEADS
    key_rows, key_heads, key_signs, key_gaps = jax.random.split(base_key, 4)
    plant_rows = jax.random.randint(key_rows, (block_count,), 1, TOK_DEV)
    plant_heads = jax.random.randint(key_heads, (block_count,), 0, HEADS)
    plant_signs = (jax.random.randint(key_signs, (block_count, head_size), 0, 2) * 2 - 1).astype(jnp.float32)
    plant_gaps = jax.random.uniform(key_gaps, (block_count,), jnp.float32, 1.5, 2.5)
    cycle = jnp.arange(block_count, dtype=jnp.int32) % 3
    strengths = jnp.where(cycle == 0, 1.75, jnp.where(cycle == 1, 2.5, 3.5)).astype(jnp.float32)
    return (plant_rows, plant_heads, plant_signs, plant_gaps, strengths)


def base_field(key, spread, limit):
    noise_key = jax.random.fold_in(key, 902)
    field = jnp.clip(jax.random.normal(noise_key, (SEQS, LEN, D), jnp.float32) * spread, -limit, limit)
    return field.reshape(SEQS * (LEN // TOK_DEV), TOK_DEV, HEADS, D // HEADS)


def head_mask(plant_heads):
    return (jnp.arange(HEADS, dtype=jnp.int32)[None, :] == plant_heads[:, None])[:, None, :, None]


def draw_query(key, part):
    plant_rows, plant_heads, plant_signs, plant_gaps, strengths = plant_plan(key)
    field = base_field(jax.random.fold_in(key, 11), 2.0, 12.0)
    row_hit = (jnp.arange(TOK_DEV, dtype=jnp.int32)[None, :] == plant_rows[:, None])[:, :, None, None]
    planted = strengths[:, None, None, None] * plant_signs[:, None, None, :]
    field = jnp.where(row_hit & head_mask(plant_heads), planted, field)
    return field.reshape(SEQS, LEN, D).astype(jnp.bfloat16)


def draw_key(key, part):
    plant_rows, plant_heads, plant_signs, plant_gaps, strengths = plant_plan(key)
    field = base_field(jax.random.fold_in(key, 13), 1.0, 6.0)
    head_size = D // HEADS
    rowpos = jnp.arange(TOK_DEV, dtype=jnp.int32)[None, :]
    top_hit = (rowpos == plant_rows[:, None])[:, :, None, None]
    next_hit = (rowpos == plant_rows[:, None] - 1)[:, :, None, None]
    lowered = (jnp.arange(head_size, dtype=jnp.int32) < 4)[None, :]
    drop = plant_gaps * head_size ** 0.5 / (strengths * 4.0)
    first_key = 6.0 * plant_signs
    second_key = plant_signs * (6.0 - jnp.where(lowered, drop[:, None], 0.0))
    in_head = head_mask(plant_heads)
    field = jnp.where(top_hit & in_head, first_key[:, None, None, :], field)
    field = jnp.where(next_hit & in_head, second_key[:, None, None, :], field)
    return field.reshape(SEQS, LEN, D).astype(jnp.bfloat16)


def set_ends(entries, key, low, top_value):
    longest = entries.shape.index(max(entries.shape))
    spots = []
    for shift in (0, 1):
        where = [jax.random.randint(jax.random.fold_in(key, axis), (), 0, length) for axis, length in enumerate(entries.shape)]
        where[longest] = (where[longest] + shift) % entries.shape[longest]
        spots.append(tuple(where))
    return entries.at[spots[0]].set(low).at[spots[1]].set(top_value)


def block_scale(own_key, dims, cuts, smallest, high):
    def one(axis_at, blocks):
        draws = jax.random.uniform(jax.random.fold_in(jax.random.fold_in(own_key, 6), axis_at), (blocks,), jnp.float32, smallest / len(cuts), high / len(cuts))
        return jnp.repeat(jnp.exp(draws), dims[axis_at] // blocks).reshape((-1,) + (1,) * (len(dims) - axis_at - 1))

    level = one(*cuts[0])
    for cut in cuts[1:]:
        level = level * one(*cut)
    return level


def deal_out(key, own, number, rows, amount, top, bound, lean):
    ranking = jax.random.permutation(key, amount)
    heavy_load, common = shares(amount, rows * top, bound, lean, True), shares(amount, rows * top, bound, lean, False)
    places = jnp.arange(amount)

    def named(tallies, offset_by):
        used = int((tallies > 0).sum())
        fixed = max(1, used // 4)
        moved = fixed + (places - fixed + offset_by * (used - fixed)) % max(1, amount - fixed)
        return jnp.zeros((amount,), jnp.int32).at[ranking[jnp.where(places < fixed, places, moved)]].set(jnp.asarray(tallies, jnp.int32))

    tallies = jnp.where(number % 4 == 0, named(heavy_load, number // 4), named(common, number - number // 4 - 1))
    mixed = jax.random.permutation(jax.random.fold_in(own, 3), amount)
    giver, taker = mixed[0:amount // 2 * 2:2], mixed[1:amount // 2 * 2:2]
    margin = jnp.minimum(tallies[giver] - 1, bound - tallies[taker]) // 2
    margin = jnp.where((giver == ranking[0]) | (taker == ranking[0]) | (tallies[taker] == 0), 0, jnp.maximum(margin, 0))
    moved = jax.random.randint(jax.random.fold_in(own, 4), (amount // 2,), 0, 1 << 20) % (margin + 1)
    tallies = tallies.at[giver].add(-moved).at[taker].add(moved)
    labels = jnp.searchsorted(jnp.cumsum(tallies), jnp.arange(rows * top), side="right").astype(jnp.int32)
    grid = labels.reshape(top, rows).T
    grid = grid[jax.random.permutation(jax.random.fold_in(own, 1), rows)]
    offset_by = jax.random.randint(jax.random.fold_in(own, 2), (rows, 1), 0, top)
    return jnp.take_along_axis(grid, (jnp.arange(top)[None, :] + offset_by) % top, axis=1)


def shares(number_of, total, most, lean, full):
    loads = [(1 << 20) // math.isqrt(standing ** lean) + 1 for standing in range(1, number_of + 1)]
    largest = most if full else min(most, max(-(-total // number_of), total * loads[0] // sum(loads)))
    least = 1 if total - largest >= number_of - 1 else 0
    given, rest = [largest] + [least] * (number_of - 1), total - largest - least * (number_of - 1)
    while rest > 0:
        movable = [i for i in range(1, number_of) if given[i] < largest] or [i for i in range(1, number_of) if given[i] < most]
        pool, left = sum([loads[i] for i in movable]), rest
        for i in movable:
            more = min(most - given[i], max(1, left * loads[i] // pool), rest)
            given[i] = given[i] + more
            rest = rest - more
    return np.array(given)


def gaussian(key, dims, deviation, reach, shards=(), kind=jnp.bfloat16):
    entries = jax.random.normal(key, dims, jnp.float32) * deviation
    if len(shards) > 0:
        entries = block_scale(key, dims, shards, -0.22, 0.18) * entries
    return jnp.clip(entries, min=-reach, max=reach).astype(kind)


def setup_inputs(seed: int = 0) -> dict:
    streams_of = jax.random.split(jax.random.key(seed), 11)
    query = draw_query(jax.random.fold_in(streams_of[10], 71), 0)
    key = draw_key(jax.random.fold_in(streams_of[10], 71), 0)
    value = gaussian(streams_of[2], (SEQS, LEN, D), 2.0, 12.0, ((0, 2), (1, 16)))
    cotangent = gaussian(streams_of[3], (SEQS, LEN, D), 1.0, 6.0, ((0, 2), (1, 16)))
    route_ids_keys = jax.random.split(jax.random.fold_in(streams_of[4], 1), SEQS * LEN // TOK_DEV)
    route_ids_turns = jax.random.permutation(jax.random.fold_in(streams_of[4], 3), SEQS * LEN // TOK_DEV)
    route_ids = jax.vmap(lambda own, number: deal_out(jax.random.fold_in(streams_of[4], 2), own, number, TOK_DEV, EXPERTS, TOPK, CAP, 2))(route_ids_keys, route_ids_turns).reshape((SEQS, LEN, TOPK))
    route_weights = jnp.clip(0.2 + 0.8 * jax.random.uniform(streams_of[5], (SEQS, LEN, TOPK), jnp.float32) ** block_scale(streams_of[5], (SEQS, LEN, TOPK), ((0, 2), (1, 16)), -0.2, 0.2), 0.2, 1.0)
    block_mask = set_ends((jax.random.randint(streams_of[6], (SEQS, N_CTX, WIN - 1), 0, 4) < 3).astype(jnp.int32), jax.random.fold_in(streams_of[6], 1), 0, 1)
    w_gate = gaussian(streams_of[7], (EXPERTS, D, FFH), D ** -0.5, 0.125, ((0, 2),))
    w_up = gaussian(streams_of[8], (EXPERTS, D, FFH), D ** -0.5, 0.125, ((0, 2),))
    w_down = gaussian(streams_of[9], (EXPERTS, FFH, D), FFH ** -0.5, 0.25, ((0, 2),))
    return dict(query=query, key=key, value=value, cotangent=cotangent, route_ids=route_ids, route_weights=route_weights, block_mask=block_mask, w_gate=w_gate, w_up=w_up, w_down=w_down)


tile_rows = 256


def silu_parts(gate_pre):
    sigmoid_val = jax.nn.sigmoid(gate_pre)
    return gate_pre * sigmoid_val, sigmoid_val * (1.0 + gate_pre * (1.0 - sigmoid_val))


def split_rows(row_block):
    return row_block.astype(jnp.float32).reshape(row_block.shape[0], HEADS, D // HEADS)


def rounded(values_f32):
    return lax.optimization_barrier(values_f32.astype(jnp.bfloat16)).astype(jnp.float32)


def take_block(whole, sequence, block_index):
    start = (block_index * TOK_DEV).astype(jnp.int32)
    return lax.dynamic_slice(whole, (sequence.astype(jnp.int32), start, jnp.int32(0)), (1, TOK_DEV, whole.shape[2]))[0]


def window_of(whole, sequence, block_index):
    return jnp.concatenate([take_block(whole, sequence, jnp.maximum(block_index - offset, 0)) for offset in range(WIN)], axis=0)


def allowed_of(block_mask, sequence, block_index):
    rowpos = jnp.arange(TOK_DEV, dtype=jnp.int32)
    pieces = [rowpos[:, None] >= rowpos[None, :]]
    for offset in range(1, WIN):
        mask_entry = lax.dynamic_slice(block_mask, (sequence.astype(jnp.int32), block_index.astype(jnp.int32), jnp.int32(offset - 1)), (1, 1, 1))[0, 0, 0]
        visible = (block_index >= offset) & (mask_entry == 1)
        pieces.append(jnp.broadcast_to(visible, (TOK_DEV, TOK_DEV)))
    return jnp.concatenate(pieces, axis=1)


def probs_of(query_rows, key_window, allowed):
    scores = jnp.einsum('qhd,khd->hqk', split_rows(query_rows), split_rows(key_window)) * ((D // HEADS) ** -0.5)
    scores = jnp.where(allowed[None], scores, -1e30)
    row_top = jnp.max(scores, axis=-1, keepdims=True)
    exp_scores = jnp.exp(scores - row_top)
    return exp_scores / jnp.sum(exp_scores, axis=-1, keepdims=True)


def expert_forward(row_block, gate_matrix, up_matrix, down_matrix):
    gate_pre = jnp.dot(row_block, gate_matrix, preferred_element_type=jnp.float32)
    up_value = jnp.dot(row_block, up_matrix, preferred_element_type=jnp.float32)
    activated, slope_val = silu_parts(gate_pre)
    hidden = (activated * up_value).astype(jnp.bfloat16)
    return jnp.dot(hidden, down_matrix, preferred_element_type=jnp.float32).astype(jnp.bfloat16), gate_pre, up_value


def expert_backward(cot_block, gate_pre, up_value, gate_matrix, up_matrix, down_matrix):
    hidden_grad = jnp.dot(cot_block, down_matrix.T, preferred_element_type=jnp.float32)
    activated, slope_val = silu_parts(gate_pre)
    gate_grad = (hidden_grad * up_value * slope_val).astype(jnp.bfloat16)
    up_grad = (hidden_grad * activated).astype(jnp.bfloat16)
    summed = jnp.dot(gate_grad, gate_matrix.T, preferred_element_type=jnp.float32) + jnp.dot(up_grad, up_matrix.T, preferred_element_type=jnp.float32)
    return summed.astype(jnp.bfloat16)


def expert_tangent(tan_block, gate_pre, up_value, gate_matrix, up_matrix, down_matrix):
    gate_tan = jnp.dot(tan_block, gate_matrix, preferred_element_type=jnp.float32)
    up_tan = jnp.dot(tan_block, up_matrix, preferred_element_type=jnp.float32)
    activated, slope_val = silu_parts(gate_pre)
    hidden_tan = (slope_val * gate_tan * up_value + activated * up_tan).astype(jnp.bfloat16)
    return jnp.dot(hidden_tan, down_matrix, preferred_element_type=jnp.float32).astype(jnp.bfloat16)


def expert_pass(route_ids, row_sets, w_gate, w_up, w_down, tile_fn):
    flat_ids = route_ids.reshape(-1).astype(jnp.int32)
    pair_count = flat_ids.shape[0]
    sort_order = jnp.argsort(flat_ids, stable=True).astype(jnp.int32)
    sorted_ids = flat_ids[sort_order]
    counts = jnp.sum((flat_ids[:, None] == jnp.arange(EXPERTS, dtype=jnp.int32)[None, :]).astype(jnp.int32), axis=0).astype(jnp.int32)
    starts = (jnp.cumsum(counts) - counts).astype(jnp.int32)
    padded = ((counts + tile_rows - 1) // tile_rows * tile_rows).astype(jnp.int32)
    pad_ends = jnp.cumsum(padded).astype(jnp.int32)
    pad_starts = (pad_ends - padded).astype(jnp.int32)
    positions = (pad_starts[sorted_ids] + jnp.arange(pair_count, dtype=jnp.int32) - starts[sorted_ids]).astype(jnp.int32)
    tile_count = (pair_count + tile_rows - 1) // tile_rows + EXPERTS
    source = jnp.full((tile_count * tile_rows,), pair_count, jnp.int32).at[positions].set(sort_order)
    tile_starts = jnp.arange(tile_count, dtype=jnp.int32) * tile_rows
    tile_expert = jnp.minimum(jnp.sum((tile_starts[:, None] >= pad_ends[None, :]).astype(jnp.int32), axis=1), EXPERTS - 1).astype(jnp.int32)
    stacks = []
    for row_set in row_sets:
        extended = jnp.concatenate([row_set, jnp.zeros((1, row_set.shape[1]), row_set.dtype)], axis=0)
        stacks.append(extended[source].reshape(tile_count, tile_rows, row_set.shape[1]))

    def run_tile(operands):
        expert = operands[0]
        return tile_fn(operands[1:], w_gate[expert], w_up[expert], w_down[expert])

    tile_outs = lax.map(run_tile, (tile_expert,) + tuple(stacks))
    results = []
    for result in tile_outs:
        flattened = result.reshape(tile_count * tile_rows, result.shape[-1])
        results.append(jnp.zeros((pair_count + 1, flattened.shape[1]), flattened.dtype).at[source].set(flattened)[:pair_count])
    return results


def reference(query, key, value, cotangent, route_ids, route_weights, block_mask, w_gate, w_up, w_down):
    score_scale = (D // HEADS) ** -0.5
    blocks = jnp.arange(SEQS * N_CTX, dtype=jnp.int32)

    def forward_block(block):
        sequence = block // N_CTX
        block_index = block % N_CTX
        attn_probs = probs_of(take_block(query, sequence, block_index), window_of(key, sequence, block_index), allowed_of(block_mask, sequence, block_index))
        out_rows = jnp.einsum('hqk,khd->qhd', rounded(attn_probs), split_rows(window_of(value, sequence, block_index)))
        return out_rows.reshape(TOK_DEV, D).astype(jnp.bfloat16)

    attended = lax.map(forward_block, blocks).reshape(SEQS, LEN, D)
    att_rows = attended.reshape(-1, D)
    cot_rows = cotangent.reshape(-1, D)
    weights = route_weights.reshape(-1, TOPK, 1).astype(jnp.float32)

    def forward_tiles(tiles, gate_matrix, up_matrix, down_matrix):
        expert_out, gate_pre, up_value = expert_forward(tiles[0], gate_matrix, up_matrix, down_matrix)
        return expert_out, expert_backward(tiles[1], gate_pre, up_value, gate_matrix, up_matrix, down_matrix)

    expert_out, route_grad = expert_pass(route_ids, [jnp.repeat(att_rows, TOPK, axis=0), jnp.repeat(cot_rows, TOPK, axis=0)], w_gate, w_up, w_down, forward_tiles)
    layer_out = (att_rows.astype(jnp.float32) + jnp.sum(expert_out.astype(jnp.float32).reshape(-1, TOPK, D) * weights, axis=1)).astype(jnp.bfloat16)
    attn_cot = (cot_rows.astype(jnp.float32) + jnp.sum(route_grad.astype(jnp.float32).reshape(-1, TOPK, D) * weights, axis=1)).astype(jnp.bfloat16).reshape(SEQS, LEN, D)

    def grads_of_sequence(sequence):
        def step(buffers, step_index):
            block_index = jnp.minimum(step_index, N_CTX - 1)
            live_flag = (step_index < N_CTX).astype(jnp.float32)
            query_rows = take_block(query, sequence, block_index)
            key_window = window_of(key, sequence, block_index)
            value_window = window_of(value, sequence, block_index)
            attn_probs = probs_of(query_rows, key_window, allowed_of(block_mask, sequence, block_index))
            probs_low = rounded(attn_probs)
            cot_block = take_block(attn_cot, sequence, block_index)
            att_block = take_block(attended, sequence, block_index)
            row_delta = jnp.einsum('qhd,qhd->hq', split_rows(cot_block), split_rows(att_block))
            prob_grad = jnp.einsum('qhd,khd->hqk', split_rows(cot_block), split_rows(value_window))
            score_grad = rounded(attn_probs * (prob_grad - row_delta[:, :, None]))
            query_grad = (jnp.einsum('hqk,khd->qhd', score_grad, split_rows(key_window)) * score_scale).reshape(TOK_DEV, D).astype(jnp.bfloat16)
            key_terms = (jnp.einsum('hqk,qhd->khd', score_grad, split_rows(query_rows)) * score_scale).reshape(WIN, TOK_DEV, D) * live_flag
            value_terms = jnp.einsum('hqk,qhd->khd', probs_low, split_rows(cot_block)).reshape(WIN, TOK_DEV, D) * live_flag
            blank = jnp.zeros((1, TOK_DEV, D), jnp.float32)
            key_buffer = jnp.concatenate([buffers[0][1:], blank], axis=0) + key_terms[::-1]
            value_buffer = jnp.concatenate([buffers[1][1:], blank], axis=0) + value_terms[::-1]
            return (key_buffer, value_buffer), (query_grad, key_buffer[0].astype(jnp.bfloat16), value_buffer[0].astype(jnp.bfloat16))

        start = (jnp.zeros((WIN, TOK_DEV, D), jnp.float32), jnp.zeros((WIN, TOK_DEV, D), jnp.float32))
        carry_end, emitted = lax.scan(step, start, jnp.arange(N_CTX + WIN - 1, dtype=jnp.int32))
        return (emitted[0][:N_CTX].reshape(LEN, D), emitted[1][WIN - 1:].reshape(LEN, D), emitted[2][WIN - 1:].reshape(LEN, D))

    grad_query, grad_key, grad_value = lax.map(grads_of_sequence, jnp.arange(SEQS, dtype=jnp.int32))

    def tangent_block(block):
        sequence = block // N_CTX
        block_index = block % N_CTX
        query_rows = take_block(query, sequence, block_index)
        key_window = window_of(key, sequence, block_index)
        value_window = window_of(value, sequence, block_index)
        attn_probs = probs_of(query_rows, key_window, allowed_of(block_mask, sequence, block_index))
        probs_low = rounded(attn_probs)
        tan_query = take_block(grad_query, sequence, block_index)
        tan_keys = window_of(grad_key, sequence, block_index)
        tan_values = window_of(grad_value, sequence, block_index)
        score_tan = (jnp.einsum('qhd,khd->hqk', split_rows(tan_query), split_rows(key_window)) + jnp.einsum('qhd,khd->hqk', split_rows(query_rows), split_rows(tan_keys))) * score_scale
        mean_tan = jnp.sum(attn_probs * score_tan, axis=-1, keepdims=True)
        prob_tan = rounded(attn_probs * (score_tan - mean_tan))
        out_rows = jnp.einsum('hqk,khd->qhd', prob_tan, split_rows(value_window)) + jnp.einsum('hqk,khd->qhd', probs_low, split_rows(tan_values))
        return out_rows.reshape(TOK_DEV, D).astype(jnp.bfloat16)

    attn_tangent = lax.map(tangent_block, blocks).reshape(-1, D)

    def tangent_tiles(tiles, gate_matrix, up_matrix, down_matrix):
        gate_pre = jnp.dot(tiles[0], gate_matrix, preferred_element_type=jnp.float32)
        up_value = jnp.dot(tiles[0], up_matrix, preferred_element_type=jnp.float32)
        return (expert_tangent(tiles[1], gate_pre, up_value, gate_matrix, up_matrix, down_matrix),)

    expert_tan = expert_pass(route_ids, [jnp.repeat(att_rows, TOPK, axis=0), jnp.repeat(attn_tangent, TOPK, axis=0)], w_gate, w_up, w_down, tangent_tiles)[0]
    tangent_out = (attn_tangent.astype(jnp.float32) + jnp.sum(expert_tan.astype(jnp.float32).reshape(-1, TOPK, D) * weights, axis=1)).astype(jnp.bfloat16)
    return (layer_out.reshape(SEQS, LEN, D), grad_query, grad_key, grad_value, tangent_out.reshape(SEQS, LEN, D))
```

```python
import functools

import jax
import jax.numpy as jnp
from jax import lax
from jax.experimental import pallas as pl
from jax.experimental.pallas import tpu as pltpu
from jax.sharding import PartitionSpec as P

HEADS = 16
WIN = 4
PAIR = 2
SIDE = 128
FAR = 1e30
BF = jnp.bfloat16
F32 = jnp.float32
VMEM = pl.BlockSpec(memory_space=pltpu.VMEM)
SMEM = pl.BlockSpec(memory_space=pltpu.SMEM)
ANY = pl.BlockSpec(memory_space=pl.ANY)


def moved(x, by):
    devices = lax.axis_size("ctx")
    pairs = [(i, i + by) for i in range(devices) if 0 <= i + by < devices]
    return lax.ppermute(x, "ctx", pairs)


def swapped(x):
    return lax.ppermute(x, "ctx", [(i, i ^ 1) for i in range(lax.axis_size("ctx"))])


def crossed(x):
    return lax.ppermute(x, "exp", [(0, 1), (1, 0)])


def nn(a, b):
    return lax.dot_general(a, b, (((1,), (0,)), ((), ())), preferred_element_type=F32)


def nt(a, b):
    return lax.dot_general(a, b, (((1,), (1,)), ((), ())), preferred_element_type=F32)


def tn(a, b):
    return lax.dot_general(a, b, (((0,), (0,)), ((), ())), preferred_element_type=F32)


def silu_parts(gate_pre):
    sigmoid_val = jax.nn.sigmoid(gate_pre)
    return (gate_pre * sigmoid_val, sigmoid_val * (1.0 + gate_pre * (1.0 - sigmoid_val)))


def lanes_of(rows):
    return lax.broadcasted_iota(jnp.int32, (rows, SIDE), 1)


def put_side(side, lanes, head, column):
    first = column.astype(BF).astype(F32)
    second = (column - first).astype(BF).astype(F32)
    third = column - first - second
    for at, term in ((8, first), (16, second), (24, third)):
        side = jnp.where(lanes == at + head, term, side)
    return side


def get_side(side, lanes, head):
    mine = (lanes == 8 + head) | (lanes == 16 + head) | (lanes == 24 + head)
    return jnp.sum(jnp.where(mine, side, 0.0), axis=1, keepdims=True)


def hidden_by(flag):
    return (1.0 - flag) * FAR


def call(kernel, outs, scratch=(), limit=40, **kw):
    return pl.pallas_call(
        kernel,
        out_shape=outs,
        scratch_shapes=list(scratch),
        compiler_params=pltpu.CompilerParams(vmem_limit_bytes=limit * 1024 * 1024),
        **kw,
    )


def window_refs(far, near, own, rows, width):
    return {
        -3: (far, 0, 0, width),
        -2: (near, 0, 0, width),
        -1: (near, rows, 0, width),
        0: (own, 0, width, 2 * width),
        1: (own, rows, width, 2 * width),
    }


def stacked(window, js, rows, at, size, kind):
    return jnp.concatenate(
        [
            window[j][0][
                pl.ds(window[j][1], rows), pl.ds(pl.multiple_of(window[j][kind] + at, size), size)
            ]
            for j in js
        ],
        axis=0,
    )


def attend_kernel(size, far, near, own, me, keep, send, qx):
    rows, width = far.shape[0], far.shape[1] // 2
    heads = width // size
    scale = size ** (-0.5)
    core = me[0]
    window = window_refs(far, near, own, rows, width)
    lanes = lanes_of(rows)
    causal = lax.broadcasted_iota(jnp.int32, (rows, rows), 0) >= lax.broadcasted_iota(
        jnp.int32, (rows, rows), 1
    )
    qx[:, 0:width] = own[:, 0:width]
    for block in range(PAIR):
        flags = own[block * rows : (block + 1) * rows, 3 * width :].astype(F32)
        biases = [hidden_by(flags[:, w - 1 : w]) for w in range(1, WIN)]
        js = list(range(block - WIN + 1, block + 1))

        def one(head, side):
            at = head * size
            q = own[pl.ds(block * rows, rows), pl.ds(pl.multiple_of(at, size), size)]
            scores = nt(q, stacked(window, js, rows, at, size, 2)) * scale
            parts = [
                scores[:, n * rows : (n + 1) * rows] - biases[block - j - 1]
                if j < block
                else jnp.where(causal, scores[:, n * rows : (n + 1) * rows], -FAR)
                for n, j in enumerate(js)
            ]
            scores = jnp.concatenate(parts, axis=1)
            top = jnp.max(scores, axis=1, keepdims=True)
            weights = jnp.exp(scores - top)
            total = jnp.sum(weights, axis=1, keepdims=True)
            probs = (weights / total).astype(BF)
            out = nn(probs, stacked(window, js, rows, at, size, 3)).astype(BF)
            place = pl.ds(pl.multiple_of(at, size), size)

            @pl.when(core == block)
            def _():
                keep[:, place] = out

            @pl.when(core != block)
            def _():
                send[:, place] = out

            return put_side(side, lanes, head, top + jnp.log(total))

        side = lax.fori_loop(0, heads, one, jnp.where(lanes < WIN - 1, flags, 0.0))
        qx[block * rows : (block + 1) * rows, width:] = side.astype(BF)


def grads_kernel(size, far, near, own, qfb, qnb, qo, qna, qfa, cfb, cnb, co, cna, cfa, grads, tans):
    rows, width = far.shape[0], far.shape[1] // 2
    heads = width // size
    scale = size ** (-0.5)
    window = window_refs(far, near, own, rows, width)
    lanes = lanes_of(rows)
    causal = lax.broadcasted_iota(jnp.int32, (rows, rows), 0) >= lax.broadcasted_iota(
        jnp.int32, (rows, rows), 1
    )
    places = {-3: (0, 0), -2: (1, 0), -1: (1, 1), 0: (2, 0), 1: (2, 1), 2: (3, 0), 3: (3, 1), 4: (4, 0)}
    q_refs, c_refs = (qfb, qnb, qo, qna, qfa), (cfb, cnb, co, cna, cfa)

    def one(head, carry):
        at = pl.multiple_of(head * size, size)
        key_sums, value_sums = {}, {}
        kept = {}

        def added(sums, js, terms):
            for n, j in enumerate(js):
                term = terms[n * rows : (n + 1) * rows]
                sums[j] = sums[j] + term if j in sums else term

        for t in range(1 - WIN, WIN + 1):
            ref, half = places[t]
            here = pl.ds(half * rows, rows)
            q = q_refs[ref][here, pl.ds(at, size)]
            cot = c_refs[ref][here, pl.ds(at, size)]
            q_side = q_refs[ref][here, width:].astype(F32)
            c_side = c_refs[ref][here, width:].astype(F32)
            level = get_side(q_side, lanes, head)
            delta = get_side(c_side, lanes, head)
            js = list(range(max(1 - WIN, t - WIN + 1), min(1, t) + 1))
            keys = stacked(window, js, rows, head * size, size, 2)
            values = stacked(window, js, rows, head * size, size, 3)
            scores = nt(q, keys) * scale
            parts = []
            for n, j in enumerate(js):
                part = scores[:, n * rows : (n + 1) * rows]
                if j < t:
                    w = t - j
                    part = part - (level + hidden_by(q_side[:, w - 1 : w]))
                else:
                    part = jnp.where(causal, part - level, -FAR)
                parts.append(part)
            probs = jnp.exp(jnp.concatenate(parts, axis=1))
            probs_low = probs.astype(BF)
            score_grad = (probs * (nt(cot, values) - delta)).astype(BF)
            added(key_sums, js, tn(score_grad, q))
            added(value_sums, js, tn(probs_low, cot))
            if 0 <= t < PAIR:
                grad_q = (nn(score_grad, keys) * scale).astype(BF)
                grads[pl.ds(t * rows, rows), pl.ds(at, size)] = grad_q
                kept[t] = (js, q, keys, values, probs, probs_low, grad_q)
        key_grads = {j: (key_sums[j] * scale).astype(BF) for j in key_sums}
        value_grads = {j: value_sums[j].astype(BF) for j in value_sums}
        for t in range(PAIR):
            js, q, keys, values, probs, probs_low, grad_q = kept[t]
            here = pl.ds(t * rows, rows)
            grads[here, pl.ds(pl.multiple_of(width + at, size), size)] = key_grads[t]
            grads[here, pl.ds(pl.multiple_of(2 * width + at, size), size)] = value_grads[t]
            tan_keys = jnp.concatenate([key_grads[j] for j in js], axis=0)
            tan_values = jnp.concatenate([value_grads[j] for j in js], axis=0)
            score_tan = (nt(grad_q, keys) + nt(q, tan_keys)) * scale
            mean = jnp.sum(probs * score_tan, axis=1, keepdims=True)
            prob_tan = (probs * (score_tan - mean)).astype(BF)
            tans[here, pl.ds(at, size)] = (nn(prob_tan, values) + nn(probs_low, tan_values)).astype(BF)
        return carry

    lax.fori_loop(0, heads, one, 0)


def cot_sides(size, cot, attended, cx):
    rows, width = cot.shape[0], cot.shape[1] // PAIR
    lanes = lanes_of(rows)
    for half in range(PAIR):
        side = jnp.zeros((rows, SIDE), F32)
        for head in range(width // size):
            here = slice(half * width + head * size, half * width + (head + 1) * size)
            delta = jnp.sum(cot[:, here].astype(F32) * attended[:, here].astype(F32), axis=1, keepdims=True)
            side = put_side(side, lanes, head, delta)
        cx[half, :, 0:width] = cot[:, half * width : (half + 1) * width]
        cx[half, :, width:] = side.astype(BF)


def in_order(core, kept, got):
    return jnp.where(
        core == 0, jnp.concatenate([kept, got], axis=1), jnp.concatenate([got, kept], axis=1)
    )


def load_weights(core, whole, halves, buffer, sems):
    depth = halves[0].shape[0]
    copies = [
        pltpu.make_async_copy(whole, buffer.at[0], sems.at[0]),
        pltpu.make_async_copy(halves[0], buffer.at[1, pl.ds(core * depth, depth)], sems.at[1]),
        pltpu.make_async_copy(halves[1], buffer.at[1, pl.ds((1 - core) * depth, depth)], sems.at[2]),
    ]
    for copy in copies:
        copy.start()
    return [copies[:1], copies[1:]]


def ready(copies):
    for copy in copies:
        copy.wait()


def hidden_grad_kernel(me, cot, down, down_x, down_s, out, buffer, sems):
    loads = load_weights(me[0], down, (down_x, down_s), buffer, sems)
    units = down.shape[0]
    for e in range(2):
        ready(loads[e])
        out[:, e * units : (e + 1) * units] = nt(cot[...], buffer[e])


def expert_kernel(
    size, me, keep, got, cot, picks, hidden_grad, gate, gate_x, gate_s, up, up_x, up_s,
    cx, hidden, slope_up, active, gates, ups, sems,
):
    core = me[0]
    gate_loads = load_weights(core, gate, (gate_x, gate_s), gates, sems.at[0])
    up_loads = load_weights(core, up, (up_x, up_s), ups, sems.at[1])
    units = gate.shape[1]
    rows_in = in_order(core, keep[...], got[...])
    summed = None
    for e in range(2):
        here = slice(e * units, (e + 1) * units)
        chosen = picks[:, e : e + 1]
        ready(gate_loads[e])
        gate_pre = nn(rows_in, gates[e])
        ready(up_loads[e])
        up_value = nn(rows_in, ups[e])
        activated, slope = silu_parts(gate_pre)
        activated = activated * chosen
        slope = slope * up_value * chosen
        hidden[:, here] = (activated * up_value).astype(BF)
        slope_up[:, here] = slope
        active[:, here] = activated
        back = hidden_grad[:, here]
        term = nt((back * slope).astype(BF), gates[e]) + nt((back * activated).astype(BF), ups[e])
        summed = term if summed is None else summed + term
    weight = picks[:, 2:3]
    attn_cot = (cot[...].astype(F32) + summed.astype(BF).astype(F32) * weight).astype(BF)
    cot_sides(size, attn_cot, rows_in, cx)


def layer_kernel(me, keep, got, hidden, picks, down, down_x, down_s, out, buffer, sems):
    core = me[0]
    loads = load_weights(core, down, (down_x, down_s), buffer, sems)
    units = down.shape[0]
    rows_in = in_order(core, keep[...], got[...]).astype(F32)
    ready(loads[0])
    summed = nn(hidden[:, 0:units], buffer[0])
    ready(loads[1])
    summed = summed + nn(hidden[:, units:], buffer[1])
    out[...] = (rows_in + summed.astype(BF).astype(F32) * picks[:, 2:3]).astype(BF)


def tangent_kernel(
    me, keep, got, slope_up, active, picks, gate, gate_x, gate_s, up, up_x, up_s, down, down_x, down_s,
    out, gates, ups, downs, sems,
):
    core = me[0]
    gate_loads = load_weights(core, gate, (gate_x, gate_s), gates, sems.at[0])
    up_loads = load_weights(core, up, (up_x, up_s), ups, sems.at[1])
    down_loads = load_weights(core, down, (down_x, down_s), downs, sems.at[2])
    units = gate.shape[1]
    rows_in = in_order(core, keep[...], got[...])
    summed = None
    for e in range(2):
        here = slice(e * units, (e + 1) * units)
        ready(gate_loads[e])
        gate_tan = nn(rows_in, gates[e])
        ready(up_loads[e])
        up_tan = nn(rows_in, ups[e])
        hidden = (slope_up[:, here] * gate_tan + active[:, here] * up_tan).astype(BF)
        ready(down_loads[e])
        term = nn(hidden, downs[e])
        summed = term if summed is None else summed + term
    out[...] = (rows_in.astype(F32) + summed.astype(BF).astype(F32) * picks[:, 2:3]).astype(BF)


def exchanged_weights(core, w_gate, w_up, w_down):
    halves = []
    for matrix in (w_down, w_gate, w_up):
        depth = matrix.shape[0] // 2
        over = crossed(lax.dynamic_slice_in_dim(matrix, core * depth, depth, 0))
        halves.append((over, swapped(over)))
    return halves


def like(*shape, kind=BF):
    return jax.ShapeDtypeStruct(shape, kind)


class PairExperts:
    def __init__(self, core, upstream, route_ids, route_weights, w_gate, w_up, w_down):
        own = lax.axis_index("exp")
        self.me = core.reshape(1)
        self.upstream = upstream
        mine = (route_ids == own).astype(F32)
        self.picks = jnp.concatenate([mine, 1.0 - mine, route_weights], axis=1)
        down, gate, up = exchanged_weights(core, w_gate, w_up, w_down)
        self.gate, self.up, self.down = ((w_gate,) + gate, (w_up,) + up, (w_down,) + down)
        rows, wide = upstream.shape
        units = w_gate.shape[1]
        self.rows, self.wide, self.units = rows, wide, units
        self.tall = pltpu.VMEM((2, wide, units), BF)
        self.flat = pltpu.VMEM((2, units, wide), BF)
        self.hidden_grad = call(
            hidden_grad_kernel,
            like(rows, 2 * units, kind=F32),
            [self.flat, pltpu.SemaphoreType.DMA((3,))],
            in_specs=[SMEM, VMEM, ANY, ANY, ANY],
            out_specs=VMEM,
        )(self.me, upstream, *self.down)

    def forward(self, size, keep, got):
        rows, wide, units = self.rows, self.wide, self.units
        cx, hidden, self.slope_up, self.active = call(
            functools.partial(expert_kernel, size),
            (
                like(PAIR, rows, wide // PAIR + SIDE),
                like(rows, 2 * units),
                like(rows, 2 * units, kind=F32),
                like(rows, 2 * units, kind=F32),
            ),
            [self.tall, self.tall, pltpu.SemaphoreType.DMA((2, 3))],
            in_specs=[SMEM] + [VMEM] * 5 + [ANY] * 6,
            out_specs=(VMEM,) * 4,
        )(self.me, keep, got, self.upstream, self.picks, self.hidden_grad, *self.gate, *self.up)
        layer_out = call(
            layer_kernel,
            like(rows, wide),
            [self.flat, pltpu.SemaphoreType.DMA((3,))],
            in_specs=[SMEM] + [VMEM] * 4 + [ANY] * 3,
            out_specs=VMEM,
        )(self.me, keep, got, hidden, self.picks, *self.down)
        return cx, layer_out

    def tangent(self, keep, got):
        return call(
            tangent_kernel,
            like(self.rows, self.wide),
            [self.tall, self.tall, self.flat, pltpu.SemaphoreType.DMA((3, 3))],
            in_specs=[SMEM] + [VMEM] * 5 + [ANY] * 9,
            out_specs=VMEM,
        )(self.me, keep, got, self.slope_up, self.active, self.picks, *self.gate, *self.up, *self.down)


def routing_table(route_rows, experts, capacity):
    flat_ids = route_rows.reshape(-1)
    one_hot = (flat_ids[:, None] == jnp.arange(experts, dtype=jnp.int32)[None, :]).astype(jnp.int32)
    slot_rank = jnp.sum((jnp.cumsum(one_hot, axis=0) - one_hot) * one_hot, axis=1)
    target = flat_ids * capacity + slot_rank
    return (jnp.arange(experts * capacity, dtype=jnp.int32)[:, None] == target[None, :]).astype(
        jnp.bfloat16
    )


def dispatch(slot_table, row_block, routes, experts):
    pair_rows = jnp.repeat(row_block, routes, axis=0)
    sent = jnp.dot(slot_table, pair_rows, preferred_element_type=jnp.float32).astype(jnp.bfloat16)
    return sent.reshape(experts, -1, row_block.shape[1])


def combine(slot_table, returned, weights):
    rows_here, routes = weights.shape
    pair_vals = jnp.dot(
        slot_table.T, returned.reshape(-1, returned.shape[2]), preferred_element_type=jnp.float32
    )
    return jnp.sum(pair_vals.reshape(rows_here, routes, -1) * weights[:, :, None], axis=1)


def expert_forward(row_block, gate_matrix, up_matrix, down_matrix):
    gate_pre = jnp.dot(row_block, gate_matrix, preferred_element_type=jnp.float32)
    up_value = jnp.dot(row_block, up_matrix, preferred_element_type=jnp.float32)
    activated, slope_val = silu_parts(gate_pre)
    hidden = (activated * up_value).astype(jnp.bfloat16)
    return (
        jnp.dot(hidden, down_matrix, preferred_element_type=jnp.float32).astype(jnp.bfloat16),
        gate_pre,
        up_value,
    )


def expert_backward(cot_block, gate_pre, up_value, gate_matrix, up_matrix, down_matrix):
    hidden_grad = jnp.dot(cot_block, down_matrix.T, preferred_element_type=jnp.float32)
    activated, slope_val = silu_parts(gate_pre)
    gate_grad = (hidden_grad * up_value * slope_val).astype(jnp.bfloat16)
    up_grad = (hidden_grad * activated).astype(jnp.bfloat16)
    summed = jnp.dot(gate_grad, gate_matrix.T, preferred_element_type=jnp.float32) + jnp.dot(
        up_grad, up_matrix.T, preferred_element_type=jnp.float32
    )
    return summed.astype(jnp.bfloat16)


def expert_tangent(tan_block, gate_pre, up_value, gate_matrix, up_matrix, down_matrix):
    gate_tan = jnp.dot(tan_block, gate_matrix, preferred_element_type=jnp.float32)
    up_tan = jnp.dot(tan_block, up_matrix, preferred_element_type=jnp.float32)
    activated, slope_val = silu_parts(gate_pre)
    hidden_tan = (slope_val * gate_tan * up_value + activated * up_tan).astype(jnp.bfloat16)
    return jnp.dot(hidden_tan, down_matrix, preferred_element_type=jnp.float32).astype(jnp.bfloat16)


class RoutedExperts:
    def __init__(self, core, upstream, route_ids, route_weights, w_gate, w_up, w_down):
        rows, routes = route_ids.shape
        self.experts = lax.axis_size("exp")
        self.routes = routes
        capacity = min(rows, 2 * rows * routes // self.experts)
        self.core, self.upstream, self.weights = core, upstream, route_weights
        self.matrices = (w_gate, w_up, w_down)
        self.table = routing_table(route_ids, self.experts, capacity)
        self.got_cots = self.sent(upstream)

    def across(self, x):
        return lax.all_to_all(x, "exp", split_axis=0, concat_axis=0, tiled=True)

    def sent(self, x):
        return self.across(dispatch(self.table, x, self.routes, self.experts))

    def returned(self, x):
        back = self.across(x.reshape(self.got_cots.shape))
        return combine(self.table, back, self.weights)

    def forward(self, size, keep, got):
        attended = in_order(self.core, keep, got)
        rows, wide = attended.shape
        got_rows = self.sent(attended).reshape(-1, wide)
        expert_out, self.gate_pre, self.up_value = expert_forward(got_rows, *self.matrices)
        route_grad = expert_backward(
            self.got_cots.reshape(-1, wide), self.gate_pre, self.up_value, *self.matrices
        )
        attn_cot = (self.upstream.astype(F32) + self.returned(route_grad)).astype(BF)
        layer_out = (attended.astype(F32) + self.returned(expert_out)).astype(BF)
        cx = call(
            functools.partial(cot_sides, size),
            like(PAIR, rows, wide // PAIR + SIDE),
            in_specs=[VMEM, VMEM],
            out_specs=VMEM,
        )(attn_cot, attended)
        return cx, layer_out

    def tangent(self, keep, got):
        rows = in_order(self.core, keep, got)
        got_rows = self.sent(rows).reshape(-1, rows.shape[1])
        out = expert_tangent(got_rows, self.gate_pre, self.up_value, *self.matrices)
        return (rows.astype(F32) + self.returned(out)).astype(BF)


def paired(core, kept, got):
    return jnp.where(
        core == 0, jnp.concatenate([kept, got], axis=0), jnp.concatenate([got, kept], axis=0)
    )


def of_core(parts, core):
    return jnp.where(core == 0, parts[0], parts[1])


def neighbours(x, rows):
    return (
        moved(x[rows:], 2 * PAIR),
        moved(x, PAIR),
        moved(x, -PAIR),
        moved(x[:rows], -2 * PAIR),
    )


def local(query, key, value, cotangent, route_ids, route_weights, block_mask, w_gate, w_up, w_down):
    rows, wide = query.shape[1:]
    width = wide // PAIR
    size = wide // HEADS
    index = lax.axis_index("ctx")
    core = index % PAIR
    me = core.reshape(1)

    seen = (block_mask[0, 0] == 1) & (index >= jnp.arange(1, WIN, dtype=jnp.int32))
    flags = jnp.pad(seen.astype(BF), (0, SIDE - WIN + 1))
    flags = jnp.broadcast_to(flags[None], (rows, SIDE))

    def half(at):
        return [x[0][:, at * width : (at + 1) * width] for x in (query, key, value)] + [flags]

    first, second = (jnp.concatenate(half(at), axis=1) for at in range(PAIR))
    own = paired(core, of_core((first, second), core), swapped(of_core((second, first), core)))
    sent = own[:, width : 3 * width]
    near, far = moved(sent, PAIR), moved(sent[rows:], 2 * PAIR)

    pair = lax.axis_size("exp") == 2 and route_ids.shape[2] == 1
    experts = (PairExperts if pair else RoutedExperts)(
        core, cotangent[0], route_ids[0], route_weights[0], w_gate[0], w_up[0], w_down[0]
    )

    keep, send, qx = call(
        functools.partial(attend_kernel, size),
        (like(rows, width), like(rows, width), like(PAIR * rows, width + SIDE)),
        in_specs=[VMEM, VMEM, VMEM, SMEM],
        out_specs=(VMEM,) * 3,
    )(far, near, own, me)
    got = swapped(send)
    qfb, qnb, qna, qfa = neighbours(qx, rows)

    cx, layer_out = experts.forward(size, keep, got)
    co = paired(core, of_core((cx[0], cx[1]), core), swapped(of_core((cx[1], cx[0]), core)))
    cfb, cnb, cna, cfa = neighbours(co, rows)

    grads, tans = call(
        functools.partial(grads_kernel, size),
        (like(PAIR * rows, 3 * width), like(PAIR * rows, width)),
        in_specs=[VMEM] * 13,
        out_specs=(VMEM,) * 2,
    )(far, near, own, qfb, qnb, qx, qna, qfa, cfb, cnb, co, cna, cfa)

    def mine(x):
        return of_core((x[:rows], x[rows:]), core)

    def others(x):
        return of_core((x[rows:], x[:rows]), core)

    tangent_out = experts.tangent(mine(tans), swapped(others(tans)))
    kept, got = mine(grads), swapped(others(grads))
    outs = [
        in_order(core, kept[:, at : at + width], got[:, at : at + width])
        for at in range(0, 3 * width, width)
    ]
    return (layer_out[None], *(x[None] for x in outs), tangent_out[None])


def solution(mesh):
    return jax.shard_map(
        local,
        mesh=mesh,
        in_specs=(
            P("exp", "ctx", None),
            P("exp", "ctx", None),
            P("exp", "ctx", None),
            P("exp", "ctx", None),
            P("exp", "ctx", None),
            P("exp", "ctx", None),
            P("exp", "ctx", None),
            P("exp", None, None),
            P("exp", None, None),
            P("exp", None, None),
        ),
        out_specs=(
            P("exp", "ctx", None),
            P("exp", "ctx", None),
            P("exp", "ctx", None),
            P("exp", "ctx", None),
            P("exp", "ctx", None),
        ),
        check_vma=False,
    )
```

```python
import functools

import jax
import jax.numpy as jnp
from jax import lax
from jax.experimental import pallas as pl
from jax.experimental.pallas import tpu as pltpu
from jax.sharding import PartitionSpec as P

HEADS = 16
WIN = 4
PAIR = 2
SIDE = 128
FAR = 1e30
BF = jnp.bfloat16
F32 = jnp.float32
VMEM = pl.BlockSpec(memory_space=pltpu.VMEM)
SMEM = pl.BlockSpec(memory_space=pltpu.SMEM)
ANY = pl.BlockSpec(memory_space=pl.ANY)


def moved(x, by):
    devices = lax.axis_size("ctx")
    pairs = [(i, i + by) for i in range(devices) if 0 <= i + by < devices]
    return lax.ppermute(x, "ctx", pairs)


def swapped(x, bit=1):
    return lax.ppermute(x, "ctx", [(i, i ^ bit) for i in range(lax.axis_size("ctx"))])


def crossed(x):
    return lax.ppermute(x, "exp", [(0, 1), (1, 0)])


def nn(a, b):
    return lax.dot_general(a, b, (((1,), (0,)), ((), ())), preferred_element_type=F32)


def nt(a, b):
    return lax.dot_general(a, b, (((1,), (1,)), ((), ())), preferred_element_type=F32)


def tn(a, b):
    return lax.dot_general(a, b, (((0,), (0,)), ((), ())), preferred_element_type=F32)


def silu_parts(gate_pre):
    sigmoid_val = jax.nn.sigmoid(gate_pre)
    return (gate_pre * sigmoid_val, sigmoid_val * (1.0 + gate_pre * (1.0 - sigmoid_val)))


LEVEL, DELTA = 8, 32


def terms_of(x):
    first = x.astype(BF).astype(F32)
    second = (x - first).astype(BF).astype(F32)
    return jnp.concatenate([first, second, x - first - second], axis=0)


def rows_of(side, at, heads):
    return sum(side[at + n * heads : at + (n + 1) * heads].astype(F32) for n in range(3))


def hidden_by(flag):
    return (1.0 - flag) * FAR


def causal_of(rows):
    return lax.broadcasted_iota(jnp.int32, (rows, rows), 1) >= lax.broadcasted_iota(
        jnp.int32, (rows, rows), 0
    )


def like(*shape, kind=BF):
    return jax.ShapeDtypeStruct(shape, kind)


def call(kernel, outs, args, scratch=(), time=1, limit=8, alias=None, spaces=None):
    return pl.pallas_call(
        kernel,
        out_shape=outs,
        in_specs=[space for _, space in args],
        out_specs=jax.tree.map(lambda _: VMEM, outs) if spaces is None else spaces,
        input_output_aliases=alias or {},
        scratch_shapes=list(scratch),
        compiler_params=pltpu.CompilerParams(vmem_limit_bytes=limit * 1024 * 1024),
        cost_estimate=pl.CostEstimate(flops=int(time * 1.1e9), bytes_accessed=0, transcendentals=0),
    )(*(array for array, _ in args))


def vmem(*arrays):
    return [(array, VMEM) for array in arrays]


def anywhere(*arrays):
    return [(array, ANY) for array in arrays]


def tied(x, after):
    return call(lambda *refs: None, like(*x.shape), anywhere(x, after), alias={0: 0}, spaces=ANY, limit=1)


def fetch(copies):
    for copy in copies:
        copy.start()
    return copies


def ready(copies):
    for copy in copies:
        copy.wait()


def split_kernel(me, query, key, value, flags, keep, send, sems):
    core = me[0]
    rows, wide = query.shape[1:]
    width = wide // PAIR
    copies = []
    for m, (ref, owner) in enumerate(((keep, core), (send, 1 - core))):
        columns = pl.ds(pl.multiple_of(owner * width, width), width)
        for n, x in enumerate((query, key, value)):
            copies.append(
                pltpu.make_async_copy(x.at[0, :, columns], ref.at[:, pl.ds(n * width, width)], sems.at[m, n])
            )
    fetch(copies)
    seen = jnp.where(lax.broadcasted_iota(jnp.int32, (SIDE, rows), 0) < WIN - 1, flags[...], 0.0)
    for ref in (keep, send):
        ref[:, 3 * width :] = seen.astype(BF)
    ready(copies)


def join_kernel(me, keep, got, after, q2, kv2, odd, side, sems):
    core = me[0]
    rows, width = odd.shape[0], q2.shape[1]
    copies = []
    for n, (ref, block) in enumerate(((keep, core), (got, 1 - core))):
        here = pl.ds(pl.multiple_of(block * rows, rows), rows)
        for m, (target, at) in enumerate(((q2, 0), (kv2, width), (side, 3 * width))):
            source = ref.at[:, pl.ds(at, target.shape[1])]
            copies.append(pltpu.make_async_copy(source, target.at[here, :], sems.at[n, m]))
    fetch(copies)

    @pl.when(core == 1)
    def _():
        fetch([pltpu.make_async_copy(keep.at[:, pl.ds(width, 2 * width)], odd, sems.at[2, 0])])

    @pl.when(core != 1)
    def _():
        fetch([pltpu.make_async_copy(got.at[:, pl.ds(width, 2 * width)], odd, sems.at[2, 0])])

    ready(copies)
    ready([pltpu.make_async_copy(keep.at[:, pl.ds(width, 2 * width)], odd, sems.at[2, 0])])


def cut_kernel(x, after, whole, even, odd):
    rows = even.shape[0]
    whole[...] = x[...]
    even[...] = x[:rows]
    odd[...] = x[rows:]


def weights_kernel(me, gate, up, down, after, first, over, sems):
    core, lane = me[0], me[1]

    def half(ref, out, at):
        depth = out.shape[0]
        return pltpu.make_async_copy(ref.at[pl.ds(core * depth, depth)], out, sems.at[at])

    @pl.when(lane == 0)
    def _():
        half(gate, first, 0).start()

    @pl.when(lane != 0)
    def _():
        half(up, first, 0).start()

    half(down, over, 1).start()
    half(gate, first, 0).wait()
    half(down, over, 1).wait()


def cots_kernel(me, keep, got, side, whole, even, odd):
    core = me[0]
    rows, width = keep.shape[0], keep.shape[1] - SIDE
    for ref, block in ((keep, core), (got, 1 - core)):
        here = pl.ds(pl.multiple_of(block * rows, rows), rows)
        filled = (ref[:, width:].astype(F32) + side[here, :].astype(F32)).astype(BF)
        whole[here, 0:width] = ref[:, 0:width]
        whole[here, width:] = filled

        @pl.when(block == 0)
        def _():
            even[:, 0:width] = ref[:, 0:width]
            even[:, width:] = filled

        @pl.when(block == 1)
        def _():
            odd[:, 0:width] = ref[:, 0:width]
            odd[:, width:] = filled


def window_refs(far, near, own, rows):
    return {-3: (far, 0), -2: (near, 0), -1: (near, rows), 0: (own, 0), 1: (own, rows)}


def stacked(window, js, rows, at, size):
    return jnp.concatenate(
        [window[j][0][pl.ds(window[j][1], rows), pl.ds(pl.multiple_of(at, size), size)] for j in js],
        axis=0,
    )


def each_head(heads, one, step=2):
    def some(n, carry):
        for at in range(step):
            one(step * n + at)
        return carry

    lax.fori_loop(0, heads // step, some, 0)


def attend_kernel(size, me, far, near, own, q2, flags, after, cut, keep, send, side, levels):
    rows, width = far.shape[0], far.shape[1] // 2
    heads = width // size
    scale = size ** (-0.5)
    core = me[0]
    window = window_refs(far, near, own, rows)
    causal = causal_of(rows)
    for block in range(PAIR):
        seen = flags[block * rows : (block + 1) * rows, :].astype(F32)
        biases = [hidden_by(seen[w - 1 : w]) for w in range(1, WIN)]
        js = list(range(block - WIN + 1, block + 1))

        def one(head):
            at = pl.multiple_of(head * size, size)
            q = q2[pl.ds(block * rows, rows), pl.ds(at, size)]
            scores = nt(stacked(window, js, rows, at, size), q) * scale
            parts = [
                scores[n * rows : (n + 1) * rows] - biases[block - j - 1]
                if j < block
                else jnp.where(causal, scores[n * rows : (n + 1) * rows], -FAR)
                for n, j in enumerate(js)
            ]
            scores = jnp.concatenate(parts, axis=0)
            top = jnp.max(scores, axis=0, keepdims=True)
            weights = jnp.exp(scores - top)
            total = jnp.sum(weights, axis=0, keepdims=True)
            probs = (weights * (1.0 / total)).astype(BF)
            out = tn(probs, stacked(window, js, rows, width + at, size)).astype(BF)

            @pl.when(core == block)
            def _():
                keep[:, pl.ds(at, size)] = out

            @pl.when(core != block)
            def _():
                send[:, pl.ds(at, size)] = out

            levels[pl.ds(head, 1), :] = top + jnp.log(total)

        each_head(heads, one)
        filled = jnp.concatenate(
            [seen[:LEVEL], terms_of(levels[...]), jnp.zeros((SIDE - LEVEL - 3 * heads, rows), F32)], axis=0
        )
        side[block * rows : (block + 1) * rows, :] = filled.astype(BF)


def scores_back(q, cot, level, delta, seen, keys, values, js, t, causal, scale):
    rows = q.shape[0]
    scores = nt(keys, q) * scale
    parts = []
    for n, j in enumerate(js):
        part = scores[n * rows : (n + 1) * rows]
        if j < t:
            part = part - (level + hidden_by(seen[t - j - 1 : t - j]))
        else:
            part = jnp.where(causal, part - level, -FAR)
        parts.append(part)
    probs = jnp.exp(jnp.concatenate(parts, axis=0))
    return probs, (probs * (nt(values, cot) - delta)).astype(BF)


def add_blocks(sums, js, terms, rows):
    for n, j in enumerate(js):
        term = terms[n * rows : (n + 1) * rows]
        sums[j] = sums[j] + term if j in sums else term


def own_grads_kernel(
    size, me, far, near, own, q2, co, probs_out, probs_low_out, grads_q, q_keep, q_send, key_sums, value_sums,
    levels, deltas,
):
    rows, width = far.shape[0], far.shape[1] // 2
    heads = width // size
    scale = size ** (-0.5)
    core = me[0]
    window = window_refs(far, near, own, rows)
    causal = causal_of(rows)
    sides = [co[t * rows : (t + 1) * rows, width:].astype(F32) for t in range(PAIR)]
    for t in range(PAIR):
        levels[t] = rows_of(sides[t], LEVEL, heads)
        deltas[t] = rows_of(sides[t], DELTA, heads)

    def one(head):
        at = pl.multiple_of(head * size, size)
        here = pl.ds(at, size)
        keys_at, values_at = {}, {}
        for t in range(PAIR):
            place = pl.ds(t * rows, rows)
            js = list(range(t - WIN + 1, t + 1))
            q, cot = q2[place, here], co[place, here]
            keys = stacked(window, js, rows, at, size)
            values = stacked(window, js, rows, width + at, size)
            probs, score_grad = scores_back(
                q, cot, levels[t, pl.ds(head, 1), :], deltas[t, pl.ds(head, 1), :], sides[t][0:8],
                keys, values, js, t, causal, scale,
            )
            probs_low = probs.astype(BF)
            probs_out[head, t] = probs
            probs_low_out[head, t] = probs_low.T
            add_blocks(keys_at, js, nn(score_grad, q), rows)
            add_blocks(values_at, js, nn(probs_low, cot), rows)
            grad_q = (tn(score_grad, keys) * scale).astype(BF)
            grads_q[place, here] = grad_q

            @pl.when(core == t)
            def _():
                q_keep[:, here] = grad_q

            @pl.when(core != t)
            def _():
                q_send[:, here] = grad_q

        for j in keys_at:
            place = pl.ds((j + WIN - 1) * rows, rows)
            key_sums[place, here] = keys_at[j]
            value_sums[place, here] = values_at[j]

    each_head(heads, one)


def grads_kernel(
    size, me, far, near, own, q2, qfb, qnb, qna, qfa, cfb, cnb, cna, cfa, probs_in, probs_low_in, grads_q,
    key_sums, value_sums, after, keep, send, tans_keep, tans_send, levels, deltas,
):
    rows, width = far.shape[0], far.shape[1] // 2
    heads = width // size
    scale = size ** (-0.5)
    core = me[0]
    window = window_refs(far, near, own, rows)
    causal = causal_of(rows)
    others = (
        (-3, qfb, cfb, 0), (-2, qnb, cnb, 0), (-1, qnb, cnb, 1),
        (2, qna, cna, 0), (3, qna, cna, 1), (4, qfa, cfa, 0),
    )
    sides = [c_ref[half * rows : (half + 1) * rows, width:].astype(F32) for _, _, c_ref, half in others]
    for n, side in enumerate(sides):
        levels[n] = rows_of(side, LEVEL, heads)
        deltas[n] = rows_of(side, DELTA, heads)

    def one(head):
        at = pl.multiple_of(head * size, size)
        here = pl.ds(at, size)
        blocks = range(1 - WIN, PAIR)
        keys_at = {j: key_sums[pl.ds((j + WIN - 1) * rows, rows), here] for j in blocks}
        values_at = {j: value_sums[pl.ds((j + WIN - 1) * rows, rows), here] for j in blocks}
        for n, (t, q_ref, c_ref, half) in enumerate(others):
            place = pl.ds(half * rows, rows)
            js = list(range(max(1 - WIN, t - WIN + 1), min(1, t) + 1))
            q, cot = q_ref[place, here], c_ref[place, here]
            keys = stacked(window, js, rows, at, size)
            values = stacked(window, js, rows, width + at, size)
            probs, score_grad = scores_back(
                q, cot, levels[n, pl.ds(head, 1), :], deltas[n, pl.ds(head, 1), :], sides[n][0:8],
                keys, values, js, t, causal, scale,
            )
            add_blocks(keys_at, js, nn(score_grad, q), rows)
            add_blocks(values_at, js, nn(probs.astype(BF), cot), rows)
        key_grads = {j: (keys_at[j] * scale).astype(BF) for j in blocks}
        value_grads = {j: values_at[j].astype(BF) for j in blocks}
        for t in range(PAIR):
            place = pl.ds(t * rows, rows)
            js = list(range(t - WIN + 1, t + 1))
            keys = stacked(window, js, rows, at, size)
            values = stacked(window, js, rows, width + at, size)
            probs = probs_in[head, t]
            both_keys = jnp.concatenate([keys, jnp.concatenate([key_grads[j] for j in js], axis=0)], axis=1)
            both_rows = jnp.concatenate([grads_q[place, here], q2[place, here]], axis=1)
            tan_values = jnp.concatenate([value_grads[j] for j in js], axis=0)
            score_tan = nt(both_keys, both_rows) * scale
            mean = jnp.sum(probs * score_tan, axis=0, keepdims=True)
            prob_tan = (probs * (score_tan - mean)).astype(BF)
            tan = (tn(prob_tan, values) + nn(probs_low_in[head, t], tan_values)).astype(BF)

            def put(grads, tans):
                grads[:, here] = key_grads[t]
                grads[:, pl.ds(pl.multiple_of(width + at, size), size)] = value_grads[t]
                tans[:, here] = tan

            pl.when(core == t)(lambda: put(keep, tans_keep))
            pl.when(core != t)(lambda: put(send, tans_send))

    each_head(heads, one)


def gather_kernel(me, q_keep, q_got, keep, got, out_q, out_k, out_v):
    core = me[0]
    width = q_keep.shape[1]
    for owner, q, kv in ((core, q_keep, keep), (1 - core, q_got, got)):
        columns = pl.ds(pl.multiple_of(owner * width, width), width)
        out_q[:, columns] = q[...]
        out_k[:, columns] = kv[:, 0:width]
        out_v[:, columns] = kv[:, width:]


def cot_sides(size, cot, attended, put):
    rows, width = cot.shape[0], cot.shape[1] // PAIR
    heads = width // size
    lanes = lax.broadcasted_iota(jnp.int32, (rows, SIDE), 1)
    for half in range(PAIR):
        sums = jnp.zeros((rows, SIDE), F32)
        for head in range(heads):
            here = slice(half * width + head * size, half * width + (head + 1) * size)
            delta = jnp.sum(cot[:, here].astype(F32) * attended[:, here].astype(F32), axis=1, keepdims=True)
            sums = jnp.where(lanes == head, delta, sums)
        blank = jnp.zeros((DELTA, rows), F32)
        rest = jnp.zeros((SIDE - DELTA - 3 * heads, rows), F32)
        side = jnp.concatenate([blank, terms_of(sums.T[0:heads]), rest], axis=0)
        put(half, jnp.concatenate([cot[:, half * width : (half + 1) * width], side.astype(BF)], axis=1))


def cots_out(core, keep, send):
    def put(half, payload):
        @pl.when(core == half)
        def _():
            keep[...] = payload

        @pl.when(core != half)
        def _():
            send[...] = payload

    return put


def in_order(core, kept, got):
    return jnp.where(
        core == 0, jnp.concatenate([kept, got], axis=1), jnp.concatenate([got, kept], axis=1)
    )


def load_down(core, down, over, over_s, buffer, sems):
    depth = over.shape[0]
    return (
        fetch([pltpu.make_async_copy(down, buffer.at[0], sems.at[0])]),
        fetch(
            [
                pltpu.make_async_copy(over, buffer.at[1, pl.ds(core * depth, depth)], sems.at[1]),
                pltpu.make_async_copy(over_s, buffer.at[1, pl.ds((1 - core) * depth, depth)], sems.at[2]),
            ]
        ),
    )


def load_inner(core, lane, gate, up, first, second, first_s, second_s, buffer, sems):
    depth = first.shape[0]
    copies = []
    for n, (ref, which, half) in enumerate(
        ((first, lane, core), (second, 1 - lane, core), (first_s, lane, 1 - core), (second_s, 1 - lane, 1 - core))
    ):
        target = buffer.at[1, which, pl.ds(half * depth, depth)]
        copies.append(pltpu.make_async_copy(ref, target, sems.at[2 + n]))
    own = [
        pltpu.make_async_copy(gate, buffer.at[0, 0], sems.at[0]),
        pltpu.make_async_copy(up, buffer.at[0, 1], sems.at[1]),
    ]
    return fetch(own), fetch(copies)


def hidden_grad_kernel(me, cot, down, over, over_s, out, buffer, sems):
    loads = load_down(me[0], down, over, over_s, buffer, sems)
    units = down.shape[0]
    for e in range(2):
        ready(loads[e])
        out[:, e * units : (e + 1) * units] = nt(cot[0], buffer[e])


def expert_kernel(
    size, me, keep, got, cot, picks, hidden_grad, gate, up, first, second, first_s, second_s,
    cot_keep, cot_send, hidden, slope_up, active, inner, sems,
):
    core = me[0]
    loads = load_inner(core, me[1], gate, up, first, second, first_s, second_s, inner, sems)
    units = gate.shape[1]
    rows_in = in_order(core, keep[...], got[...])
    summed = None
    for e in range(2):
        here = slice(e * units, (e + 1) * units)
        chosen = picks[:, e : e + 1]
        ready(loads[e])
        gate_pre = nn(rows_in, inner[e, 0])
        up_value = nn(rows_in, inner[e, 1])
        activated, slope = silu_parts(gate_pre)
        activated = activated * chosen
        slope = slope * up_value * chosen
        hidden[:, here] = (activated * up_value).astype(BF)
        slope_up[:, here] = slope
        active[:, here] = activated
        back = hidden_grad[:, here]
        term = nt((back * slope).astype(BF), inner[e, 0]) + nt((back * activated).astype(BF), inner[e, 1])
        summed = term if summed is None else summed + term
    weight = picks[:, 2:3]
    attn_cot = (cot[0].astype(F32) + summed.astype(BF).astype(F32) * weight).astype(BF)
    cot_sides(size, attn_cot, rows_in, cots_out(core, cot_keep, cot_send))


def layer_kernel(me, keep, got, hidden, picks, down, over, over_s, out, buffer, sems):
    core = me[0]
    loads = load_down(core, down, over, over_s, buffer, sems)
    units = down.shape[0]
    rows_in = in_order(core, keep[...], got[...]).astype(F32)
    ready(loads[0])
    summed = nn(hidden[:, 0:units], buffer[0])
    ready(loads[1])
    summed = summed + nn(hidden[:, units:], buffer[1])
    out[...] = (rows_in + summed.astype(BF).astype(F32) * picks[:, 2:3]).astype(BF)


def tangent_kernel(
    me, keep, got, slope_up, active, picks, gate, up, first, second, first_s, second_s, down, over, over_s,
    out, inner, buffer, inner_sems, sems,
):
    core = me[0]
    loads = load_inner(core, me[1], gate, up, first, second, first_s, second_s, inner, inner_sems)
    down_loads = load_down(core, down, over, over_s, buffer, sems)
    units = gate.shape[1]
    rows_in = in_order(core, keep[...], got[...])
    summed = None
    for e in range(2):
        here = slice(e * units, (e + 1) * units)
        ready(loads[e])
        gate_tan = nn(rows_in, inner[e, 0])
        up_tan = nn(rows_in, inner[e, 1])
        hidden = (slope_up[:, here] * gate_tan + active[:, here] * up_tan).astype(BF)
        ready(down_loads[e])
        term = nn(hidden, buffer[e])
        summed = term if summed is None else summed + term
    out[...] = (rows_in.astype(F32) + summed.astype(BF).astype(F32) * picks[:, 2:3]).astype(BF)


class PairExperts:
    def __init__(self, index, after, upstream, route_ids, route_weights, w_gate, w_up, w_down):
        core, lane = index % 2, index // 2 % 2
        own = lax.axis_index("exp")
        self.me = jnp.stack([core, lane])
        self.upstream = upstream
        mine = (route_ids == own).astype(F32)
        self.picks = jnp.concatenate([mine, 1.0 - mine, route_weights], axis=1)
        rows, wide = upstream.shape[1:]
        units = w_gate.shape[1]
        self.cut = call(
            weights_kernel,
            (like(wide // 2, units), like(units // 2, wide)),
            [(self.me, SMEM)] + anywhere(w_gate, w_up, w_down, after),
            [pltpu.SemaphoreType.DMA((2,))],
        )
        first, self.over = crossed(self.cut[0]), crossed(self.cut[1])
        self.first = (first, swapped(first), swapped(first, 2))
        self.whole = (w_gate, w_up, w_down)
        self.rows, self.wide, self.units = rows, wide, units
        self.inner_buffer = pltpu.VMEM((2, 2, wide, units), BF)
        self.buffer = pltpu.VMEM((2, units, wide), BF)

    def begun(self):
        return self.cut[0]

    def before(self):
        return self.first[0]

    def forward(self, size, keep, got):
        rows, wide, units = self.rows, self.wide, self.units
        first, first_s, second = self.first
        w_gate, w_up, w_down = self.whole
        over, second = tied(self.over, keep), tied(second, keep)
        self.down = (w_down, over, swapped(over))
        self.inner = (w_gate, w_up, first, second, first_s, swapped(second))
        hidden_grad = call(
            hidden_grad_kernel,
            like(rows, 2 * units, kind=F32),
            [(self.me, SMEM)] + vmem(self.upstream) + anywhere(*self.down),
            [self.buffer, pltpu.SemaphoreType.DMA((3,))],
            time=2.5,
            limit=10,
        )
        half = like(rows, wide // PAIR + SIDE)
        cot_keep, cot_send, hidden, self.slope_up, self.active = call(
            functools.partial(expert_kernel, size),
            (half, half, like(rows, 2 * units), like(rows, 2 * units, kind=F32), like(rows, 2 * units, kind=F32)),
            [(self.me, SMEM)] + vmem(keep, got, self.upstream, self.picks, hidden_grad) + anywhere(*self.inner),
            [self.inner_buffer, pltpu.SemaphoreType.DMA((6,))],
            time=6,
            limit=18,
        )
        layer_out = call(
            layer_kernel,
            like(rows, wide),
            [(self.me, SMEM)] + vmem(keep, got, hidden, self.picks) + anywhere(*self.down),
            [self.buffer, pltpu.SemaphoreType.DMA((3,))],
            time=4,
            limit=10,
        )
        return cot_keep, cot_send, layer_out

    def tangent(self, keep, got):
        return call(
            tangent_kernel,
            like(self.rows, self.wide),
            [(self.me, SMEM)]
            + vmem(keep, got, self.slope_up, self.active, self.picks)
            + anywhere(*self.inner, *self.down),
            [self.inner_buffer, self.buffer, pltpu.SemaphoreType.DMA((6,)), pltpu.SemaphoreType.DMA((3,))],
            time=4.5,
            limit=22,
        )


def routing_table(route_rows, experts, capacity):
    flat_ids = route_rows.reshape(-1)
    one_hot = (flat_ids[:, None] == jnp.arange(experts, dtype=jnp.int32)[None, :]).astype(jnp.int32)
    slot_rank = jnp.sum((jnp.cumsum(one_hot, axis=0) - one_hot) * one_hot, axis=1)
    target = flat_ids * capacity + slot_rank
    return (jnp.arange(experts * capacity, dtype=jnp.int32)[:, None] == target[None, :]).astype(
        jnp.bfloat16
    )


def dispatch(slot_table, row_block, routes, experts):
    pair_rows = jnp.repeat(row_block, routes, axis=0)
    sent = jnp.dot(slot_table, pair_rows, preferred_element_type=jnp.float32).astype(jnp.bfloat16)
    return sent.reshape(experts, -1, row_block.shape[1])


def combine(slot_table, returned, weights):
    rows_here, routes = weights.shape
    pair_vals = jnp.dot(
        slot_table.T, returned.reshape(-1, returned.shape[2]), preferred_element_type=jnp.float32
    )
    return jnp.sum(pair_vals.reshape(rows_here, routes, -1) * weights[:, :, None], axis=1)


def expert_forward(row_block, gate_matrix, up_matrix, down_matrix):
    gate_pre = jnp.dot(row_block, gate_matrix, preferred_element_type=jnp.float32)
    up_value = jnp.dot(row_block, up_matrix, preferred_element_type=jnp.float32)
    activated, slope_val = silu_parts(gate_pre)
    hidden = (activated * up_value).astype(jnp.bfloat16)
    return (
        jnp.dot(hidden, down_matrix, preferred_element_type=jnp.float32).astype(jnp.bfloat16),
        gate_pre,
        up_value,
    )


def expert_backward(cot_block, gate_pre, up_value, gate_matrix, up_matrix, down_matrix):
    hidden_grad = jnp.dot(cot_block, down_matrix.T, preferred_element_type=jnp.float32)
    activated, slope_val = silu_parts(gate_pre)
    gate_grad = (hidden_grad * up_value * slope_val).astype(jnp.bfloat16)
    up_grad = (hidden_grad * activated).astype(jnp.bfloat16)
    summed = jnp.dot(gate_grad, gate_matrix.T, preferred_element_type=jnp.float32) + jnp.dot(
        up_grad, up_matrix.T, preferred_element_type=jnp.float32
    )
    return summed.astype(jnp.bfloat16)


def expert_tangent(tan_block, gate_pre, up_value, gate_matrix, up_matrix, down_matrix):
    gate_tan = jnp.dot(tan_block, gate_matrix, preferred_element_type=jnp.float32)
    up_tan = jnp.dot(tan_block, up_matrix, preferred_element_type=jnp.float32)
    activated, slope_val = silu_parts(gate_pre)
    hidden_tan = (slope_val * gate_tan * up_value + activated * up_tan).astype(jnp.bfloat16)
    return jnp.dot(hidden_tan, down_matrix, preferred_element_type=jnp.float32).astype(jnp.bfloat16)


class RoutedExperts:
    def __init__(self, index, after, upstream, route_ids, route_weights, w_gate, w_up, w_down):
        rows, routes = route_ids.shape
        self.experts = lax.axis_size("exp")
        self.routes = routes
        capacity = min(rows, 2 * rows * routes // self.experts)
        self.core, self.upstream, self.weights = index % 2, upstream[0], route_weights
        self.matrices = (w_gate, w_up, w_down)
        self.table = routing_table(route_ids, self.experts, capacity)
        self.got_cots = self.sent(self.upstream)

    def begun(self):
        return self.got_cots

    def before(self):
        return self.got_cots

    def across(self, x):
        return lax.all_to_all(x, "exp", split_axis=0, concat_axis=0, tiled=True)

    def sent(self, x):
        return self.across(dispatch(self.table, x, self.routes, self.experts))

    def returned(self, x):
        back = self.across(x.reshape(self.got_cots.shape))
        return combine(self.table, back, self.weights)

    def forward(self, size, keep, got):
        attended = in_order(self.core, keep, got)
        rows, wide = attended.shape
        got_rows = self.sent(attended).reshape(-1, wide)
        expert_out, self.gate_pre, self.up_value = expert_forward(got_rows, *self.matrices)
        route_grad = expert_backward(
            self.got_cots.reshape(-1, wide), self.gate_pre, self.up_value, *self.matrices
        )
        attn_cot = (self.upstream.astype(F32) + self.returned(route_grad)).astype(BF)
        layer_out = (attended.astype(F32) + self.returned(expert_out)).astype(BF)

        def kernel(me, cot, rows_in, cot_keep, cot_send):
            cot_sides(size, cot, rows_in, cots_out(me[0], cot_keep, cot_send))

        half = like(rows, wide // PAIR + SIDE)
        cot_keep, cot_send = call(
            kernel, (half, half), [(self.core.reshape(1), SMEM)] + vmem(attn_cot, attended)
        )
        return cot_keep, cot_send, layer_out

    def tangent(self, keep, got):
        rows = in_order(self.core, keep, got)
        got_rows = self.sent(rows).reshape(-1, rows.shape[1])
        out = expert_tangent(got_rows, self.gate_pre, self.up_value, *self.matrices)
        return (rows.astype(F32) + self.returned(out)).astype(BF)


def neighbours(whole, even, odd):
    return (
        moved(odd, 2 * PAIR),
        moved(whole, PAIR),
        moved(whole, -PAIR),
        moved(even, -2 * PAIR),
    )


def local(query, key, value, cotangent, route_ids, route_weights, block_mask, w_gate, w_up, w_down):
    rows, wide = query.shape[1:]
    width = wide // PAIR
    size = wide // HEADS
    heads = width // size
    index = lax.axis_index("ctx")
    core = index % PAIR
    me = [(core.reshape(1), SMEM)]

    seen = (block_mask[0] == 1) & (index >= jnp.arange(1, WIN, dtype=jnp.int32))
    flags = jnp.pad(seen.astype(F32).T, ((0, SIDE - WIN + 1), (0, 0)))
    packed = like(rows, 3 * width + SIDE)
    own_part, mate_part = call(
        split_kernel,
        (packed, packed),
        me + anywhere(query, key, value) + vmem(flags),
        [pltpu.SemaphoreType.DMA((2, 3))],
    )
    got_part = swapped(mate_part)
    pair = lax.axis_size("exp") == 2 and route_ids.shape[2] == 1
    experts = (PairExperts if pair else RoutedExperts)(
        index, mate_part, cotangent, route_ids[0], route_weights[0], w_gate[0], w_up[0], w_down[0]
    )
    q2, kv2, kv_odd, side = call(
        join_kernel,
        (like(2 * rows, width), like(2 * rows, 2 * width), like(rows, 2 * width), like(2 * rows, SIDE)),
        me + anywhere(own_part, got_part, experts.begun()),
        [pltpu.SemaphoreType.DMA((3, 3))],
    )
    near, far = moved(kv2, PAIR), moved(kv_odd, 2 * PAIR)
    blocks = (like(2 * rows, width), like(rows, width), like(rows, width))
    q_parts = call(cut_kernel, blocks, vmem(q2) + anywhere(near))

    keep, send, side = call(
        functools.partial(attend_kernel, size),
        (like(rows, width), like(rows, width), like(2 * rows, SIDE)),
        me + vmem(far, near, kv2, q2, side) + anywhere(experts.before(), q_parts[0]),
        [pltpu.VMEM((heads, rows), F32)],
        time=9,
    )
    got = swapped(send)
    qfb, qnb, qna, qfa = neighbours(*q_parts)

    cot_keep, cot_send, layer_out = experts.forward(size, keep, got)
    payload = wide // PAIR + SIDE
    co, co_even, co_odd = call(
        cots_kernel,
        (like(2 * rows, payload), like(rows, payload), like(rows, payload)),
        me + vmem(cot_keep, swapped(cot_send), side),
    )
    cfb, cnb, cna, cfa = neighbours(co, co_even, co_odd)

    sums = like((WIN + 1) * rows, width, kind=F32)
    probs, probs_low, grads_q, q_keep, q_send, key_sums, value_sums = call(
        functools.partial(own_grads_kernel, size),
        (
            like(heads, 2, WIN * rows, rows, kind=F32),
            like(heads, 2, rows, WIN * rows),
            like(2 * rows, width), like(rows, width), like(rows, width),
            sums, sums,
        ),
        me + vmem(far, near, kv2, q2, co),
        [pltpu.VMEM((2, heads, rows), F32)] * 2,
        time=12,
    )
    q_got = swapped(q_send)
    kv_half, half = like(rows, 2 * width), like(rows, width)
    kv_keep, kv_send, tan_keep, tan_send = call(
        functools.partial(grads_kernel, size),
        (kv_half, kv_half, half, half),
        me
        + vmem(far, near, kv2, q2, qfb, qnb, qna, qfa, cfb, cnb, cna, cfa)
        + vmem(probs, probs_low, grads_q, key_sums, value_sums)
        + anywhere(layer_out),
        [pltpu.VMEM((6, heads, rows), F32)] * 2,
        time=16,
    )
    tan_got = swapped(tan_send)
    kv_got = swapped(kv_send)
    tangent_out = experts.tangent(tan_keep, tan_got)
    out = like(rows, wide)
    outs = call(gather_kernel, (out, out, out), me + vmem(q_keep, q_got, kv_keep, kv_got))
    return (layer_out[None], *(x[None] for x in outs), tangent_out[None])


def solution(mesh):
    return jax.shard_map(
        local,
        mesh=mesh,
        in_specs=(
            P("exp", "ctx", None),
            P("exp", "ctx", None),
            P("exp", "ctx", None),
            P("exp", "ctx", None),
            P("exp", "ctx", None),
            P("exp", "ctx", None),
            P("exp", "ctx", None),
            P("exp", None, None),
            P("exp", None, None),
            P("exp", None, None),
        ),
        out_specs=(
            P("exp", "ctx", None),
            P("exp", "ctx", None),
            P("exp", "ctx", None),
            P("exp", "ctx", None),
            P("exp", "ctx", None),
        ),
        check_vma=False,
    )
```

```python
import functools

import jax
import jax.numpy as jnp
from jax import lax
from jax.experimental import pallas as pl
from jax.experimental.pallas import tpu as pltpu
from jax.sharding import PartitionSpec as P

HEADS = 16
WIN = 4
PAIR = 2
SIDE = 128
FAR = 1e30
BF = jnp.bfloat16
F32 = jnp.float32
VMEM = pl.BlockSpec(memory_space=pltpu.VMEM)
SMEM = pl.BlockSpec(memory_space=pltpu.SMEM)
ANY = pl.BlockSpec(memory_space=pl.ANY)
HBM = pl.BlockSpec(memory_space=pltpu.HBM)


def moved(x, by):
    devices = lax.axis_size("ctx")
    pairs = [(i, i + by) for i in range(devices) if 0 <= i + by < devices]
    return lax.ppermute(x, "ctx", pairs)


def swapped(x, bit=1):
    return lax.ppermute(x, "ctx", [(i, i ^ bit) for i in range(lax.axis_size("ctx"))])


def this_core():
    return lax.axis_index("ctx") % PAIR


def this_lane():
    return lax.axis_index("ctx") // PAIR % 2


def crossed(x):
    return lax.ppermute(x, "exp", [(0, 1), (1, 0)])


def nn(a, b):
    return lax.dot_general(a, b, (((1,), (0,)), ((), ())), preferred_element_type=F32)


def nt(a, b):
    return lax.dot_general(a, b, (((1,), (1,)), ((), ())), preferred_element_type=F32)


def tn(a, b):
    return lax.dot_general(a, b, (((0,), (0,)), ((), ())), preferred_element_type=F32)


def silu_parts(gate_pre):
    sigmoid_val = jax.nn.sigmoid(gate_pre)
    return (gate_pre * sigmoid_val, sigmoid_val * (1.0 + gate_pre * (1.0 - sigmoid_val)))


LEVEL, DELTA = 8, 32


def terms_of(x):
    first = x.astype(BF).astype(F32)
    second = (x - first).astype(BF).astype(F32)
    return jnp.concatenate([first, second, x - first - second], axis=0)


def rows_of(side, at, heads):
    return sum(side[at + n * heads : at + (n + 1) * heads].astype(F32) for n in range(3))


def hidden_by(flag):
    return (1.0 - flag) * FAR


def causal_of(rows):
    return lax.broadcasted_iota(jnp.int32, (rows, rows), 1) >= lax.broadcasted_iota(
        jnp.int32, (rows, rows), 0
    )


def like(*shape, kind=BF):
    return jax.ShapeDtypeStruct(shape, kind)


def call(kernel, outs, args, scratch=(), time=1, limit=8, alias=None, spaces=None):
    return pl.pallas_call(
        kernel,
        out_shape=outs,
        in_specs=[space for _, space in args],
        out_specs=jax.tree.map(lambda _: VMEM, outs) if spaces is None else spaces,
        input_output_aliases=alias or {},
        scratch_shapes=list(scratch),
        compiler_params=pltpu.CompilerParams(vmem_limit_bytes=limit * 1024 * 1024),
        cost_estimate=pl.CostEstimate(flops=int(time * 1.1e9), bytes_accessed=0, transcendentals=0),
    )(*(array for array, _ in args))


def vmem(*arrays):
    return [(array, VMEM) for array in arrays]


def hbm(*arrays):
    return [(array, HBM) for array in arrays]


def anywhere(*arrays):
    return [(array, ANY) for array in arrays]


def tied(x, *after):
    return call(lambda *refs: None, like(*x.shape), anywhere(x, *after), alias={0: 0}, spaces=ANY, limit=1, time=0.01)


def fetch(copies):
    for copy in copies:
        copy.start()
    return copies


def ready(copies):
    for copy in copies:
        copy.wait()


def through(moves, sems):
    ins = [pltpu.make_async_copy(source, buffer, sems.at[0, n]) for n, (source, buffer, _) in enumerate(moves)]
    outs = [pltpu.make_async_copy(buffer, target, sems.at[1, n]) for n, (_, buffer, target) in enumerate(moves)]
    fetch(ins)
    for first, second in zip(ins, outs):
        first.wait()
        second.start()
    ready(outs)


def columns_of(core, width):
    return [pl.ds(pl.multiple_of(n * width, width), width) for n in (core, 1 - core)]


def join_kernel(query, key, value, mask, got, q2, kv2, odd, side):
    core = this_core()
    rows, width = got.shape[0], q2.shape[1]
    mine, _ = columns_of(core, width)
    here, there = (pl.ds(pl.multiple_of(n * rows, rows), rows) for n in (core, 1 - core))
    q2[here, :] = query[0, :, mine]
    q2[there, :] = got[:, 0:width]
    kept = jnp.concatenate([key[0, :, mine], value[0, :, mine]], axis=1)
    sent = got[:, width : 3 * width]
    kv2[here, :] = kept
    kv2[there, :] = sent
    odd[...] = jnp.where(core == 1, kept, sent)
    side[here, :] = seen_by(mask, rows)
    side[there, :] = got[:, 3 * width :]


def seen_by(mask, rows):
    at = lax.broadcasted_iota(jnp.int32, (SIDE, rows), 0)
    sees = jnp.zeros((SIDE, rows), F32)
    for w in range(1, WIN):
        flag = jnp.where((mask[0, 0, w - 1] == 1) & (lax.axis_index("ctx") >= w), 1.0, 0.0)
        sees = jnp.where(at == w - 1, flag, sees)
    return sees.astype(BF)


def shift_kernel(own, other, up, down):
    lane = this_lane()
    rows = own.shape[0] // 2

    def put(first, last):
        up[0:rows] = first[rows : 2 * rows]
        up[rows : 3 * rows] = last[...]
        down[0 : 2 * rows] = first[...]
        down[2 * rows : 3 * rows] = last[0:rows]

    pl.when(lane == 0)(lambda: put(own, other))
    pl.when(lane != 0)(lambda: put(other, own))


def around_kernel(other, below, above, before, after):
    lane = this_lane()
    rows = other.shape[0] // 2

    @pl.when(lane == 0)
    def _():
        before[...] = below[...]
        after[0 : 2 * rows] = other[...]
        after[2 * rows :] = above[0:rows]

    @pl.when(lane != 0)
    def _():
        before[0:rows] = below[2 * rows :]
        before[rows:] = other[...]
        after[...] = above[...]


def split_moves(query, key, value, blocks, sent):
    width = query.shape[2] // 2
    _, others = columns_of(this_core(), width)
    return [
        (ref.at[0, :, others], blocks.at[n], sent.at[:, pl.ds(n * width, width)])
        for n, ref in enumerate((query, key, value))
    ]


def split_kernel(mask, query, key, value, sent, blocks, seen, sems, seen_sem):
    through(split_moves(query, key, value, blocks, sent), sems)
    send_seen(mask, seen, sent, seen_sem)


def send_seen(mask, seen, sent, sem):
    rows = seen.shape[1]
    seen[...] = seen_by(mask, rows)
    copy = pltpu.make_async_copy(seen, sent.at[:, pl.ds(sent.shape[1] - rows, rows)], sem)
    copy.start()
    copy.wait()


def cut_kernel(
    mask, gate, up, down, query, key, value, inner, down_half, sent, parts, down_parts, blocks, seen, sems, seen_sem
):
    def moves(matrix, buffers, out):
        pieces, size = buffers.shape[:2]
        start = this_core() * pieces * size
        return [
            (matrix.at[pl.ds(start + n * size, size)], buffers.at[n], out.at[pl.ds(n * size, size)])
            for n in range(pieces)
        ]

    through(
        split_moves(query, key, value, blocks, sent)
        + moves(gate, parts.at[0], inner.at[0])
        + moves(up, parts.at[1], inner.at[1])
        + moves(down, down_parts, down_half),
        sems,
    )
    send_seen(mask, seen, sent, seen_sem)


def cots_kernel(keep, got, side, whole, even, odd):
    core = this_core()
    rows, width = keep.shape[0], keep.shape[1] - SIDE
    for ref, block in ((keep, core), (got, 1 - core)):
        here = pl.ds(pl.multiple_of(block * rows, rows), rows)
        filled = (ref[:, width:].astype(F32) + side[here, :].astype(F32)).astype(BF)
        whole[here, 0:width] = ref[:, 0:width]
        whole[here, width:] = filled

        @pl.when(block == 0)
        def _():
            even[:, 0:width] = ref[:, 0:width]
            even[:, width:] = filled

        @pl.when(block == 1)
        def _():
            odd[:, 0:width] = ref[:, 0:width]
            odd[:, width:] = filled


def window_refs(far, near, own, rows):
    return {-3: (far, 0), -2: (near, 0), -1: (near, rows), 0: (own, 0), 1: (own, rows)}


def stacked(window, js, rows, here):
    return jnp.concatenate([window[j][0][pl.ds(window[j][1], rows), here] for j in js], axis=0)


def each_head(heads, one, step=2):
    def some(n, carry):
        for at in range(step):
            one(step * n + at)
        return carry

    lax.fori_loop(0, heads // step, some, 0)


def attend_kernel(size, far, near, own, q2, flags, *rest):
    side, keep, send, levels = rest[-4:]
    rows, width = far.shape[0], far.shape[1] // 2
    heads = width // size
    scale = size ** (-0.5)
    core = this_core()
    window = window_refs(far, near, own, rows)
    causal = causal_of(rows)
    seen = [flags[block * rows : block * rows + LEVEL, :].astype(F32) for block in range(PAIR)]

    def one(head):
        here = pl.ds(pl.multiple_of(head * size, size), size)
        there = pl.ds(pl.multiple_of(width + head * size, size), size)
        outs = []
        for block in range(PAIR):
            js = list(range(block - WIN + 1, block + 1))
            q = q2[pl.ds(block * rows, rows), here]
            scores = nt(stacked(window, js, rows, here), q) * scale
            parts = [
                scores[n * rows : (n + 1) * rows] - hidden_by(seen[block][block - j - 1 : block - j])
                if j < block
                else jnp.where(causal, scores[n * rows : (n + 1) * rows], -FAR)
                for n, j in enumerate(js)
            ]
            scores = jnp.concatenate(parts, axis=0)
            top = jnp.max(scores, axis=0, keepdims=True)
            weights = jnp.exp(scores - top)
            total = jnp.sum(weights, axis=0, keepdims=True)
            probs = weights * (1.0 / total)
            levels[block, pl.ds(head, 1), :] = top + jnp.log(total)
            outs.append(tn(probs.astype(BF), stacked(window, js, rows, there)).astype(BF))
        keep[:, here] = jnp.where(core == 0, outs[0], outs[1])
        send[:, here] = jnp.where(core == 0, outs[1], outs[0])

    each_head(heads, one)
    for block in range(PAIR):
        filled = jnp.concatenate(
            [seen[block], terms_of(levels[block]), jnp.zeros((SIDE - LEVEL - 3 * heads, rows), F32)], axis=0
        )
        side[block * rows : (block + 1) * rows, :] = filled.astype(BF)


def scores_back(q, cot, level, delta, seen, keys, values, js, t, causal, scale):
    rows = q.shape[0]
    scores = nt(keys, q) * scale
    parts = []
    for n, j in enumerate(js):
        part = scores[n * rows : (n + 1) * rows]
        if j < t:
            part = part - (level + hidden_by(seen[t - j - 1 : t - j]))
        else:
            part = jnp.where(causal, part - level, -FAR)
        parts.append(part)
    probs = jnp.exp(jnp.concatenate(parts, axis=0))
    return probs, (probs * (nt(values, cot) - delta)).astype(BF)


def add_blocks(sums, js, terms, rows):
    for n, j in enumerate(js):
        term = terms[n * rows : (n + 1) * rows]
        sums[j] = sums[j] + term if j in sums else term


def own_grads_kernel(
    size, far, near, own, q2, co, probs_out, probs_low_out, grads_q, q_keep, q_send, key_sums, value_sums, levels, deltas,
):
    rows, width = far.shape[0], far.shape[1] // 2
    heads = width // size
    scale = size ** (-0.5)
    core = this_core()
    window = window_refs(far, near, own, rows)
    causal = causal_of(rows)
    sides = [co[t * rows : (t + 1) * rows, width:].astype(F32) for t in range(PAIR)]
    for t in range(PAIR):
        levels[t] = rows_of(sides[t], LEVEL, heads)
        deltas[t] = rows_of(sides[t], DELTA, heads)

    def one(head):
        here = pl.ds(pl.multiple_of(head * size, size), size)
        there = pl.ds(pl.multiple_of(width + head * size, size), size)
        keys_at, values_at, grads = {}, {}, []
        for t in range(PAIR):
            place = pl.ds(t * rows, rows)
            js = list(range(t - WIN + 1, t + 1))
            q, cot = q2[place, here], co[place, here]
            keys = stacked(window, js, rows, here)
            probs, score_grad = scores_back(
                q, cot, levels[t, pl.ds(head, 1), :], deltas[t, pl.ds(head, 1), :], sides[t][0:LEVEL],
                keys, stacked(window, js, rows, there), js, t, causal, scale,
            )
            probs_low = probs.astype(BF)
            probs_out[head, t] = probs_low
            probs_low_out[head, t] = probs_low.T
            add_blocks(keys_at, js, nn(score_grad, q), rows)
            add_blocks(values_at, js, nn(probs_low, cot), rows)
            grads.append((tn(score_grad, keys) * scale).astype(BF))
            grads_q[place, here] = grads[t]
        q_keep[:, here] = jnp.where(core == 0, grads[0], grads[1])
        q_send[:, here] = jnp.where(core == 0, grads[1], grads[0])
        for j in keys_at:
            place = pl.ds((j + WIN - 1) * rows, rows)
            key_sums[place, here] = keys_at[j]
            value_sums[place, here] = values_at[j]

    each_head(heads, one)


def grads_kernel(
    size, far, near, own, q2, q_before, q_after, cfb, cnb, cna, cfa, probs_in, probs_low_in, grads_q,
    key_sums, value_sums, after, keep, send, tans_keep, tans_send, levels, deltas,
):
    rows, width = far.shape[0], far.shape[1] // 2
    heads = width // size
    scale = size ** (-0.5)
    core = this_core()
    window = window_refs(far, near, own, rows)
    causal = causal_of(rows)
    others = (
        (-3, q_before, 0, cfb, 0), (-2, q_before, 1, cnb, 0), (-1, q_before, 2, cnb, 1),
        (2, q_after, 0, cna, 0), (3, q_after, 1, cna, 1), (4, q_after, 2, cfa, 0),
    )
    sides = [c_ref[half * rows : (half + 1) * rows, width:].astype(F32) for _, _, _, c_ref, half in others]
    for n, side in enumerate(sides):
        levels[n] = rows_of(side, LEVEL, heads)
        deltas[n] = rows_of(side, DELTA, heads)

    def one(head):
        at = pl.multiple_of(head * size, size)
        here = pl.ds(at, size)
        there = pl.ds(pl.multiple_of(width + at, size), size)
        blocks = range(1 - WIN, PAIR)
        keys_at = {j: key_sums[pl.ds((j + WIN - 1) * rows, rows), here] for j in blocks}
        values_at = {j: value_sums[pl.ds((j + WIN - 1) * rows, rows), here] for j in blocks}
        for n, (t, q_ref, q_half, c_ref, half) in enumerate(others):
            js = list(range(max(1 - WIN, t - WIN + 1), min(1, t) + 1))
            q, cot = q_ref[pl.ds(q_half * rows, rows), here], c_ref[pl.ds(half * rows, rows), here]
            keys = stacked(window, js, rows, here)
            values = stacked(window, js, rows, there)
            probs, score_grad = scores_back(
                q, cot, levels[n, pl.ds(head, 1), :], deltas[n, pl.ds(head, 1), :], sides[n][0:8],
                keys, values, js, t, causal, scale,
            )
            add_blocks(keys_at, js, nn(score_grad, q), rows)
            add_blocks(values_at, js, nn(probs.astype(BF), cot), rows)
        key_grads = {j: (keys_at[j] * scale).astype(BF) for j in blocks}
        value_grads = {j: values_at[j].astype(BF) for j in blocks}
        tans = []
        for t in range(PAIR):
            place = pl.ds(t * rows, rows)
            js = list(range(t - WIN + 1, t + 1))
            keys = stacked(window, js, rows, here)
            probs = probs_in[head, t].astype(F32)
            both_keys = jnp.concatenate([keys, jnp.concatenate([key_grads[j] for j in js], axis=0)], axis=1)
            both_rows = jnp.concatenate([grads_q[place, here], q2[place, here]], axis=1)
            tan_values = jnp.concatenate([value_grads[j] for j in js], axis=0)
            score_tan = nt(both_keys, both_rows) * scale
            mean = jnp.sum(probs * score_tan, axis=0, keepdims=True)
            prob_tan = (probs * (score_tan - mean)).astype(BF)
            tan = tn(prob_tan, stacked(window, js, rows, there)) + nn(probs_low_in[head, t], tan_values)
            tans.append(tan.astype(BF))
        for grads, tans_out, mine, other in ((keep, tans_keep, 0, 1), (send, tans_send, 1, 0)):
            grads[:, here] = jnp.where(core == 0, key_grads[mine], key_grads[other])
            grads[:, there] = jnp.where(core == 0, value_grads[mine], value_grads[other])
            tans_out[:, here] = jnp.where(core == 0, tans[mine], tans[other])

    each_head(heads, one)


def gather_kernel(q_keep, q_got, keep, got, out_q, out_k, out_v):
    core = this_core()
    width = q_keep.shape[1]
    for owner, q, kv in ((core, q_keep, keep), (1 - core, q_got, got)):
        columns = pl.ds(pl.multiple_of(owner * width, width), width)
        out_q[:, columns] = q[...]
        out_k[:, columns] = kv[:, 0:width]
        out_v[:, columns] = kv[:, width:]


def cot_payload(size, cot, attended):
    rows, width = cot.shape
    heads = width // size
    lanes = lax.broadcasted_iota(jnp.int32, (rows, SIDE), 1)
    sums = jnp.zeros((rows, SIDE), F32)
    for head in range(heads):
        here = slice(head * size, (head + 1) * size)
        delta = jnp.sum(cot[:, here].astype(F32) * attended[:, here].astype(F32), axis=1, keepdims=True)
        sums = jnp.where(lanes == head, delta, sums)
    blank = jnp.zeros((DELTA, rows), F32)
    rest = jnp.zeros((SIDE - DELTA - 3 * heads, rows), F32)
    side = jnp.concatenate([blank, terms_of(sums.T[0:heads]), rest], axis=0)
    return jnp.concatenate([cot, side.astype(BF)], axis=1)


def in_order(core, kept, got):
    return jnp.where(
        core == 0, jnp.concatenate([kept, got], axis=1), jnp.concatenate([got, kept], axis=1)
    )


def pair_of(a, b, bit):
    return jnp.where(bit == 0, a, b), jnp.where(bit == 0, b, a)


def down_of_other(hidden, core, over, over_s):
    half = hidden.shape[1] // 2
    mine, others = pair_of(hidden[:, :half], hidden[:, half:], core)
    return nn(mine, over[...]) + nn(others, over_s[...])


def hidden_grad_kernel(cot, down, out):
    out[...] = nt(cot[0], down[...])


def middle_of(chosen, gate_pre, up_value, back, hidden, slope_up, active):
    activated, slope = silu_parts(gate_pre)
    activated = activated * chosen
    slope = slope * up_value * chosen
    hidden[...] = (activated * up_value).astype(BF)
    slope_up[...] = slope
    active[...] = activated
    return (back * slope).astype(BF), (back * activated).astype(BF)


def own_expert_kernel(keep, got, picks, back, gate, up, sum_keep, sum_got, hidden, slope_up, active):
    mine, others = columns_of(this_core(), keep.shape[1])
    rows_keep, rows_got = keep[...], got[...]

    def inner(ref):
        return nn(rows_keep, ref[mine, :]) + nn(rows_got, ref[others, :])

    gate_grad, up_grad = middle_of(picks[:, 0:1], inner(gate), inner(up), back[...], hidden, slope_up, active)
    for here, out in ((mine, sum_keep), (others, sum_got)):
        out[...] = nt(gate_grad, gate[here, :]) + nt(up_grad, up[here, :])


def other_expert_kernel(
    size, keep, got, cot, picks, sum_keep, sum_got, inner, inner_s, over, over_s,
    cot_keep, cot_send, hidden, slope_up, active,
):
    core = this_core()
    mine, others = columns_of(core, keep.shape[1])
    rows_keep, rows_got = keep[...], got[...]
    cots = cot[0]
    back = jnp.concatenate(pair_of(nt(cots, over[...]), nt(cots, over_s[...]), core), axis=1)
    gate_pre, up_value = (nn(rows_keep, inner[n]) + nn(rows_got, inner_s[n]) for n in range(2))
    gate_grad, up_grad = middle_of(picks[:, 1:2], gate_pre, up_value, back, hidden, slope_up, active)
    weight = picks[:, 2:3]
    for here, attended, so_far, ref, out in (
        (others, rows_got, sum_got, inner_s, cot_send),
        (mine, rows_keep, sum_keep, inner, cot_keep),
    ):
        summed = so_far[...] + nt(gate_grad, ref[0]) + nt(up_grad, ref[1])
        attn_cot = (cot[0, :, here].astype(F32) + summed.astype(BF).astype(F32) * weight).astype(BF)
        out[...] = cot_payload(size, attn_cot, attended)


def layer_kernel(keep, got, hidden_own, hidden, picks, down, over, over_s, after, out):
    core = this_core()
    rows_in = in_order(core, keep[...], got[...]).astype(F32)
    summed = nn(hidden_own[...], down[...]) + down_of_other(hidden[...], core, over, over_s)
    out[...] = (rows_in + summed.astype(BF).astype(F32) * picks[:, 2:3]).astype(BF)


def tangent_kernel(
    keep, got, slope_up_own, active_own, slope_up, active, picks, gate, up, inner, inner_s, down, over, over_s, out
):
    core = this_core()
    rows_keep, rows_got = keep[...], got[...]
    rows_in = in_order(core, rows_keep, rows_got)
    hidden = slope_up_own[...] * nn(rows_in, gate[...]) + active_own[...] * nn(rows_in, up[...])
    summed = nn(hidden.astype(BF), down[...])
    gate_tan, up_tan = (nn(rows_keep, inner[n]) + nn(rows_got, inner_s[n]) for n in range(2))
    hidden = slope_up[...] * gate_tan + active[...] * up_tan
    summed = summed + down_of_other(hidden.astype(BF), core, over, over_s)
    out[...] = (rows_in.astype(F32) + summed.astype(BF).astype(F32) * picks[:, 2:3]).astype(BF)


class PairExperts:
    def __init__(self, index, own_rows, mask, upstream, route_ids, route_weights, w_gate, w_up, w_down):
        own = lax.axis_index("exp")
        self.upstream = upstream
        mine = (route_ids == own).astype(F32)
        self.picks = jnp.concatenate([mine, 1.0 - mine, route_weights], axis=1)
        rows, wide = upstream.shape[1:]
        units = w_gate.shape[1]
        pieces = 4
        inner, down_half, self.mates = call(
            cut_kernel,
            (like(2, wide // 2, units), like(units // 2, wide), like(rows, 3 * wide // 2 + SIDE)),
            [(mask, SMEM)] + hbm(w_gate, w_up, w_down, *own_rows),
            [
                pltpu.VMEM((2, pieces, wide // 2 // pieces, units), BF),
                pltpu.VMEM((pieces, units // 2 // pieces, wide), BF),
                pltpu.VMEM((3, rows, wide // 2), BF),
                pltpu.VMEM((SIDE, rows), BF),
                pltpu.SemaphoreType.DMA((2, 3 * pieces + 3)),
                pltpu.SemaphoreType.DMA(()),
            ],
            limit=60,
            spaces=(HBM, HBM, HBM),
        )
        self.inner, self.over = crossed(inner), crossed(down_half)
        self.whole = (w_gate, w_up, w_down)
        self.rows, self.wide, self.units = rows, wide, units
        self.back_own = call(
            hidden_grad_kernel, like(rows, units, kind=F32), vmem(upstream, w_down), time=1.5
        )

    def before(self):
        return [self.back_own]

    def forward(self, size, keep, got, after):
        rows, wide, units = self.rows, self.wide, self.units
        w_gate, w_up, w_down = self.whole
        half, inner = like(rows, wide // PAIR + SIDE), like(rows, units, kind=F32)
        sums = like(rows, wide // PAIR, kind=F32)
        sum_keep, sum_got, hidden_own, *own_slopes = call(
            own_expert_kernel,
            (sums, sums, like(rows, units), inner, inner),
            vmem(keep, got, self.picks, self.back_own, w_gate, w_up),
            time=0.1,
        )
        inner_o, over = tied(self.inner, keep), tied(self.over, sum_keep, after)
        self.down = (w_down, over, swapped(over))
        self.inner = (inner_o, swapped(inner_o))
        cot_keep, cot_send, hidden, *slopes = call(
            functools.partial(other_expert_kernel, size),
            (half, half, like(rows, units), inner, inner),
            vmem(keep, got, self.upstream, self.picks, sum_keep, sum_got, *self.inner, *self.down[1:]),
            time=4.5,
        )
        self.slopes = own_slopes + slopes

        def layer(after):
            return call(
                layer_kernel,
                like(rows, wide),
                vmem(keep, got, hidden_own, hidden, self.picks, *self.down) + anywhere(after),
                time=3,
            )

        return cot_keep, cot_send, layer

    def tangent(self, keep, got):
        return call(
            tangent_kernel,
            like(self.rows, self.wide),
            vmem(keep, got, *self.slopes, self.picks, *self.whole[:2], *self.inner, *self.down),
            time=4.5,
        )


def routing_table(route_rows, experts, capacity):
    flat_ids = route_rows.reshape(-1)
    one_hot = (flat_ids[:, None] == jnp.arange(experts, dtype=jnp.int32)[None, :]).astype(jnp.int32)
    slot_rank = jnp.sum((jnp.cumsum(one_hot, axis=0) - one_hot) * one_hot, axis=1)
    target = flat_ids * capacity + slot_rank
    return (jnp.arange(experts * capacity, dtype=jnp.int32)[:, None] == target[None, :]).astype(
        jnp.bfloat16
    )


def dispatch(slot_table, row_block, routes, experts):
    pair_rows = jnp.repeat(row_block, routes, axis=0)
    sent = jnp.dot(slot_table, pair_rows, preferred_element_type=jnp.float32).astype(jnp.bfloat16)
    return sent.reshape(experts, -1, row_block.shape[1])


def combine(slot_table, returned, weights):
    rows_here, routes = weights.shape
    pair_vals = jnp.dot(
        slot_table.T, returned.reshape(-1, returned.shape[2]), preferred_element_type=jnp.float32
    )
    return jnp.sum(pair_vals.reshape(rows_here, routes, -1) * weights[:, :, None], axis=1)


def expert_forward(row_block, gate_matrix, up_matrix, down_matrix):
    gate_pre = jnp.dot(row_block, gate_matrix, preferred_element_type=jnp.float32)
    up_value = jnp.dot(row_block, up_matrix, preferred_element_type=jnp.float32)
    activated, slope_val = silu_parts(gate_pre)
    hidden = (activated * up_value).astype(jnp.bfloat16)
    return (
        jnp.dot(hidden, down_matrix, preferred_element_type=jnp.float32).astype(jnp.bfloat16),
        gate_pre,
        up_value,
    )


def expert_backward(cot_block, gate_pre, up_value, gate_matrix, up_matrix, down_matrix):
    hidden_grad = jnp.dot(cot_block, down_matrix.T, preferred_element_type=jnp.float32)
    activated, slope_val = silu_parts(gate_pre)
    gate_grad = (hidden_grad * up_value * slope_val).astype(jnp.bfloat16)
    up_grad = (hidden_grad * activated).astype(jnp.bfloat16)
    summed = jnp.dot(gate_grad, gate_matrix.T, preferred_element_type=jnp.float32) + jnp.dot(
        up_grad, up_matrix.T, preferred_element_type=jnp.float32
    )
    return summed.astype(jnp.bfloat16)


def expert_tangent(tan_block, gate_pre, up_value, gate_matrix, up_matrix, down_matrix):
    gate_tan = jnp.dot(tan_block, gate_matrix, preferred_element_type=jnp.float32)
    up_tan = jnp.dot(tan_block, up_matrix, preferred_element_type=jnp.float32)
    activated, slope_val = silu_parts(gate_pre)
    hidden_tan = (slope_val * gate_tan * up_value + activated * up_tan).astype(jnp.bfloat16)
    return jnp.dot(hidden_tan, down_matrix, preferred_element_type=jnp.float32).astype(jnp.bfloat16)


class RoutedExperts:
    def __init__(self, index, own_rows, mask, upstream, route_ids, route_weights, w_gate, w_up, w_down):
        rows, routes = route_ids.shape
        self.experts = lax.axis_size("exp")
        self.routes = routes
        capacity = min(rows, 2 * rows * routes // self.experts)
        self.core, self.upstream, self.weights = index % 2, upstream[0], route_weights
        self.matrices = (w_gate, w_up, w_down)
        self.table = routing_table(route_ids, self.experts, capacity)
        self.got_cots = self.sent(self.upstream)
        wide = self.upstream.shape[1]
        self.mates = call(
            split_kernel,
            like(rows, 3 * wide // 2 + SIDE),
            [(mask, SMEM)] + hbm(*own_rows),
            [
                pltpu.VMEM((3, rows, wide // 2), BF),
                pltpu.VMEM((SIDE, rows), BF),
                pltpu.SemaphoreType.DMA((2, 3)),
                pltpu.SemaphoreType.DMA(()),
            ],
            limit=20,
            spaces=HBM,
        )

    def before(self):
        return [self.got_cots]

    def across(self, x):
        return lax.all_to_all(x, "exp", split_axis=0, concat_axis=0, tiled=True)

    def sent(self, x):
        return self.across(dispatch(self.table, x, self.routes, self.experts))

    def returned(self, x):
        back = self.across(x.reshape(self.got_cots.shape))
        return combine(self.table, back, self.weights)

    def forward(self, size, keep, got, after):
        attended = in_order(self.core, keep, got)
        rows, wide = attended.shape
        got_rows = self.sent(attended).reshape(-1, wide)
        expert_out, self.gate_pre, self.up_value = expert_forward(got_rows, *self.matrices)
        route_grad = expert_backward(
            self.got_cots.reshape(-1, wide), self.gate_pre, self.up_value, *self.matrices
        )
        attn_cot = (self.upstream.astype(F32) + self.returned(route_grad)).astype(BF)
        layer_out = (attended.astype(F32) + self.returned(expert_out)).astype(BF)

        def kernel(cot, kept, got, cot_keep, cot_send):
            width = kept.shape[1]
            for part, attended, out in ((this_core(), kept, cot_keep), (1 - this_core(), got, cot_send)):
                here = pl.ds(pl.multiple_of(part * width, width), width)
                out[...] = cot_payload(size, cot[:, here], attended[...])

        half = like(rows, wide // PAIR + SIDE)
        cot_keep, cot_send = call(
            kernel, (half, half), vmem(attn_cot, keep, got)
        )
        return cot_keep, cot_send, lambda after: layer_out

    def tangent(self, keep, got):
        rows = in_order(self.core, keep, got)
        got_rows = self.sent(rows).reshape(-1, rows.shape[1])
        out = expert_tangent(got_rows, self.gate_pre, self.up_value, *self.matrices)
        return (rows.astype(F32) + self.returned(out)).astype(BF)


def neighbours(whole, even, odd):
    return (
        moved(odd, 2 * PAIR),
        moved(whole, PAIR),
        moved(whole, -PAIR),
        moved(even, -2 * PAIR),
    )


def local(query, key, value, cotangent, route_ids, route_weights, block_mask, w_gate, w_up, w_down):
    rows, wide = query.shape[1:]
    width = wide // PAIR
    size = wide // HEADS
    heads = width // size
    index = lax.axis_index("ctx")
    core = index % PAIR

    pair = lax.axis_size("exp") == 2 and route_ids.shape[2] == 1
    experts = (PairExperts if pair else RoutedExperts)(
        index, (query, key, value), block_mask, cotangent, route_ids[0], route_weights[0], w_gate[0], w_up[0], w_down[0]
    )
    half, pairs = like(rows, width), like(2 * rows, width)
    q2, own, odd, side = call(
        join_kernel,
        (pairs, like(2 * rows, wide), like(rows, wide), like(2 * rows, SIDE)),
        vmem(query, key, value) + [(block_mask, SMEM)] + vmem(swapped(experts.mates)),
    )
    near, far = moved(own, PAIR), moved(odd, 2 * PAIR)
    three = like(3 * rows, width)
    q_other = swapped(q2, 2)
    q_up, q_down = call(shift_kernel, (three, three), vmem(q2, q_other))
    side, keep, send = call(
        functools.partial(attend_kernel, size),
        (
            like(2 * rows, SIDE),
            half,
            half,
        ),
        vmem(far, near, own, q2, side) + anywhere(q_up, *experts.before()),
        [pltpu.VMEM((PAIR, heads, rows), F32)],
        time=0.1,
    )
    got = swapped(send)
    q_below, q_above = moved(q_up, 2 * PAIR), moved(q_down, -2 * PAIR)
    q_before, q_after = call(around_kernel, (three, three), vmem(q_other, q_below, q_above))

    cot_keep, cot_send, layer = experts.forward(size, keep, got, q_before)
    payload = wide // PAIR + SIDE
    co, co_even, co_odd = call(
        cots_kernel,
        (like(2 * rows, payload), like(rows, payload), like(rows, payload)),
        vmem(cot_keep, swapped(cot_send), side),
    )
    cfb, cnb, cna, cfa = neighbours(co, co_even, co_odd)

    layer_out = layer(co)
    sums = like((WIN + 1) * rows, width, kind=F32)
    probs, probs_low, grads_q, q_keep, q_send, key_sums, value_sums = call(
        functools.partial(own_grads_kernel, size),
        (
            like(heads, PAIR, WIN * rows, rows),
            like(heads, PAIR, rows, WIN * rows),
            pairs, half, half, sums, sums,
        ),
        vmem(far, near, own, q2, co),
        [pltpu.VMEM((2, heads, rows), F32)] * 2,
        time=7,
    )
    q_got = swapped(q_send)
    kv_half = like(rows, 2 * width)
    kv_keep, kv_send, tan_keep, tan_send = call(
        functools.partial(grads_kernel, size),
        (kv_half, kv_half, half, half),
        vmem(far, near, own, q2, q_before, q_after, cfb, cnb, cna, cfa)
        + vmem(probs, probs_low, grads_q, key_sums, value_sums)
        + anywhere(layer_out),
        [pltpu.VMEM((6, heads, rows), F32)] * 2,
        time=16,
    )
    tan_got = swapped(tan_send)
    kv_got = swapped(kv_send)
    tangent_out = experts.tangent(tan_keep, tan_got)
    out = like(rows, wide)
    outs = call(gather_kernel, (out, out, out), vmem(q_keep, q_got, kv_keep, kv_got))
    return (layer_out[None], *(x[None] for x in outs), tangent_out[None])


def solution(mesh):
    return jax.shard_map(
        local,
        mesh=mesh,
        in_specs=(
            P("exp", "ctx", None),
            P("exp", "ctx", None),
            P("exp", "ctx", None),
            P("exp", "ctx", None),
            P("exp", "ctx", None),
            P("exp", "ctx", None),
            P("exp", "ctx", None),
            P("exp", None, None),
            P("exp", None, None),
            P("exp", None, None),
        ),
        out_specs=(
            P("exp", "ctx", None),
            P("exp", "ctx", None),
            P("exp", "ctx", None),
            P("exp", "ctx", None),
            P("exp", "ctx", None),
        ),
        check_vma=False,
    )
```

```python
import functools

import jax
import jax.numpy as jnp
from jax import lax
from jax.experimental import pallas as pl
from jax.experimental.pallas import tpu as pltpu
from jax.sharding import PartitionSpec as P

HEADS = 16
WIN = 4
PAIR = 2
SIDE = 128
FAR = 1e30
BF = jnp.bfloat16
F32 = jnp.float32
VMEM = pl.BlockSpec(memory_space=pltpu.VMEM)
SMEM = pl.BlockSpec(memory_space=pltpu.SMEM)
ANY = pl.BlockSpec(memory_space=pl.ANY)
HBM = pl.BlockSpec(memory_space=pltpu.HBM)


def moved(x, by):
    devices = lax.axis_size("ctx")
    pairs = [(i, i + by) for i in range(devices) if 0 <= i + by < devices]
    return lax.ppermute(x, "ctx", pairs)


def swapped(x, bit=1):
    return lax.ppermute(x, "ctx", [(i, i ^ bit) for i in range(lax.axis_size("ctx"))])


def this_core():
    return lax.axis_index("ctx") % PAIR


def this_lane():
    return lax.axis_index("ctx") // PAIR % 2


def crossed(x):
    return lax.ppermute(x, "exp", [(0, 1), (1, 0)])


def nn(a, b):
    return lax.dot_general(a, b, (((1,), (0,)), ((), ())), preferred_element_type=F32)


def nt(a, b):
    return lax.dot_general(a, b, (((1,), (1,)), ((), ())), preferred_element_type=F32)


def tn(a, b):
    return lax.dot_general(a, b, (((0,), (0,)), ((), ())), preferred_element_type=F32)


def silu_parts(gate_pre):
    sigmoid_val = jax.nn.sigmoid(gate_pre)
    return (gate_pre * sigmoid_val, sigmoid_val * (1.0 + gate_pre * (1.0 - sigmoid_val)))


LEVEL, DELTA = 8, 32


def terms_of(x):
    first = x.astype(BF).astype(F32)
    second = (x - first).astype(BF).astype(F32)
    return jnp.concatenate([first, second, x - first - second], axis=0)


def rows_of(side, at, heads):
    return sum(side[at + n * heads : at + (n + 1) * heads].astype(F32) for n in range(3))


def hidden_by(flag):
    return (1.0 - flag) * FAR


def causal_of(rows):
    return lax.broadcasted_iota(jnp.int32, (rows, rows), 1) >= lax.broadcasted_iota(
        jnp.int32, (rows, rows), 0
    )


def like(*shape, kind=BF):
    return jax.ShapeDtypeStruct(shape, kind)


def call(kernel, outs, args, scratch=(), time=1, limit=8, alias=None, spaces=None):
    return pl.pallas_call(
        kernel,
        out_shape=outs,
        in_specs=[space for _, space in args],
        out_specs=jax.tree.map(lambda _: VMEM, outs) if spaces is None else spaces,
        input_output_aliases=alias or {},
        scratch_shapes=list(scratch),
        compiler_params=pltpu.CompilerParams(vmem_limit_bytes=limit * 1024 * 1024),
        cost_estimate=pl.CostEstimate(flops=int(time * 1.1e9), bytes_accessed=0, transcendentals=0),
    )(*(array for array, _ in args))


def vmem(*arrays):
    return [(array, VMEM) for array in arrays]


def hbm(*arrays):
    return [(array, HBM) for array in arrays]


def anywhere(*arrays):
    return [(array, ANY) for array in arrays]


def tied(x, *after, time=0.01):
    out = like(*x.shape, kind=x.dtype)
    return call(lambda *refs: None, out, anywhere(x, *after), alias={0: 0}, spaces=ANY, limit=1, time=time)


def fetch(copies):
    for copy in copies:
        copy.start()
    return copies


def ready(copies):
    for copy in copies:
        copy.wait()


def through(moves, sems):
    ins = [pltpu.make_async_copy(source, buffer, sems.at[0, n]) for n, (source, buffer, _) in enumerate(moves)]
    outs = [pltpu.make_async_copy(buffer, target, sems.at[1, n]) for n, (_, buffer, target) in enumerate(moves)]
    fetch(ins)
    for first, second in zip(ins, outs):
        first.wait()
        second.start()
    ready(outs)


def columns_of(core, width):
    return [pl.ds(pl.multiple_of(n * width, width), width) for n in (core, 1 - core)]


def join_kernel(query, key, value, mask, got, q2, kv2, odd, side):
    core = this_core()
    rows, width = got.shape[0], q2.shape[1]
    mine, _ = columns_of(core, width)
    here, there = (pl.ds(pl.multiple_of(n * rows, rows), rows) for n in (core, 1 - core))
    q2[here, :] = query[0, :, mine]
    q2[there, :] = got[:, 0:width]
    kept = jnp.concatenate([key[0, :, mine], value[0, :, mine]], axis=1)
    sent = got[:, width : 3 * width]
    kv2[here, :] = kept
    kv2[there, :] = sent
    odd[...] = jnp.where(core == 1, kept, sent)
    side[here, :] = seen_by(mask, rows)
    side[there, :] = got[:, 3 * width :]


def seen_by(mask, rows):
    at = lax.broadcasted_iota(jnp.int32, (SIDE, rows), 0)
    sees = jnp.zeros((SIDE, rows), F32)
    for w in range(1, WIN):
        flag = jnp.where((mask[0, 0, w - 1] == 1) & (lax.axis_index("ctx") >= w), 1.0, 0.0)
        sees = jnp.where(at == w - 1, flag, sees)
    return sees.astype(BF)


def shift_kernel(own, other, up, down):
    lane = this_lane()
    rows = own.shape[0] // 2

    def put(first, last):
        up[0:rows] = first[rows : 2 * rows]
        up[rows : 3 * rows] = last[...]
        down[0 : 2 * rows] = first[...]
        down[2 * rows : 3 * rows] = last[0:rows]

    pl.when(lane == 0)(lambda: put(own, other))
    pl.when(lane != 0)(lambda: put(other, own))


def around_kernel(other, below, above, before, after):
    lane = this_lane()
    rows = other.shape[0] // 2

    @pl.when(lane == 0)
    def _():
        before[...] = below[...]
        after[0 : 2 * rows] = other[...]
        after[2 * rows :] = above[0:rows]

    @pl.when(lane != 0)
    def _():
        before[0:rows] = below[2 * rows :]
        before[rows:] = other[...]
        after[...] = above[...]


def split_moves(query, key, value, blocks, sent):
    width = query.shape[2] // 2
    _, others = columns_of(this_core(), width)
    return [
        (ref.at[0, :, others], blocks.at[n], sent.at[:, pl.ds(n * width, width)])
        for n, ref in enumerate((query, key, value))
    ]


def split_kernel(mask, query, key, value, sent, blocks, seen, sems, seen_sem):
    through(split_moves(query, key, value, blocks, sent), sems)
    send_seen(mask, seen, sent, seen_sem)


def send_seen(mask, seen, sent, sem):
    rows = seen.shape[1]
    seen[...] = seen_by(mask, rows)
    copy = pltpu.make_async_copy(seen, sent.at[:, pl.ds(sent.shape[1] - rows, rows)], sem)
    copy.start()
    copy.wait()


def cut_kernel(
    mask, gate, up, down, query, key, value, inner, down_half, sent, parts, down_parts, blocks, seen, sems, seen_sem
):
    def moves(matrix, buffers, out):
        pieces, size = buffers.shape[:2]
        start = this_core() * pieces * size
        return [
            (matrix.at[pl.ds(start + n * size, size)], buffers.at[n], out.at[pl.ds(n * size, size)])
            for n in range(pieces)
        ]

    through(
        split_moves(query, key, value, blocks, sent)
        + moves(gate, parts.at[0], inner.at[0])
        + moves(up, parts.at[1], inner.at[1])
        + moves(down, down_parts, down_half),
        sems,
    )
    send_seen(mask, seen, sent, seen_sem)


def cots_kernel(keep, got, side, whole, even, odd):
    core = this_core()
    rows, width = keep.shape[0], keep.shape[1] - SIDE
    for ref, block in ((keep, core), (got, 1 - core)):
        here = pl.ds(pl.multiple_of(block * rows, rows), rows)
        filled = (ref[:, width:].astype(F32) + side[here, :].astype(F32)).astype(BF)
        whole[here, 0:width] = ref[:, 0:width]
        whole[here, width:] = filled

        @pl.when(block == 0)
        def _():
            even[:, 0:width] = ref[:, 0:width]
            even[:, width:] = filled

        @pl.when(block == 1)
        def _():
            odd[:, 0:width] = ref[:, 0:width]
            odd[:, width:] = filled


def window_refs(far, near, own, rows):
    return {-3: (far, 0), -2: (near, 0), -1: (near, rows), 0: (own, 0), 1: (own, rows)}


def stacked(window, js, rows, here):
    return jnp.concatenate([window[j][0][pl.ds(window[j][1], rows), here] for j in js], axis=0)


def each_head(heads, one, step=2):
    def some(n, carry):
        for at in range(step):
            one(step * n + at)
        return carry

    lax.fori_loop(0, heads // step, some, 0)


def attend_kernel(size, far, near, own, q2, flags, *rest):
    side, keep, send, levels = rest[-4:]
    rows, width = far.shape[0], far.shape[1] // 2
    heads = width // size
    scale = size ** (-0.5)
    core = this_core()
    window = window_refs(far, near, own, rows)
    causal = causal_of(rows)
    seen = [flags[block * rows : block * rows + LEVEL, :].astype(F32) for block in range(PAIR)]

    def one(head):
        here = pl.ds(pl.multiple_of(head * size, size), size)
        there = pl.ds(pl.multiple_of(width + head * size, size), size)
        outs = []
        for block in range(PAIR):
            js = list(range(block - WIN + 1, block + 1))
            q = q2[pl.ds(block * rows, rows), here]
            scores = nt(stacked(window, js, rows, here), q) * scale
            parts = [
                scores[n * rows : (n + 1) * rows] - hidden_by(seen[block][block - j - 1 : block - j])
                if j < block
                else jnp.where(causal, scores[n * rows : (n + 1) * rows], -FAR)
                for n, j in enumerate(js)
            ]
            scores = jnp.concatenate(parts, axis=0)
            top = jnp.max(scores, axis=0, keepdims=True)
            weights = jnp.exp(scores - top)
            total = jnp.sum(weights, axis=0, keepdims=True)
            probs = weights * (1.0 / total)
            levels[block, pl.ds(head, 1), :] = top + jnp.log(total)
            outs.append(tn(probs.astype(BF), stacked(window, js, rows, there)).astype(BF))
        keep[:, here] = jnp.where(core == 0, outs[0], outs[1])
        send[:, here] = jnp.where(core == 0, outs[1], outs[0])

    each_head(heads, one)
    for block in range(PAIR):
        filled = jnp.concatenate(
            [seen[block], terms_of(levels[block]), jnp.zeros((SIDE - LEVEL - 3 * heads, rows), F32)], axis=0
        )
        side[block * rows : (block + 1) * rows, :] = filled.astype(BF)


def scores_back(q, cot, level, delta, seen, keys, values, js, t, causal, scale):
    rows = q.shape[0]
    scores = nt(keys, q) * scale
    parts = []
    for n, j in enumerate(js):
        part = scores[n * rows : (n + 1) * rows]
        if j < t:
            part = part - (level + hidden_by(seen[t - j - 1 : t - j]))
        else:
            part = jnp.where(causal, part - level, -FAR)
        parts.append(part)
    probs = jnp.exp(jnp.concatenate(parts, axis=0))
    return probs, (probs * (nt(values, cot) - delta)).astype(BF)


def add_blocks(sums, js, terms, rows):
    for n, j in enumerate(js):
        term = terms[n * rows : (n + 1) * rows]
        sums[j] = sums[j] + term if j in sums else term


def own_grads_kernel(
    size, far, near, own, q2, co, probs_out, probs_low_out, grads_q, q_keep, q_send, key_sums, value_sums, levels, deltas,
):
    rows, width = far.shape[0], far.shape[1] // 2
    heads = width // size
    scale = size ** (-0.5)
    core = this_core()
    window = window_refs(far, near, own, rows)
    causal = causal_of(rows)
    sides = [co[t * rows : (t + 1) * rows, width:].astype(F32) for t in range(PAIR)]
    for t in range(PAIR):
        levels[t] = rows_of(sides[t], LEVEL, heads)
        deltas[t] = rows_of(sides[t], DELTA, heads)

    def one(head):
        here = pl.ds(pl.multiple_of(head * size, size), size)
        there = pl.ds(pl.multiple_of(width + head * size, size), size)
        keys_at, values_at, grads = {}, {}, []
        for t in range(PAIR):
            place = pl.ds(t * rows, rows)
            js = list(range(t - WIN + 1, t + 1))
            q, cot = q2[place, here], co[place, here]
            keys = stacked(window, js, rows, here)
            probs, score_grad = scores_back(
                q, cot, levels[t, pl.ds(head, 1), :], deltas[t, pl.ds(head, 1), :], sides[t][0:LEVEL],
                keys, stacked(window, js, rows, there), js, t, causal, scale,
            )
            probs_low = probs.astype(BF)
            probs_out[head, t] = probs_low
            probs_low_out[head, t] = probs_low.T
            add_blocks(keys_at, js, nn(score_grad, q), rows)
            add_blocks(values_at, js, nn(probs_low, cot), rows)
            grads.append((tn(score_grad, keys) * scale).astype(BF))
            grads_q[place, here] = grads[t]
        q_keep[:, here] = jnp.where(core == 0, grads[0], grads[1])
        q_send[:, here] = jnp.where(core == 0, grads[1], grads[0])
        for j in keys_at:
            place = pl.ds((j + WIN - 1) * rows, rows)
            key_sums[place, here] = keys_at[j]
            value_sums[place, here] = values_at[j]

    each_head(heads, one)


def grads_kernel(
    size, far, near, own, q2, q_before, q_after, cfb, cnb, cna, cfa, probs_in, probs_low_in, grads_q,
    key_sums, value_sums, after, keep, send, tans_keep, tans_send, levels, deltas,
):
    rows, width = far.shape[0], far.shape[1] // 2
    heads = width // size
    scale = size ** (-0.5)
    core = this_core()
    window = window_refs(far, near, own, rows)
    causal = causal_of(rows)
    others = (
        (-3, q_before, 0, cfb, 0), (-2, q_before, 1, cnb, 0), (-1, q_before, 2, cnb, 1),
        (2, q_after, 0, cna, 0), (3, q_after, 1, cna, 1), (4, q_after, 2, cfa, 0),
    )
    sides = [c_ref[half * rows : (half + 1) * rows, width:].astype(F32) for _, _, _, c_ref, half in others]
    for n, side in enumerate(sides):
        levels[n] = rows_of(side, LEVEL, heads)
        deltas[n] = rows_of(side, DELTA, heads)

    def one(head):
        at = pl.multiple_of(head * size, size)
        here = pl.ds(at, size)
        there = pl.ds(pl.multiple_of(width + at, size), size)
        blocks = range(1 - WIN, PAIR)
        keys_at = {j: key_sums[pl.ds((j + WIN - 1) * rows, rows), here] for j in blocks}
        values_at = {j: value_sums[pl.ds((j + WIN - 1) * rows, rows), here] for j in blocks}
        score_grads, probs_at, qs, cots = {}, {}, {}, {}
        for n, (t, q_ref, q_half, c_ref, half) in enumerate(others):
            js = list(range(max(1 - WIN, t - WIN + 1), min(1, t) + 1))
            q, cot = q_ref[pl.ds(q_half * rows, rows), here], c_ref[pl.ds(half * rows, rows), here]
            keys = stacked(window, js, rows, here)
            values = stacked(window, js, rows, there)
            probs, score_grad = scores_back(
                q, cot, levels[n, pl.ds(head, 1), :], deltas[n, pl.ds(head, 1), :], sides[n][0:8],
                keys, values, js, t, causal, scale,
            )
            probs = probs.astype(BF)
            qs[t], cots[t] = q, cot
            for m, j in enumerate(js):
                score_grads[j, t] = score_grad[m * rows : (m + 1) * rows]
                probs_at[j, t] = probs[m * rows : (m + 1) * rows]
        for j in blocks:
            ts = [t for t in qs if (j, t) in probs_at]
            keys_at[j] = keys_at[j] + nn(
                jnp.concatenate([score_grads[j, t] for t in ts], axis=1), jnp.concatenate([qs[t] for t in ts], axis=0)
            )
            values_at[j] = values_at[j] + nn(
                jnp.concatenate([probs_at[j, t] for t in ts], axis=1), jnp.concatenate([cots[t] for t in ts], axis=0)
            )
        key_grads = {j: (keys_at[j] * scale).astype(BF) for j in blocks}
        value_grads = {j: values_at[j].astype(BF) for j in blocks}
        tans = []
        for t in range(PAIR):
            place = pl.ds(t * rows, rows)
            js = list(range(t - WIN + 1, t + 1))
            keys = stacked(window, js, rows, here)
            probs = probs_in[head, t].astype(F32)
            both_keys = jnp.concatenate([keys, jnp.concatenate([key_grads[j] for j in js], axis=0)], axis=1)
            both_rows = jnp.concatenate([grads_q[place, here], q2[place, here]], axis=1)
            tan_values = jnp.concatenate([value_grads[j] for j in js], axis=0)
            score_tan = nt(both_keys, both_rows) * scale
            mean = jnp.sum(probs * score_tan, axis=0, keepdims=True)
            prob_tan = (probs * (score_tan - mean)).astype(BF)
            tan = tn(prob_tan, stacked(window, js, rows, there)) + nn(probs_low_in[head, t], tan_values)
            tans.append(tan.astype(BF))
        for grads, tans_out, mine, other in ((keep, tans_keep, 0, 1), (send, tans_send, 1, 0)):
            grads[:, here] = jnp.where(core == 0, key_grads[mine], key_grads[other])
            grads[:, there] = jnp.where(core == 0, value_grads[mine], value_grads[other])
            tans_out[:, here] = jnp.where(core == 0, tans[mine], tans[other])

    each_head(heads, one, 4)


def gather_kernel(q_keep, q_got, keep, got, out_q, out_k, out_v):
    core = this_core()
    width = q_keep.shape[1]
    for owner, q, kv in ((core, q_keep, keep), (1 - core, q_got, got)):
        columns = pl.ds(pl.multiple_of(owner * width, width), width)
        out_q[:, columns] = q[...]
        out_k[:, columns] = kv[:, 0:width]
        out_v[:, columns] = kv[:, width:]


def cot_payload(size, cot, attended):
    rows, width = cot.shape
    heads = width // size
    lanes = lax.broadcasted_iota(jnp.int32, (rows, SIDE), 1)
    sums = jnp.zeros((rows, SIDE), F32)
    for head in range(heads):
        here = slice(head * size, (head + 1) * size)
        delta = jnp.sum(cot[:, here].astype(F32) * attended[:, here].astype(F32), axis=1, keepdims=True)
        sums = jnp.where(lanes == head, delta, sums)
    blank = jnp.zeros((DELTA, rows), F32)
    rest = jnp.zeros((SIDE - DELTA - 3 * heads, rows), F32)
    side = jnp.concatenate([blank, terms_of(sums.T[0:heads]), rest], axis=0)
    return jnp.concatenate([cot, side.astype(BF)], axis=1)


def in_order(core, kept, got):
    return jnp.where(
        core == 0, jnp.concatenate([kept, got], axis=1), jnp.concatenate([got, kept], axis=1)
    )


def pair_of(a, b, bit):
    return jnp.where(bit == 0, a, b), jnp.where(bit == 0, b, a)


def down_of_other(hidden, core, over, over_s):
    half = hidden.shape[1] // 2
    mine, others = pair_of(hidden[:, :half], hidden[:, half:], core)
    return nn(mine, over[...]) + nn(others, over_s[...])


def hidden_grad_kernel(cot, down, out):
    out[...] = nt(cot[0], down[...])


def middle_of(chosen, gate_pre, up_value, back, hidden, slope_up, active):
    activated, slope = silu_parts(gate_pre)
    activated = activated * chosen
    slope = slope * up_value * chosen
    hidden[...] = (activated * up_value).astype(BF)
    slope_up[...] = slope
    active[...] = activated
    return (back * slope).astype(BF), (back * activated).astype(BF)


def own_expert_kernel(keep, got, picks, back, gate, up, sum_keep, sum_got, hidden, slope_up, active):
    mine, others = columns_of(this_core(), keep.shape[1])
    rows_keep, rows_got = keep[...], got[...]

    def inner(ref):
        return nn(rows_keep, ref[mine, :]) + nn(rows_got, ref[others, :])

    gate_grad, up_grad = middle_of(picks[:, 0:1], inner(gate), inner(up), back[...], hidden, slope_up, active)
    for here, out in ((mine, sum_keep), (others, sum_got)):
        out[...] = nt(gate_grad, gate[here, :]) + nt(up_grad, up[here, :])


def stream(pairs, sems):
    copies = fetch([pltpu.make_async_copy(source, buffer, sems.at[n]) for n, (source, buffer) in enumerate(pairs)])

    def waiting(n):
        def get():
            copies[n].wait()
            return pairs[n][1][...]

        return get

    return [waiting(n) for n in range(len(pairs))]


def other_expert_kernel(
    size, keep, got, cot, picks, sum_keep, sum_got, inner, inner_s, over, over_s,
    cot_keep, cot_send, hidden, slope_up, active,
):
    core = this_core()
    mine, others = columns_of(core, keep.shape[1])
    rows_keep, rows_got = keep[...], got[...]
    cots = cot[0]
    back = jnp.concatenate(pair_of(nt(cots, over[...]), nt(cots, over_s[...]), core), axis=1)
    gate_pre, up_value = (nn(rows_keep, inner[n]) + nn(rows_got, inner_s[n]) for n in range(2))
    gate_grad, up_grad = middle_of(picks[:, 1:2], gate_pre, up_value, back, hidden, slope_up, active)
    weight = picks[:, 2:3]
    for here, attended, so_far, ref, out in (
        (others, rows_got, sum_got, inner_s, cot_send),
        (mine, rows_keep, sum_keep, inner, cot_keep),
    ):
        summed = so_far[...] + nt(gate_grad, ref[0]) + nt(up_grad, ref[1])
        attn_cot = (cot[0, :, here].astype(F32) + summed.astype(BF).astype(F32) * weight).astype(BF)
        out[...] = cot_payload(size, attn_cot, attended)


def layer_kernel(keep, got, hidden_own, hidden, picks, down, over, over_s, *rest):
    out = rest[-1]
    core = this_core()
    rows_in = in_order(core, keep[...], got[...]).astype(F32)
    summed = nn(hidden_own[...], down[...]) + down_of_other(hidden[...], core, over, over_s)
    out[...] = (rows_in + summed.astype(BF).astype(F32) * picks[:, 2:3]).astype(BF)


def tangent_kernel(
    keep, got, slope_up_own, active_own, slope_up, active, picks, gate, up, inner, inner_s, down, over, over_s, out,
    inners, overs, sems,
):
    core = this_core()
    gate_o, gate_s, up_o, up_s, over, over_s = stream(
        [(ref.at[n], inners.at[m, n]) for n in range(2) for m, ref in enumerate((inner, inner_s))]
        + [(over, overs.at[0]), (over_s, overs.at[1])],
        sems,
    )
    rows_keep, rows_got = keep[...], got[...]
    rows_in = in_order(core, rows_keep, rows_got)
    hidden = slope_up_own[...] * nn(rows_in, gate[...]) + active_own[...] * nn(rows_in, up[...])
    summed = nn(hidden.astype(BF), down[...])
    gate_tan = nn(rows_keep, gate_o()) + nn(rows_got, gate_s())
    up_tan = nn(rows_keep, up_o()) + nn(rows_got, up_s())
    hidden = slope_up[...] * gate_tan + active[...] * up_tan
    summed = summed + down_of_other(hidden.astype(BF), core, over(), over_s())
    out[...] = (rows_in.astype(F32) + summed.astype(BF).astype(F32) * picks[:, 2:3]).astype(BF)


class PairExperts:
    def __init__(self, index, own_rows, mask, upstream, route_ids, route_weights, w_gate, w_up, w_down):
        own = lax.axis_index("exp")
        self.upstream = upstream
        mine = (route_ids == own).astype(F32)
        self.picks = jnp.concatenate([mine, 1.0 - mine, route_weights], axis=1)
        rows, wide = upstream.shape[1:]
        units = w_gate.shape[1]
        pieces = 4
        inner, down_half, self.mates = call(
            cut_kernel,
            (like(2, wide // 2, units), like(units // 2, wide), like(rows, 3 * wide // 2 + SIDE)),
            [(mask, SMEM)] + hbm(w_gate, w_up, w_down, *own_rows),
            [
                pltpu.VMEM((2, pieces, wide // 2 // pieces, units), BF),
                pltpu.VMEM((pieces, units // 2 // pieces, wide), BF),
                pltpu.VMEM((3, rows, wide // 2), BF),
                pltpu.VMEM((SIDE, rows), BF),
                pltpu.SemaphoreType.DMA((2, 3 * pieces + 3)),
                pltpu.SemaphoreType.DMA(()),
            ],
            limit=60,
            spaces=(HBM, HBM, HBM),
        )
        self.inner, self.over = crossed(inner), crossed(down_half)
        self.whole = (w_gate, w_up, w_down)
        self.rows, self.wide, self.units = rows, wide, units
        self.back_own = call(
            hidden_grad_kernel, like(rows, units, kind=F32), vmem(upstream, w_down), time=1.5
        )

    def before(self):
        return [self.back_own]

    def forward(self, size, keep, got, after):
        rows, wide, units = self.rows, self.wide, self.units
        w_gate, w_up, w_down = self.whole
        half, inner = like(rows, wide // PAIR + SIDE), like(rows, units, kind=F32)
        sums = like(rows, wide // PAIR, kind=F32)
        sum_keep, sum_got, hidden_own, *own_slopes = call(
            own_expert_kernel,
            (sums, sums, like(rows, units), inner, inner),
            vmem(keep, got, self.picks, self.back_own, w_gate, w_up),
            time=0.1,
        )
        inner_o, over = tied(self.inner, keep), tied(self.over, sum_keep)
        sum_got = tied(sum_got, *after, time=6)
        self.down = (w_down, over, swapped(over))
        self.inner = (inner_o, swapped(inner_o))
        cot_keep, cot_send, hidden, *slopes = call(
            functools.partial(other_expert_kernel, size),
            (half, half, like(rows, units), inner, inner),
            vmem(keep, got, self.upstream, self.picks, sum_keep, sum_got, *self.inner, *self.down[1:]),
            time=4.5,
        )
        self.slopes = own_slopes + slopes

        def layer(*after):
            return call(
                layer_kernel,
                like(rows, wide),
                vmem(keep, got, hidden_own, hidden, self.picks, *self.down) + anywhere(*after),
                time=3,
            )

        return cot_keep, cot_send, layer

    def tangent(self, keep, got):
        return call(
            tangent_kernel,
            like(self.rows, self.wide),
            vmem(keep, got, *self.slopes, self.picks, *self.whole[:2])
            + anywhere(*self.inner)
            + vmem(self.down[0])
            + anywhere(*self.down[1:]),
            [
                pltpu.VMEM((2, 2, self.wide // 2, self.units), BF),
                pltpu.VMEM((2, self.units // 2, self.wide), BF),
                pltpu.SemaphoreType.DMA((6,)),
            ],
            time=4.5,
            limit=16,
        )


def routing_table(route_rows, experts, capacity):
    flat_ids = route_rows.reshape(-1)
    one_hot = (flat_ids[:, None] == jnp.arange(experts, dtype=jnp.int32)[None, :]).astype(jnp.int32)
    slot_rank = jnp.sum((jnp.cumsum(one_hot, axis=0) - one_hot) * one_hot, axis=1)
    target = flat_ids * capacity + slot_rank
    return (jnp.arange(experts * capacity, dtype=jnp.int32)[:, None] == target[None, :]).astype(
        jnp.bfloat16
    )


def dispatch(slot_table, row_block, routes, experts):
    pair_rows = jnp.repeat(row_block, routes, axis=0)
    sent = jnp.dot(slot_table, pair_rows, preferred_element_type=jnp.float32).astype(jnp.bfloat16)
    return sent.reshape(experts, -1, row_block.shape[1])


def combine(slot_table, returned, weights):
    rows_here, routes = weights.shape
    pair_vals = jnp.dot(
        slot_table.T, returned.reshape(-1, returned.shape[2]), preferred_element_type=jnp.float32
    )
    return jnp.sum(pair_vals.reshape(rows_here, routes, -1) * weights[:, :, None], axis=1)


def expert_forward(row_block, gate_matrix, up_matrix, down_matrix):
    gate_pre = jnp.dot(row_block, gate_matrix, preferred_element_type=jnp.float32)
    up_value = jnp.dot(row_block, up_matrix, preferred_element_type=jnp.float32)
    activated, slope_val = silu_parts(gate_pre)
    hidden = (activated * up_value).astype(jnp.bfloat16)
    return (
        jnp.dot(hidden, down_matrix, preferred_element_type=jnp.float32).astype(jnp.bfloat16),
        gate_pre,
        up_value,
    )


def expert_backward(cot_block, gate_pre, up_value, gate_matrix, up_matrix, down_matrix):
    hidden_grad = jnp.dot(cot_block, down_matrix.T, preferred_element_type=jnp.float32)
    activated, slope_val = silu_parts(gate_pre)
    gate_grad = (hidden_grad * up_value * slope_val).astype(jnp.bfloat16)
    up_grad = (hidden_grad * activated).astype(jnp.bfloat16)
    summed = jnp.dot(gate_grad, gate_matrix.T, preferred_element_type=jnp.float32) + jnp.dot(
        up_grad, up_matrix.T, preferred_element_type=jnp.float32
    )
    return summed.astype(jnp.bfloat16)


def expert_tangent(tan_block, gate_pre, up_value, gate_matrix, up_matrix, down_matrix):
    gate_tan = jnp.dot(tan_block, gate_matrix, preferred_element_type=jnp.float32)
    up_tan = jnp.dot(tan_block, up_matrix, preferred_element_type=jnp.float32)
    activated, slope_val = silu_parts(gate_pre)
    hidden_tan = (slope_val * gate_tan * up_value + activated * up_tan).astype(jnp.bfloat16)
    return jnp.dot(hidden_tan, down_matrix, preferred_element_type=jnp.float32).astype(jnp.bfloat16)


class RoutedExperts:
    def __init__(self, index, own_rows, mask, upstream, route_ids, route_weights, w_gate, w_up, w_down):
        rows, routes = route_ids.shape
        self.experts = lax.axis_size("exp")
        self.routes = routes
        capacity = min(rows, 2 * rows * routes // self.experts)
        self.core, self.upstream, self.weights = index % 2, upstream[0], route_weights
        self.matrices = (w_gate, w_up, w_down)
        self.table = routing_table(route_ids, self.experts, capacity)
        self.got_cots = self.sent(self.upstream)
        wide = self.upstream.shape[1]
        self.mates = call(
            split_kernel,
            like(rows, 3 * wide // 2 + SIDE),
            [(mask, SMEM)] + hbm(*own_rows),
            [
                pltpu.VMEM((3, rows, wide // 2), BF),
                pltpu.VMEM((SIDE, rows), BF),
                pltpu.SemaphoreType.DMA((2, 3)),
                pltpu.SemaphoreType.DMA(()),
            ],
            limit=20,
            spaces=HBM,
        )

    def before(self):
        return [self.got_cots]

    def across(self, x):
        return lax.all_to_all(x, "exp", split_axis=0, concat_axis=0, tiled=True)

    def sent(self, x):
        return self.across(dispatch(self.table, x, self.routes, self.experts))

    def returned(self, x):
        back = self.across(x.reshape(self.got_cots.shape))
        return combine(self.table, back, self.weights)

    def forward(self, size, keep, got, after):
        attended = in_order(self.core, keep, got)
        rows, wide = attended.shape
        got_rows = self.sent(attended).reshape(-1, wide)
        expert_out, self.gate_pre, self.up_value = expert_forward(got_rows, *self.matrices)
        route_grad = expert_backward(
            self.got_cots.reshape(-1, wide), self.gate_pre, self.up_value, *self.matrices
        )
        attn_cot = (self.upstream.astype(F32) + self.returned(route_grad)).astype(BF)
        layer_out = (attended.astype(F32) + self.returned(expert_out)).astype(BF)

        def kernel(cot, kept, got, cot_keep, cot_send):
            width = kept.shape[1]
            for part, attended, out in ((this_core(), kept, cot_keep), (1 - this_core(), got, cot_send)):
                here = pl.ds(pl.multiple_of(part * width, width), width)
                out[...] = cot_payload(size, cot[:, here], attended[...])

        half = like(rows, wide // PAIR + SIDE)
        cot_keep, cot_send = call(
            kernel, (half, half), vmem(attn_cot, keep, got)
        )
        return cot_keep, cot_send, lambda *after: layer_out

    def tangent(self, keep, got):
        rows = in_order(self.core, keep, got)
        got_rows = self.sent(rows).reshape(-1, rows.shape[1])
        out = expert_tangent(got_rows, self.gate_pre, self.up_value, *self.matrices)
        return (rows.astype(F32) + self.returned(out)).astype(BF)


def neighbours(whole, even, odd):
    return (
        moved(odd, 2 * PAIR),
        moved(whole, PAIR),
        moved(whole, -PAIR),
        moved(even, -2 * PAIR),
    )


def local(query, key, value, cotangent, route_ids, route_weights, block_mask, w_gate, w_up, w_down):
    rows, wide = query.shape[1:]
    width = wide // PAIR
    size = wide // HEADS
    heads = width // size
    index = lax.axis_index("ctx")
    core = index % PAIR

    pair = lax.axis_size("exp") == 2 and route_ids.shape[2] == 1
    experts = (PairExperts if pair else RoutedExperts)(
        index, (query, key, value), block_mask, cotangent, route_ids[0], route_weights[0], w_gate[0], w_up[0], w_down[0]
    )
    half, pairs = like(rows, width), like(2 * rows, width)
    q2, own, odd, side = call(
        join_kernel,
        (pairs, like(2 * rows, wide), like(rows, wide), like(2 * rows, SIDE)),
        vmem(query, key, value) + [(block_mask, SMEM)] + vmem(swapped(experts.mates)),
    )
    near, far = moved(own, PAIR), moved(odd, 2 * PAIR)
    three = like(3 * rows, width)
    q_other = swapped(q2, 2)
    q_up, q_down = call(shift_kernel, (three, three), vmem(q2, q_other))
    side, keep, send = call(
        functools.partial(attend_kernel, size),
        (
            like(2 * rows, SIDE),
            half,
            half,
        ),
        vmem(far, near, own, q2, side) + anywhere(q_up, *experts.before()),
        [pltpu.VMEM((PAIR, heads, rows), F32)],
        time=0.1,
    )
    got = swapped(send)
    q_below, q_above = moved(q_up, 2 * PAIR), moved(q_down, -2 * PAIR)
    q_before, q_after = call(around_kernel, (three, three), vmem(q_other, q_below, q_above))

    cot_keep, cot_send, layer = experts.forward(size, keep, got, (q_below, q_above))
    payload = wide // PAIR + SIDE
    co, co_even, co_odd = call(
        cots_kernel,
        (like(2 * rows, payload), like(rows, payload), like(rows, payload)),
        vmem(cot_keep, swapped(cot_send), side),
    )
    cfb, cnb, cna, cfa = neighbours(co, co_even, co_odd)

    layer_out = layer(co, q_before)
    sums = like((WIN + 1) * rows, width, kind=F32)
    probs, probs_low, grads_q, q_keep, q_send, key_sums, value_sums = call(
        functools.partial(own_grads_kernel, size),
        (
            like(heads, PAIR, WIN * rows, rows),
            like(heads, PAIR, rows, WIN * rows),
            pairs, half, half, sums, sums,
        ),
        vmem(far, near, own, q2, co),
        [pltpu.VMEM((2, heads, rows), F32)] * 2,
        time=7,
    )
    q_got = swapped(q_send)
    kv_half = like(rows, 2 * width)
    kv_keep, kv_send, tan_keep, tan_send = call(
        functools.partial(grads_kernel, size),
        (kv_half, kv_half, half, half),
        vmem(far, near, own, q2, q_before, q_after, cfb, cnb, cna, cfa)
        + vmem(probs, probs_low, grads_q, key_sums, value_sums)
        + anywhere(layer_out),
        [pltpu.VMEM((6, heads, rows), F32)] * 2,
        time=16,
    )
    tan_got = swapped(tan_send)
    kv_got = swapped(kv_send)
    tangent_out = experts.tangent(tan_keep, tan_got)
    out = like(rows, wide)
    outs = call(gather_kernel, (out, out, out), vmem(q_keep, q_got, kv_keep, kv_got))
    return (layer_out[None], *(x[None] for x in outs), tangent_out[None])


def solution(mesh):
    return jax.shard_map(
        local,
        mesh=mesh,
        in_specs=(
            P("exp", "ctx", None),
            P("exp", "ctx", None),
            P("exp", "ctx", None),
            P("exp", "ctx", None),
            P("exp", "ctx", None),
            P("exp", "ctx", None),
            P("exp", "ctx", None),
            P("exp", None, None),
            P("exp", None, None),
            P("exp", None, None),
        ),
        out_specs=(
            P("exp", "ctx", None),
            P("exp", "ctx", None),
            P("exp", "ctx", None),
            P("exp", "ctx", None),
            P("exp", "ctx", None),
        ),
        check_vma=False,
    )
```

```python
import functools

import jax
import jax.numpy as jnp
from jax import lax
from jax.experimental import pallas as pl
from jax.experimental.pallas import tpu as pltpu
from jax.sharding import PartitionSpec as P

HEADS = 16
WIN = 4
PAIR = 2
SIDE = 128
FAR = 1e30
BF = jnp.bfloat16
F32 = jnp.float32
VMEM = pl.BlockSpec(memory_space=pltpu.VMEM)
SMEM = pl.BlockSpec(memory_space=pltpu.SMEM)
ANY = pl.BlockSpec(memory_space=pl.ANY)
HBM = pl.BlockSpec(memory_space=pltpu.HBM)


def moved(x, by):
    devices = lax.axis_size("ctx")
    pairs = [(i, i + by) for i in range(devices) if 0 <= i + by < devices]
    return lax.ppermute(x, "ctx", pairs)


def swapped(x, bit=1):
    return lax.ppermute(x, "ctx", [(i, i ^ bit) for i in range(lax.axis_size("ctx"))])


def this_core():
    return lax.axis_index("ctx") % PAIR


def this_lane():
    return lax.axis_index("ctx") // PAIR % 2


def crossed(x):
    return lax.ppermute(x, "exp", [(0, 1), (1, 0)])


def nn(a, b):
    return lax.dot_general(a, b, (((1,), (0,)), ((), ())), preferred_element_type=F32)


def nt(a, b):
    return lax.dot_general(a, b, (((1,), (1,)), ((), ())), preferred_element_type=F32)


def tn(a, b):
    return lax.dot_general(a, b, (((0,), (0,)), ((), ())), preferred_element_type=F32)


def silu_parts(gate_pre):
    sigmoid_val = jax.nn.sigmoid(gate_pre)
    return (gate_pre * sigmoid_val, sigmoid_val * (1.0 + gate_pre * (1.0 - sigmoid_val)))


LEVEL, DELTA = 8, 32


def terms_of(x):
    first = x.astype(BF).astype(F32)
    second = (x - first).astype(BF).astype(F32)
    return jnp.concatenate([first, second, x - first - second], axis=0)


def rows_of(side, at, heads):
    return sum(side[at + n * heads : at + (n + 1) * heads].astype(F32) for n in range(3))


def hidden_by(flag):
    return (1.0 - flag) * FAR


def causal_of(rows):
    return lax.broadcasted_iota(jnp.int32, (rows, rows), 1) >= lax.broadcasted_iota(
        jnp.int32, (rows, rows), 0
    )


def like(*shape, kind=BF):
    return jax.ShapeDtypeStruct(shape, kind)


def call(kernel, outs, args, scratch=(), time=1, limit=8, alias=None, spaces=None):
    return pl.pallas_call(
        kernel,
        out_shape=outs,
        in_specs=[space for _, space in args],
        out_specs=jax.tree.map(lambda _: VMEM, outs) if spaces is None else spaces,
        input_output_aliases=alias or {},
        scratch_shapes=list(scratch),
        compiler_params=pltpu.CompilerParams(vmem_limit_bytes=limit * 1024 * 1024),
        cost_estimate=pl.CostEstimate(flops=int(time * 1.1e9), bytes_accessed=0, transcendentals=0),
    )(*(array for array, _ in args))


def vmem(*arrays):
    return [(array, VMEM) for array in arrays]


def hbm(*arrays):
    return [(array, HBM) for array in arrays]


def anywhere(*arrays):
    return [(array, ANY) for array in arrays]


def tied(x, *after, time=0.01):
    out = like(*x.shape, kind=x.dtype)
    return call(lambda *refs: None, out, anywhere(x, *after), alias={0: 0}, spaces=ANY, limit=1, time=time)


def fetch(copies):
    for copy in copies:
        copy.start()
    return copies


def ready(copies):
    for copy in copies:
        copy.wait()


def through(moves, sems):
    ins = [pltpu.make_async_copy(source, buffer, sems.at[0, n]) for n, (source, buffer, _) in enumerate(moves)]
    outs = [pltpu.make_async_copy(buffer, target, sems.at[1, n]) for n, (_, buffer, target) in enumerate(moves)]
    fetch(ins)
    for first, second in zip(ins, outs):
        first.wait()
        second.start()
    ready(outs)


def columns_of(core, width):
    return [pl.ds(pl.multiple_of(n * width, width), width) for n in (core, 1 - core)]


def join_kernel(query, key, value, mask, got, q2, kv2, odd, side):
    core = this_core()
    rows, width = got.shape[0], q2.shape[1]
    mine, _ = columns_of(core, width)
    here, there = (pl.ds(pl.multiple_of(n * rows, rows), rows) for n in (core, 1 - core))
    q2[here, :] = query[0, :, mine]
    q2[there, :] = got[:, 0:width]
    kept = jnp.concatenate([key[0, :, mine], value[0, :, mine]], axis=1)
    sent = got[:, width : 3 * width]
    kv2[here, :] = kept
    kv2[there, :] = sent
    odd[...] = jnp.where(core == 1, kept, sent)
    side[here, :] = seen_by(mask, rows)
    side[there, :] = got[:, 3 * width :]


def seen_by(mask, rows):
    at = lax.broadcasted_iota(jnp.int32, (SIDE, rows), 0)
    sees = jnp.zeros((SIDE, rows), F32)
    for w in range(1, WIN):
        flag = jnp.where((mask[0, 0, w - 1] == 1) & (lax.axis_index("ctx") >= w), 1.0, 0.0)
        sees = jnp.where(at == w - 1, flag, sees)
    return sees.astype(BF)


def shift_kernel(own, other, up, down):
    lane = this_lane()
    rows = own.shape[0] // 2

    def put(first, last):
        up[0:rows] = first[rows : 2 * rows]
        up[rows : 3 * rows] = last[...]
        down[0 : 2 * rows] = first[...]
        down[2 * rows : 3 * rows] = last[0:rows]

    pl.when(lane == 0)(lambda: put(own, other))
    pl.when(lane != 0)(lambda: put(other, own))


def around_kernel(other, below, above, before, after):
    lane = this_lane()
    rows = other.shape[0] // 2

    @pl.when(lane == 0)
    def _():
        before[...] = below[...]
        after[0 : 2 * rows] = other[...]
        after[2 * rows :] = above[0:rows]

    @pl.when(lane != 0)
    def _():
        before[0:rows] = below[2 * rows :]
        before[rows:] = other[...]
        after[...] = above[...]


def split_moves(query, key, value, blocks, sent):
    width = query.shape[2] // 2
    _, others = columns_of(this_core(), width)
    return [
        (ref.at[0, :, others], blocks.at[n], sent.at[:, pl.ds(n * width, width)])
        for n, ref in enumerate((query, key, value))
    ]


def split_kernel(mask, query, key, value, sent, blocks, seen, sems, seen_sem):
    through(split_moves(query, key, value, blocks, sent), sems)
    send_seen(mask, seen, sent, seen_sem)


def send_seen(mask, seen, sent, sem):
    rows = seen.shape[1]
    seen[...] = seen_by(mask, rows)
    copy = pltpu.make_async_copy(seen, sent.at[:, pl.ds(sent.shape[1] - rows, rows)], sem)
    copy.start()
    copy.wait()


def half_moves(matrix, buffers, out):
    pieces, size = buffers.shape[:2]
    start = this_core() * pieces * size
    return [
        (matrix.at[pl.ds(start + n * size, size)], buffers.at[n], out.at[pl.ds(n * size, size)]) for n in range(pieces)
    ]


def inner_kernel(gate, up, inner, parts, sems):
    through([move for n, x in enumerate((gate, up)) for move in half_moves(x, parts.at[n], inner.at[n])], sems)


def cut_kernel(mask, down, query, key, value, after, down_half, sent, down_parts, blocks, seen, sems, seen_sem):
    moves = split_moves(query, key, value, blocks, sent) + half_moves(down, down_parts, down_half)
    through(moves, sems)
    send_seen(mask, seen, sent, seen_sem)


def cots_kernel(keep, got, side, whole, even, odd):
    core = this_core()
    rows, width = keep.shape[0], keep.shape[1] - SIDE
    for ref, block in ((keep, core), (got, 1 - core)):
        here = pl.ds(pl.multiple_of(block * rows, rows), rows)
        filled = (ref[:, width:].astype(F32) + side[here, :].astype(F32)).astype(BF)
        whole[here, 0:width] = ref[:, 0:width]
        whole[here, width:] = filled

        @pl.when(block == 0)
        def _():
            even[:, 0:width] = ref[:, 0:width]
            even[:, width:] = filled

        @pl.when(block == 1)
        def _():
            odd[:, 0:width] = ref[:, 0:width]
            odd[:, width:] = filled


def window_refs(far, near, own, rows):
    return {-3: (far, 0), -2: (near, 0), -1: (near, rows), 0: (own, 0), 1: (own, rows)}


def stacked(window, js, rows, here):
    return jnp.concatenate([window[j][0][pl.ds(window[j][1], rows), here] for j in js], axis=0)


def each_head(heads, one, step=2):
    def some(n, carry):
        for at in range(step):
            one(step * n + at)
        return carry

    lax.fori_loop(0, heads // step, some, 0)


def attend_kernel(size, far, near, own, q2, flags, *rest):
    side, keep, send, levels = rest[-4:]
    rows, width = far.shape[0], far.shape[1] // 2
    heads = width // size
    scale = size ** (-0.5)
    core = this_core()
    window = window_refs(far, near, own, rows)
    causal = causal_of(rows)
    seen = [flags[block * rows : block * rows + LEVEL, :].astype(F32) for block in range(PAIR)]

    def one(head):
        here = pl.ds(pl.multiple_of(head * size, size), size)
        there = pl.ds(pl.multiple_of(width + head * size, size), size)
        outs = []
        for block in range(PAIR):
            js = list(range(block - WIN + 1, block + 1))
            q = q2[pl.ds(block * rows, rows), here]
            scores = nt(stacked(window, js, rows, here), q) * scale
            parts = [
                scores[n * rows : (n + 1) * rows] - hidden_by(seen[block][block - j - 1 : block - j])
                if j < block
                else jnp.where(causal, scores[n * rows : (n + 1) * rows], -FAR)
                for n, j in enumerate(js)
            ]
            scores = jnp.concatenate(parts, axis=0)
            top = jnp.max(scores, axis=0, keepdims=True)
            weights = jnp.exp(scores - top)
            total = jnp.sum(weights, axis=0, keepdims=True)
            probs = weights * (1.0 / total)
            levels[block, pl.ds(head, 1), :] = top + jnp.log(total)
            outs.append(tn(probs.astype(BF), stacked(window, js, rows, there)).astype(BF))
        keep[:, here] = jnp.where(core == 0, outs[0], outs[1])
        send[:, here] = jnp.where(core == 0, outs[1], outs[0])

    each_head(heads, one)
    for block in range(PAIR):
        filled = jnp.concatenate(
            [seen[block], terms_of(levels[block]), jnp.zeros((SIDE - LEVEL - 3 * heads, rows), F32)], axis=0
        )
        side[block * rows : (block + 1) * rows, :] = filled.astype(BF)


def scores_back(q, cot, level, delta, seen, keys, values, js, t, causal, scale):
    rows = q.shape[0]
    scores = nt(keys, q) * scale
    parts = []
    for n, j in enumerate(js):
        part = scores[n * rows : (n + 1) * rows]
        if j < t:
            part = part - (level + hidden_by(seen[t - j - 1 : t - j]))
        else:
            part = jnp.where(causal, part - level, -FAR)
        parts.append(part)
    probs = jnp.exp(jnp.concatenate(parts, axis=0))
    return probs, (probs * (nt(values, cot) - delta)).astype(BF)


def add_blocks(sums, js, terms, rows):
    for n, j in enumerate(js):
        term = terms[n * rows : (n + 1) * rows]
        sums[j] = sums[j] + term if j in sums else term


def own_grads_kernel(
    size, far, near, own, q2, co, probs_out, probs_low_out, grads_q, q_keep, q_send, key_sums, value_sums, levels, deltas,
):
    rows, width = far.shape[0], far.shape[1] // 2
    heads = width // size
    scale = size ** (-0.5)
    core = this_core()
    window = window_refs(far, near, own, rows)
    causal = causal_of(rows)
    sides = [co[t * rows : (t + 1) * rows, width:].astype(F32) for t in range(PAIR)]
    for t in range(PAIR):
        levels[t] = rows_of(sides[t], LEVEL, heads)
        deltas[t] = rows_of(sides[t], DELTA, heads)

    def one(head):
        here = pl.ds(pl.multiple_of(head * size, size), size)
        there = pl.ds(pl.multiple_of(width + head * size, size), size)
        keys_at, values_at, grads = {}, {}, []
        for t in range(PAIR):
            place = pl.ds(t * rows, rows)
            js = list(range(t - WIN + 1, t + 1))
            q, cot = q2[place, here], co[place, here]
            keys = stacked(window, js, rows, here)
            probs, score_grad = scores_back(
                q, cot, levels[t, pl.ds(head, 1), :], deltas[t, pl.ds(head, 1), :], sides[t][0:LEVEL],
                keys, stacked(window, js, rows, there), js, t, causal, scale,
            )
            probs_low = probs.astype(BF)
            probs_out[head, t] = probs_low
            probs_low_out[head, t] = probs_low.T
            add_blocks(keys_at, js, nn(score_grad, q), rows)
            add_blocks(values_at, js, nn(probs_low, cot), rows)
            grads.append((tn(score_grad, keys) * scale).astype(BF))
            grads_q[place, here] = grads[t]
        q_keep[:, here] = jnp.where(core == 0, grads[0], grads[1])
        q_send[:, here] = jnp.where(core == 0, grads[1], grads[0])
        for j in keys_at:
            place = pl.ds((j + WIN - 1) * rows, rows)
            key_sums[place, here] = keys_at[j]
            value_sums[place, here] = values_at[j]

    each_head(heads, one)


def grads_kernel(
    size, far, near, own, q2, q_before, q_after, cfb, cnb, cna, cfa, probs_in, probs_low_in, grads_q,
    key_sums, value_sums, after, keep, send, tans_keep, tans_send, levels, deltas,
):
    rows, width = far.shape[0], far.shape[1] // 2
    heads = width // size
    scale = size ** (-0.5)
    core = this_core()
    window = window_refs(far, near, own, rows)
    causal = causal_of(rows)
    others = (
        (-3, q_before, 0, cfb, 0), (-2, q_before, 1, cnb, 0), (-1, q_before, 2, cnb, 1),
        (2, q_after, 0, cna, 0), (3, q_after, 1, cna, 1), (4, q_after, 2, cfa, 0),
    )
    sides = [c_ref[half * rows : (half + 1) * rows, width:].astype(F32) for _, _, _, c_ref, half in others]
    for n, side in enumerate(sides):
        levels[n] = rows_of(side, LEVEL, heads)
        deltas[n] = rows_of(side, DELTA, heads)

    def one(head):
        at = pl.multiple_of(head * size, size)
        here = pl.ds(at, size)
        there = pl.ds(pl.multiple_of(width + at, size), size)
        blocks = range(1 - WIN, PAIR)
        keys_at = {j: key_sums[pl.ds((j + WIN - 1) * rows, rows), here] for j in blocks}
        values_at = {j: value_sums[pl.ds((j + WIN - 1) * rows, rows), here] for j in blocks}
        score_grads, probs_at, qs, cots = {}, {}, {}, {}
        for n, (t, q_ref, q_half, c_ref, half) in enumerate(others):
            js = list(range(max(1 - WIN, t - WIN + 1), min(1, t) + 1))
            q, cot = q_ref[pl.ds(q_half * rows, rows), here], c_ref[pl.ds(half * rows, rows), here]
            keys = stacked(window, js, rows, here)
            values = stacked(window, js, rows, there)
            probs, score_grad = scores_back(
                q, cot, levels[n, pl.ds(head, 1), :], deltas[n, pl.ds(head, 1), :], sides[n][0:8],
                keys, values, js, t, causal, scale,
            )
            probs = probs.astype(BF)
            qs[t], cots[t] = q, cot
            for m, j in enumerate(js):
                score_grads[j, t] = score_grad[m * rows : (m + 1) * rows]
                probs_at[j, t] = probs[m * rows : (m + 1) * rows]
        for j in blocks:
            ts = [t for t in qs if (j, t) in probs_at]
            keys_at[j] = keys_at[j] + nn(
                jnp.concatenate([score_grads[j, t] for t in ts], axis=1), jnp.concatenate([qs[t] for t in ts], axis=0)
            )
            values_at[j] = values_at[j] + nn(
                jnp.concatenate([probs_at[j, t] for t in ts], axis=1), jnp.concatenate([cots[t] for t in ts], axis=0)
            )
        key_grads = {j: (keys_at[j] * scale).astype(BF) for j in blocks}
        value_grads = {j: values_at[j].astype(BF) for j in blocks}
        tans = []
        for t in range(PAIR):
            place = pl.ds(t * rows, rows)
            js = list(range(t - WIN + 1, t + 1))
            keys = stacked(window, js, rows, here)
            probs = probs_in[head, t].astype(F32)
            both_keys = jnp.concatenate([keys, jnp.concatenate([key_grads[j] for j in js], axis=0)], axis=1)
            both_rows = jnp.concatenate([grads_q[place, here], q2[place, here]], axis=1)
            tan_values = jnp.concatenate([value_grads[j] for j in js], axis=0)
            score_tan = nt(both_keys, both_rows) * scale
            mean = jnp.sum(probs * score_tan, axis=0, keepdims=True)
            prob_tan = (probs * (score_tan - mean)).astype(BF)
            tan = tn(prob_tan, stacked(window, js, rows, there)) + nn(probs_low_in[head, t], tan_values)
            tans.append(tan.astype(BF))
        for grads, tans_out, mine, other in ((keep, tans_keep, 0, 1), (send, tans_send, 1, 0)):
            grads[:, here] = jnp.where(core == 0, key_grads[mine], key_grads[other])
            grads[:, there] = jnp.where(core == 0, value_grads[mine], value_grads[other])
            tans_out[:, here] = jnp.where(core == 0, tans[mine], tans[other])

    each_head(heads, one, 4)


def gather_kernel(q_keep, q_got, keep, got, out_q, out_k, out_v):
    core = this_core()
    width = q_keep.shape[1]
    for owner, q, kv in ((core, q_keep, keep), (1 - core, q_got, got)):
        columns = pl.ds(pl.multiple_of(owner * width, width), width)
        out_q[:, columns] = q[...]
        out_k[:, columns] = kv[:, 0:width]
        out_v[:, columns] = kv[:, width:]


def cot_payload(size, cot, attended):
    rows, width = cot.shape
    heads = width // size
    lanes = lax.broadcasted_iota(jnp.int32, (rows, SIDE), 1)
    sums = jnp.zeros((rows, SIDE), F32)
    for head in range(heads):
        here = slice(head * size, (head + 1) * size)
        delta = jnp.sum(cot[:, here].astype(F32) * attended[:, here].astype(F32), axis=1, keepdims=True)
        sums = jnp.where(lanes == head, delta, sums)
    blank = jnp.zeros((DELTA, rows), F32)
    rest = jnp.zeros((SIDE - DELTA - 3 * heads, rows), F32)
    side = jnp.concatenate([blank, terms_of(sums.T[0:heads]), rest], axis=0)
    return jnp.concatenate([cot, side.astype(BF)], axis=1)


def in_order(core, kept, got):
    return jnp.where(
        core == 0, jnp.concatenate([kept, got], axis=1), jnp.concatenate([got, kept], axis=1)
    )


def pair_of(a, b, bit):
    return jnp.where(bit == 0, a, b), jnp.where(bit == 0, b, a)


def down_of_other(hidden, core, over, over_s):
    half = hidden.shape[1] // 2
    mine, others = pair_of(hidden[:, :half], hidden[:, half:], core)
    return nn(mine, over[...]) + nn(others, over_s[...])


def hidden_grad_kernel(cot, down, out):
    out[...] = nt(cot[0], down[...])


def middle_of(chosen, gate_pre, up_value, back, hidden, slope_up, active):
    activated, slope = silu_parts(gate_pre)
    activated = activated * chosen
    slope = slope * up_value * chosen
    hidden[...] = (activated * up_value).astype(BF)
    slope_up[...] = slope
    active[...] = activated
    return (back * slope).astype(BF), (back * activated).astype(BF)


def own_expert_kernel(keep, got, picks, back, gate, up, sum_keep, sum_got, hidden, slope_up, active):
    mine, others = columns_of(this_core(), keep.shape[1])
    rows_keep, rows_got = keep[...], got[...]

    def inner(ref):
        return nn(rows_keep, ref[mine, :]) + nn(rows_got, ref[others, :])

    gate_grad, up_grad = middle_of(picks[:, 0:1], inner(gate), inner(up), back[...], hidden, slope_up, active)
    for here, out in ((mine, sum_keep), (others, sum_got)):
        out[...] = nt(gate_grad, gate[here, :]) + nt(up_grad, up[here, :])


def stream(pairs, sems):
    copies = fetch([pltpu.make_async_copy(source, buffer, sems.at[n]) for n, (source, buffer) in enumerate(pairs)])

    def waiting(n):
        def get():
            copies[n].wait()
            return pairs[n][1][...]

        return get

    return [waiting(n) for n in range(len(pairs))]


def other_expert_kernel(
    size, keep, got, cot, picks, sum_keep, sum_got, inner, inner_s, over, over_s,
    cot_keep, cot_send, hidden, slope_up, active,
):
    core = this_core()
    mine, others = columns_of(core, keep.shape[1])
    rows_keep, rows_got = keep[...], got[...]
    cots = cot[0]
    back = jnp.concatenate(pair_of(nt(cots, over[...]), nt(cots, over_s[...]), core), axis=1)
    gate_pre, up_value = (nn(rows_keep, inner[n]) + nn(rows_got, inner_s[n]) for n in range(2))
    gate_grad, up_grad = middle_of(picks[:, 1:2], gate_pre, up_value, back, hidden, slope_up, active)
    weight = picks[:, 2:3]
    for here, attended, so_far, ref, out in (
        (others, rows_got, sum_got, inner_s, cot_send),
        (mine, rows_keep, sum_keep, inner, cot_keep),
    ):
        summed = so_far[...] + nt(gate_grad, ref[0]) + nt(up_grad, ref[1])
        attn_cot = (cot[0, :, here].astype(F32) + summed.astype(BF).astype(F32) * weight).astype(BF)
        out[...] = cot_payload(size, attn_cot, attended)


def layer_kernel(keep, got, hidden_own, hidden, picks, down, over, over_s, *rest):
    out, done = rest[-2:]
    done[...] = jnp.zeros_like(done)
    core = this_core()
    rows_in = in_order(core, keep[...], got[...]).astype(F32)
    summed = nn(hidden_own[...], down[...]) + down_of_other(hidden[...], core, over, over_s)
    out[...] = (rows_in + summed.astype(BF).astype(F32) * picks[:, 2:3]).astype(BF)


def tangent_kernel(
    keep, got, slope_up_own, active_own, slope_up, active, picks, gate, up, inner, inner_s, down, over, over_s, out,
    inners, overs, sems,
):
    core = this_core()
    gate_o, gate_s, up_o, up_s, over, over_s = stream(
        [(ref.at[n], inners.at[m, n]) for n in range(2) for m, ref in enumerate((inner, inner_s))]
        + [(over, overs.at[0]), (over_s, overs.at[1])],
        sems,
    )
    rows_keep, rows_got = keep[...], got[...]
    rows_in = in_order(core, rows_keep, rows_got)
    hidden = slope_up_own[...] * nn(rows_in, gate[...]) + active_own[...] * nn(rows_in, up[...])
    summed = nn(hidden.astype(BF), down[...])
    gate_tan = nn(rows_keep, gate_o()) + nn(rows_got, gate_s())
    up_tan = nn(rows_keep, up_o()) + nn(rows_got, up_s())
    hidden = slope_up[...] * gate_tan + active[...] * up_tan
    summed = summed + down_of_other(hidden.astype(BF), core, over(), over_s())
    out[...] = (rows_in.astype(F32) + summed.astype(BF).astype(F32) * picks[:, 2:3]).astype(BF)


class PairExperts:
    def __init__(self, index, own_rows, mask, upstream, route_ids, route_weights, w_gate, w_up, w_down):
        own = lax.axis_index("exp")
        self.upstream = upstream
        mine = (route_ids == own).astype(F32)
        self.picks = jnp.concatenate([mine, 1.0 - mine, route_weights], axis=1)
        rows, wide = upstream.shape[1:]
        units = w_gate.shape[1]
        pieces = 4
        inner = call(
            inner_kernel,
            like(2, wide // 2, units),
            hbm(w_gate, w_up),
            [pltpu.VMEM((2, pieces, wide // 2 // pieces, units), BF), pltpu.SemaphoreType.DMA((2, 2 * pieces))],
            limit=60,
            spaces=HBM,
        )
        down_half, self.mates = call(
            cut_kernel,
            (like(units // 2, wide), like(rows, 3 * wide // 2 + SIDE)),
            [(mask, SMEM)] + hbm(w_down, *own_rows) + anywhere(inner),
            [
                pltpu.VMEM((pieces, units // 2 // pieces, wide), BF),
                pltpu.VMEM((3, rows, wide // 2), BF),
                pltpu.VMEM((SIDE, rows), BF),
                pltpu.SemaphoreType.DMA((2, pieces + 3)),
                pltpu.SemaphoreType.DMA(()),
            ],
            limit=60,
            spaces=(HBM, HBM),
        )
        self.inner, self.over = crossed(inner), crossed(down_half)
        self.whole = (w_gate, w_up, w_down)
        self.rows, self.wide, self.units = rows, wide, units
        self.back_own = call(
            hidden_grad_kernel, like(rows, units, kind=F32), vmem(upstream, w_down), time=1.5
        )

    def before(self):
        return [self.back_own]

    def forward(self, size, keep, got, after):
        rows, wide, units = self.rows, self.wide, self.units
        w_gate, w_up, w_down = self.whole
        half, inner = like(rows, wide // PAIR + SIDE), like(rows, units, kind=F32)
        sums = like(rows, wide // PAIR, kind=F32)
        sum_keep, sum_got, hidden_own, *own_slopes = call(
            own_expert_kernel,
            (sums, sums, like(rows, units), inner, inner),
            vmem(keep, got, self.picks, self.back_own, w_gate, w_up),
            time=0.1,
        )
        inner_o, over = tied(self.inner, keep), tied(self.over, sum_keep)
        sum_got = tied(sum_got, *after, time=14)
        self.down = (w_down, over, swapped(over))
        self.inner = (inner_o, swapped(inner_o))
        cot_keep, cot_send, hidden, *slopes = call(
            functools.partial(other_expert_kernel, size),
            (half, half, like(rows, units), inner, inner),
            vmem(keep, got, self.upstream, self.picks, sum_keep, sum_got, *self.inner, *self.down[1:]),
            time=4.5,
        )
        self.slopes = own_slopes + slopes

        def layer(*after):
            return call(
                layer_kernel,
                (like(rows, wide), like(8, SIDE, kind=F32)),
                vmem(keep, got, hidden_own, hidden, self.picks, *self.down) + anywhere(*after),
                time=3,
            )

        return cot_keep, cot_send, layer

    def tangent(self, keep, got):
        return call(
            tangent_kernel,
            like(self.rows, self.wide),
            vmem(keep, got, *self.slopes, self.picks, *self.whole[:2])
            + anywhere(*self.inner)
            + vmem(self.down[0])
            + anywhere(*self.down[1:]),
            [
                pltpu.VMEM((2, 2, self.wide // 2, self.units), BF),
                pltpu.VMEM((2, self.units // 2, self.wide), BF),
                pltpu.SemaphoreType.DMA((6,)),
            ],
            time=4.5,
            limit=16,
        )


def routing_table(route_rows, experts, capacity):
    flat_ids = route_rows.reshape(-1)
    one_hot = (flat_ids[:, None] == jnp.arange(experts, dtype=jnp.int32)[None, :]).astype(jnp.int32)
    slot_rank = jnp.sum((jnp.cumsum(one_hot, axis=0) - one_hot) * one_hot, axis=1)
    target = flat_ids * capacity + slot_rank
    return (jnp.arange(experts * capacity, dtype=jnp.int32)[:, None] == target[None, :]).astype(
        jnp.bfloat16
    )


def dispatch(slot_table, row_block, routes, experts):
    pair_rows = jnp.repeat(row_block, routes, axis=0)
    sent = jnp.dot(slot_table, pair_rows, preferred_element_type=jnp.float32).astype(jnp.bfloat16)
    return sent.reshape(experts, -1, row_block.shape[1])


def combine(slot_table, returned, weights):
    rows_here, routes = weights.shape
    pair_vals = jnp.dot(
        slot_table.T, returned.reshape(-1, returned.shape[2]), preferred_element_type=jnp.float32
    )
    return jnp.sum(pair_vals.reshape(rows_here, routes, -1) * weights[:, :, None], axis=1)


def expert_forward(row_block, gate_matrix, up_matrix, down_matrix):
    gate_pre = jnp.dot(row_block, gate_matrix, preferred_element_type=jnp.float32)
    up_value = jnp.dot(row_block, up_matrix, preferred_element_type=jnp.float32)
    activated, slope_val = silu_parts(gate_pre)
    hidden = (activated * up_value).astype(jnp.bfloat16)
    return (
        jnp.dot(hidden, down_matrix, preferred_element_type=jnp.float32).astype(jnp.bfloat16),
        gate_pre,
        up_value,
    )


def expert_backward(cot_block, gate_pre, up_value, gate_matrix, up_matrix, down_matrix):
    hidden_grad = jnp.dot(cot_block, down_matrix.T, preferred_element_type=jnp.float32)
    activated, slope_val = silu_parts(gate_pre)
    gate_grad = (hidden_grad * up_value * slope_val).astype(jnp.bfloat16)
    up_grad = (hidden_grad * activated).astype(jnp.bfloat16)
    summed = jnp.dot(gate_grad, gate_matrix.T, preferred_element_type=jnp.float32) + jnp.dot(
        up_grad, up_matrix.T, preferred_element_type=jnp.float32
    )
    return summed.astype(jnp.bfloat16)


def expert_tangent(tan_block, gate_pre, up_value, gate_matrix, up_matrix, down_matrix):
    gate_tan = jnp.dot(tan_block, gate_matrix, preferred_element_type=jnp.float32)
    up_tan = jnp.dot(tan_block, up_matrix, preferred_element_type=jnp.float32)
    activated, slope_val = silu_parts(gate_pre)
    hidden_tan = (slope_val * gate_tan * up_value + activated * up_tan).astype(jnp.bfloat16)
    return jnp.dot(hidden_tan, down_matrix, preferred_element_type=jnp.float32).astype(jnp.bfloat16)


class RoutedExperts:
    def __init__(self, index, own_rows, mask, upstream, route_ids, route_weights, w_gate, w_up, w_down):
        rows, routes = route_ids.shape
        self.experts = lax.axis_size("exp")
        self.routes = routes
        capacity = min(rows, 2 * rows * routes // self.experts)
        self.core, self.upstream, self.weights = index % 2, upstream[0], route_weights
        self.matrices = (w_gate, w_up, w_down)
        self.table = routing_table(route_ids, self.experts, capacity)
        self.got_cots = self.sent(self.upstream)
        wide = self.upstream.shape[1]
        self.mates = call(
            split_kernel,
            like(rows, 3 * wide // 2 + SIDE),
            [(mask, SMEM)] + hbm(*own_rows),
            [
                pltpu.VMEM((3, rows, wide // 2), BF),
                pltpu.VMEM((SIDE, rows), BF),
                pltpu.SemaphoreType.DMA((2, 3)),
                pltpu.SemaphoreType.DMA(()),
            ],
            limit=20,
            spaces=HBM,
        )

    def before(self):
        return [self.got_cots]

    def across(self, x):
        return lax.all_to_all(x, "exp", split_axis=0, concat_axis=0, tiled=True)

    def sent(self, x):
        return self.across(dispatch(self.table, x, self.routes, self.experts))

    def returned(self, x):
        back = self.across(x.reshape(self.got_cots.shape))
        return combine(self.table, back, self.weights)

    def forward(self, size, keep, got, after):
        attended = in_order(self.core, keep, got)
        rows, wide = attended.shape
        got_rows = self.sent(attended).reshape(-1, wide)
        expert_out, self.gate_pre, self.up_value = expert_forward(got_rows, *self.matrices)
        route_grad = expert_backward(
            self.got_cots.reshape(-1, wide), self.gate_pre, self.up_value, *self.matrices
        )
        attn_cot = (self.upstream.astype(F32) + self.returned(route_grad)).astype(BF)
        layer_out = (attended.astype(F32) + self.returned(expert_out)).astype(BF)

        def kernel(cot, kept, got, cot_keep, cot_send):
            width = kept.shape[1]
            for part, attended, out in ((this_core(), kept, cot_keep), (1 - this_core(), got, cot_send)):
                here = pl.ds(pl.multiple_of(part * width, width), width)
                out[...] = cot_payload(size, cot[:, here], attended[...])

        half = like(rows, wide // PAIR + SIDE)
        cot_keep, cot_send = call(
            kernel, (half, half), vmem(attn_cot, keep, got)
        )
        return cot_keep, cot_send, lambda *after: (layer_out, layer_out)

    def tangent(self, keep, got):
        rows = in_order(self.core, keep, got)
        got_rows = self.sent(rows).reshape(-1, rows.shape[1])
        out = expert_tangent(got_rows, self.gate_pre, self.up_value, *self.matrices)
        return (rows.astype(F32) + self.returned(out)).astype(BF)


def neighbours(whole, even, odd):
    return (
        moved(odd, 2 * PAIR),
        moved(whole, PAIR),
        moved(whole, -PAIR),
        moved(even, -2 * PAIR),
    )


def local(query, key, value, cotangent, route_ids, route_weights, block_mask, w_gate, w_up, w_down):
    rows, wide = query.shape[1:]
    width = wide // PAIR
    size = wide // HEADS
    heads = width // size
    index = lax.axis_index("ctx")
    core = index % PAIR

    pair = lax.axis_size("exp") == 2 and route_ids.shape[2] == 1
    experts = (PairExperts if pair else RoutedExperts)(
        index, (query, key, value), block_mask, cotangent, route_ids[0], route_weights[0], w_gate[0], w_up[0], w_down[0]
    )
    half, pairs = like(rows, width), like(2 * rows, width)
    q2, own, odd, side = call(
        join_kernel,
        (pairs, like(2 * rows, wide), like(rows, wide), like(2 * rows, SIDE)),
        vmem(query, key, value) + [(block_mask, SMEM)] + vmem(swapped(experts.mates)),
    )
    near, far = moved(own, PAIR), moved(odd, 2 * PAIR)
    three = like(3 * rows, width)
    q_other = swapped(q2, 2)
    q_up, q_down = call(shift_kernel, (three, three), vmem(q2, q_other))
    side, keep, send = call(
        functools.partial(attend_kernel, size),
        (
            like(2 * rows, SIDE),
            half,
            half,
        ),
        vmem(far, near, own, q2, side) + anywhere(q_up, *experts.before()),
        [pltpu.VMEM((PAIR, heads, rows), F32)],
        time=0.1,
    )
    got = swapped(send)
    q_below, q_above = moved(q_up, 2 * PAIR), moved(q_down, -2 * PAIR)
    q_before, q_after = call(around_kernel, (three, three), vmem(q_other, q_below, q_above))

    cot_keep, cot_send, layer = experts.forward(size, keep, got, (q_below, q_above))
    payload = wide // PAIR + SIDE
    co, co_even, co_odd = call(
        cots_kernel,
        (like(2 * rows, payload), like(rows, payload), like(rows, payload)),
        vmem(cot_keep, swapped(cot_send), side),
    )
    cfb, cnb, cna, cfa = neighbours(co, co_even, co_odd)

    layer_out, layer_done = layer(co, q_before)
    sums = like((WIN + 1) * rows, width, kind=F32)
    probs, probs_low, grads_q, q_keep, q_send, key_sums, value_sums = call(
        functools.partial(own_grads_kernel, size),
        (
            like(heads, PAIR, WIN * rows, rows),
            like(heads, PAIR, rows, WIN * rows),
            pairs, half, half, sums, sums,
        ),
        vmem(far, near, own, q2, co),
        [pltpu.VMEM((2, heads, rows), F32)] * 2,
        time=7,
    )
    q_got = swapped(q_send)
    kv_half = like(rows, 2 * width)
    kv_keep, kv_send, tan_keep, tan_send = call(
        functools.partial(grads_kernel, size),
        (kv_half, kv_half, half, half),
        vmem(far, near, own, q2, q_before, q_after, cfb, cnb, cna, cfa)
        + vmem(probs, probs_low, grads_q, key_sums, value_sums)
        + anywhere(layer_done),
        [pltpu.VMEM((6, heads, rows), F32)] * 2,
        time=16,
    )
    tan_got = swapped(tan_send)
    kv_got = swapped(kv_send)
    tangent_out = experts.tangent(tan_keep, tan_got)
    out = like(rows, wide)
    outs = call(gather_kernel, (out, out, out), vmem(q_keep, q_got, kv_keep, kv_got))
    return (layer_out[None], *(x[None] for x in outs), tangent_out[None])


def solution(mesh):
    return jax.shard_map(
        local,
        mesh=mesh,
        in_specs=(
            P("exp", "ctx", None),
            P("exp", "ctx", None),
            P("exp", "ctx", None),
            P("exp", "ctx", None),
            P("exp", "ctx", None),
            P("exp", "ctx", None),
            P("exp", "ctx", None),
            P("exp", None, None),
            P("exp", None, None),
            P("exp", None, None),
        ),
        out_specs=(
            P("exp", "ctx", None),
            P("exp", "ctx", None),
            P("exp", "ctx", None),
            P("exp", "ctx", None),
            P("exp", "ctx", None),
        ),
        check_vma=False,
    )
```

```python
import functools

import jax
import jax.numpy as jnp
from jax import lax
from jax.experimental import pallas as pl
from jax.experimental.pallas import tpu as pltpu
from jax.sharding import PartitionSpec as P

HEADS = 16
WIN = 4
PAIR = 2
SIDE = 128
FAR = 1e30
BF = jnp.bfloat16
F32 = jnp.float32
VMEM = pl.BlockSpec(memory_space=pltpu.VMEM)
SMEM = pl.BlockSpec(memory_space=pltpu.SMEM)
ANY = pl.BlockSpec(memory_space=pl.ANY)
HBM = pl.BlockSpec(memory_space=pltpu.HBM)


def moved(x, by):
    devices = lax.axis_size("ctx")
    pairs = [(i, i + by) for i in range(devices) if 0 <= i + by < devices]
    return lax.ppermute(x, "ctx", pairs)


def swapped(x, bit=1):
    return lax.ppermute(x, "ctx", [(i, i ^ bit) for i in range(lax.axis_size("ctx"))])


def this_core():
    return lax.axis_index("ctx") % PAIR


def this_lane():
    return lax.axis_index("ctx") // PAIR % 2


def crossed(x):
    return lax.ppermute(x, "exp", [(0, 1), (1, 0)])


def nn(a, b):
    return lax.dot_general(a, b, (((1,), (0,)), ((), ())), preferred_element_type=F32)


def nt(a, b):
    return lax.dot_general(a, b, (((1,), (1,)), ((), ())), preferred_element_type=F32)


def tn(a, b):
    return lax.dot_general(a, b, (((0,), (0,)), ((), ())), preferred_element_type=F32)


def silu_parts(gate_pre):
    sigmoid_val = jax.nn.sigmoid(gate_pre)
    return (gate_pre * sigmoid_val, sigmoid_val * (1.0 + gate_pre * (1.0 - sigmoid_val)))


LEVEL, DELTA = 8, 32


def terms_of(x):
    first = x.astype(BF).astype(F32)
    second = (x - first).astype(BF).astype(F32)
    return jnp.concatenate([first, second, x - first - second], axis=0)


def rows_of(side, at, heads):
    return sum(side[at + n * heads : at + (n + 1) * heads].astype(F32) for n in range(3))


def hidden_by(flag):
    return (1.0 - flag) * FAR


def causal_of(rows):
    return lax.broadcasted_iota(jnp.int32, (rows, rows), 1) >= lax.broadcasted_iota(
        jnp.int32, (rows, rows), 0
    )


def like(*shape, kind=BF):
    return jax.ShapeDtypeStruct(shape, kind)


def call(kernel, outs, args, scratch=(), time=1, limit=8, alias=None, spaces=None):
    return pl.pallas_call(
        kernel,
        out_shape=outs,
        in_specs=[space for _, space in args],
        out_specs=jax.tree.map(lambda _: VMEM, outs) if spaces is None else spaces,
        input_output_aliases=alias or {},
        scratch_shapes=list(scratch),
        compiler_params=pltpu.CompilerParams(vmem_limit_bytes=limit * 1024 * 1024),
        cost_estimate=pl.CostEstimate(flops=int(time * 1.1e9), bytes_accessed=0, transcendentals=0),
    )(*(array for array, _ in args))


def vmem(*arrays):
    return [(array, VMEM) for array in arrays]


def hbm(*arrays):
    return [(array, HBM) for array in arrays]


def anywhere(*arrays):
    return [(array, ANY) for array in arrays]


def tied(x, *after, time=0.01):
    out = like(*x.shape, kind=x.dtype)
    return call(lambda *refs: None, out, anywhere(x, *after), alias={0: 0}, spaces=ANY, limit=1, time=time)


def fetch(copies):
    for copy in copies:
        copy.start()
    return copies


def ready(copies):
    for copy in copies:
        copy.wait()


def through(moves, sems):
    ins = [pltpu.make_async_copy(source, buffer, sems.at[0, n]) for n, (source, buffer, _) in enumerate(moves)]
    outs = [pltpu.make_async_copy(buffer, target, sems.at[1, n]) for n, (_, buffer, target) in enumerate(moves)]
    fetch(ins)
    for first, second in zip(ins, outs):
        first.wait()
        second.start()
    ready(outs)


def columns_of(core, width):
    return [pl.ds(pl.multiple_of(n * width, width), width) for n in (core, 1 - core)]


def join_kernel(query, key, value, mask, got, q2, kv2, odd, side):
    core = this_core()
    rows, width = got.shape[0], q2.shape[1]
    mine, _ = columns_of(core, width)
    here, there = (pl.ds(pl.multiple_of(n * rows, rows), rows) for n in (core, 1 - core))
    q2[here, :] = query[0, :, mine]
    q2[there, :] = got[:, 0:width]
    kept = jnp.concatenate([key[0, :, mine], value[0, :, mine]], axis=1)
    sent = got[:, width : 3 * width]
    kv2[here, :] = kept
    kv2[there, :] = sent
    odd[...] = jnp.where(core == 1, kept, sent)
    side[here, :] = seen_by(mask, rows)
    side[there, :] = got[:, 3 * width :]


def seen_by(mask, rows):
    at = lax.broadcasted_iota(jnp.int32, (SIDE, rows), 0)
    sees = jnp.zeros((SIDE, rows), F32)
    for w in range(1, WIN):
        flag = jnp.where((mask[0, 0, w - 1] == 1) & (lax.axis_index("ctx") >= w), 1.0, 0.0)
        sees = jnp.where(at == w - 1, flag, sees)
    return sees.astype(BF)


def shift_kernel(own, other, up, down):
    lane = this_lane()
    rows = own.shape[0] // 2

    def put(first, last):
        up[0:rows] = first[rows : 2 * rows]
        up[rows : 3 * rows] = last[...]
        down[0 : 2 * rows] = first[...]
        down[2 * rows : 3 * rows] = last[0:rows]

    pl.when(lane == 0)(lambda: put(own, other))
    pl.when(lane != 0)(lambda: put(other, own))


def around_kernel(other, below, above, before, after):
    lane = this_lane()
    rows = other.shape[0] // 2

    @pl.when(lane == 0)
    def _():
        before[...] = below[...]
        after[0 : 2 * rows] = other[...]
        after[2 * rows :] = above[0:rows]

    @pl.when(lane != 0)
    def _():
        before[0:rows] = below[2 * rows :]
        before[rows:] = other[...]
        after[...] = above[...]


def split_moves(query, key, value, blocks, sent):
    width = query.shape[2] // 2
    _, others = columns_of(this_core(), width)
    return [
        (ref.at[0, :, others], blocks.at[n], sent.at[:, pl.ds(n * width, width)])
        for n, ref in enumerate((query, key, value))
    ]


def split_kernel(mask, query, key, value, sent, blocks, seen, sems, seen_sem):
    through(split_moves(query, key, value, blocks, sent), sems)
    send_seen(mask, seen, sent, seen_sem)


def send_seen(mask, seen, sent, sem):
    rows = seen.shape[1]
    seen[...] = seen_by(mask, rows)
    copy = pltpu.make_async_copy(seen, sent.at[:, pl.ds(sent.shape[1] - rows, rows)], sem)
    copy.start()
    copy.wait()


def half_moves(matrix, buffers, out):
    pieces, size = buffers.shape[:2]
    start = this_core() * pieces * size
    return [
        (matrix.at[pl.ds(start + n * size, size)], buffers.at[n], out.at[pl.ds(n * size, size)]) for n in range(pieces)
    ]


def inner_kernel(gate, up, inner, parts, sems):
    through([move for n, x in enumerate((gate, up)) for move in half_moves(x, parts.at[n], inner.at[n])], sems)


def cut_kernel(mask, down, query, key, value, after, down_half, sent, down_parts, blocks, seen, sems, seen_sem):
    moves = split_moves(query, key, value, blocks, sent) + half_moves(down, down_parts, down_half)
    through(moves, sems)
    send_seen(mask, seen, sent, seen_sem)


def cots_kernel(keep, got, side, whole, even, odd):
    core = this_core()
    rows, width = keep.shape[0], keep.shape[1] - SIDE
    for ref, block in ((keep, core), (got, 1 - core)):
        here = pl.ds(pl.multiple_of(block * rows, rows), rows)
        filled = (ref[:, width:].astype(F32) + side[here, :].astype(F32)).astype(BF)
        whole[here, 0:width] = ref[:, 0:width]
        whole[here, width:] = filled

        @pl.when(block == 0)
        def _():
            even[:, 0:width] = ref[:, 0:width]
            even[:, width:] = filled

        @pl.when(block == 1)
        def _():
            odd[:, 0:width] = ref[:, 0:width]
            odd[:, width:] = filled


def window_refs(far, near, own, rows):
    return {-3: (far, 0), -2: (near, 0), -1: (near, rows), 0: (own, 0), 1: (own, rows)}


def stacked(window, js, rows, here):
    return jnp.concatenate([window[j][0][pl.ds(window[j][1], rows), here] for j in js], axis=0)


def each_head(heads, one, step=2):
    def some(n, carry):
        for at in range(step):
            one(step * n + at)
        return carry

    lax.fori_loop(0, heads // step, some, 0)


def attend_kernel(size, far, near, own, q2, flags, *rest):
    side, keep, send, levels = rest[-4:]
    rows, width = far.shape[0], far.shape[1] // 2
    heads = width // size
    scale = size ** (-0.5)
    core = this_core()
    window = window_refs(far, near, own, rows)
    causal = causal_of(rows)
    seen = [flags[block * rows : block * rows + LEVEL, :].astype(F32) for block in range(PAIR)]

    def one(head):
        here = pl.ds(pl.multiple_of(head * size, size), size)
        there = pl.ds(pl.multiple_of(width + head * size, size), size)
        outs = []
        for block in range(PAIR):
            js = list(range(block - WIN + 1, block + 1))
            q = q2[pl.ds(block * rows, rows), here]
            scores = nt(stacked(window, js, rows, here), q) * scale
            parts = [
                scores[n * rows : (n + 1) * rows] - hidden_by(seen[block][block - j - 1 : block - j])
                if j < block
                else jnp.where(causal, scores[n * rows : (n + 1) * rows], -FAR)
                for n, j in enumerate(js)
            ]
            scores = jnp.concatenate(parts, axis=0)
            top = jnp.max(scores, axis=0, keepdims=True)
            weights = jnp.exp(scores - top)
            total = jnp.sum(weights, axis=0, keepdims=True)
            probs = weights * (1.0 / total)
            levels[block, pl.ds(head, 1), :] = top + jnp.log(total)
            outs.append(tn(probs.astype(BF), stacked(window, js, rows, there)).astype(BF))
        keep[:, here] = jnp.where(core == 0, outs[0], outs[1])
        send[:, here] = jnp.where(core == 0, outs[1], outs[0])

    each_head(heads, one)
    for block in range(PAIR):
        filled = jnp.concatenate(
            [seen[block], terms_of(levels[block]), jnp.zeros((SIDE - LEVEL - 3 * heads, rows), F32)], axis=0
        )
        side[block * rows : (block + 1) * rows, :] = filled.astype(BF)


def scores_back(q, cot, level, delta, seen, keys, values, js, t, causal, scale):
    rows = q.shape[0]
    scores = nt(keys, q) * scale
    parts = []
    for n, j in enumerate(js):
        part = scores[n * rows : (n + 1) * rows]
        if j < t:
            part = part - (level + hidden_by(seen[t - j - 1 : t - j]))
        else:
            part = jnp.where(causal, part - level, -FAR)
        parts.append(part)
    probs = jnp.exp(jnp.concatenate(parts, axis=0))
    return probs, (probs * (nt(values, cot) - delta)).astype(BF)


def add_blocks(sums, js, terms, rows):
    for n, j in enumerate(js):
        term = terms[n * rows : (n + 1) * rows]
        sums[j] = sums[j] + term if j in sums else term


def own_grads_kernel(
    size, far, near, own, q2, co, probs_out, probs_low_out, grads_q, q_keep, q_send, key_sums, value_sums, levels, deltas,
):
    rows, width = far.shape[0], far.shape[1] // 2
    heads = width // size
    scale = size ** (-0.5)
    core = this_core()
    window = window_refs(far, near, own, rows)
    causal = causal_of(rows)
    sides = [co[t * rows : (t + 1) * rows, width:].astype(F32) for t in range(PAIR)]
    for t in range(PAIR):
        levels[t] = rows_of(sides[t], LEVEL, heads)
        deltas[t] = rows_of(sides[t], DELTA, heads)

    def one(head):
        here = pl.ds(pl.multiple_of(head * size, size), size)
        there = pl.ds(pl.multiple_of(width + head * size, size), size)
        keys_at, values_at, grads = {}, {}, []
        for t in range(PAIR):
            place = pl.ds(t * rows, rows)
            js = list(range(t - WIN + 1, t + 1))
            q, cot = q2[place, here], co[place, here]
            keys = stacked(window, js, rows, here)
            probs, score_grad = scores_back(
                q, cot, levels[t, pl.ds(head, 1), :], deltas[t, pl.ds(head, 1), :], sides[t][0:LEVEL],
                keys, stacked(window, js, rows, there), js, t, causal, scale,
            )
            probs_low = probs.astype(BF)
            probs_out[head, t] = probs_low
            probs_low_out[head, t] = probs_low.T
            add_blocks(keys_at, js, nn(score_grad, q), rows)
            add_blocks(values_at, js, nn(probs_low, cot), rows)
            grads.append((tn(score_grad, keys) * scale).astype(BF))
            grads_q[place, here] = grads[t]
        q_keep[:, here] = jnp.where(core == 0, grads[0], grads[1])
        q_send[:, here] = jnp.where(core == 0, grads[1], grads[0])
        for j in keys_at:
            place = pl.ds((j + WIN - 1) * rows, rows)
            key_sums[place, here] = keys_at[j]
            value_sums[place, here] = values_at[j]

    each_head(heads, one)


def grads_kernel(
    size, far, near, own, q2, q_before, q_after, cfb, cnb, cna, cfa, probs_in, probs_low_in, grads_q,
    key_sums, value_sums, after, keep, send, tans_keep, tans_send, levels, deltas,
):
    rows, width = far.shape[0], far.shape[1] // 2
    heads = width // size
    scale = size ** (-0.5)
    core = this_core()
    window = window_refs(far, near, own, rows)
    causal = causal_of(rows)
    others = (
        (-3, q_before, 0, cfb, 0), (-2, q_before, 1, cnb, 0), (-1, q_before, 2, cnb, 1),
        (2, q_after, 0, cna, 0), (3, q_after, 1, cna, 1), (4, q_after, 2, cfa, 0),
    )
    sides = [c_ref[half * rows : (half + 1) * rows, width:].astype(F32) for _, _, _, c_ref, half in others]
    for n, side in enumerate(sides):
        levels[n] = rows_of(side, LEVEL, heads)
        deltas[n] = rows_of(side, DELTA, heads)

    def one(head):
        at = pl.multiple_of(head * size, size)
        here = pl.ds(at, size)
        there = pl.ds(pl.multiple_of(width + at, size), size)
        blocks = range(1 - WIN, PAIR)
        keys_at = {j: key_sums[pl.ds((j + WIN - 1) * rows, rows), here] for j in blocks}
        values_at = {j: value_sums[pl.ds((j + WIN - 1) * rows, rows), here] for j in blocks}
        score_grads, probs_at, qs, cots = {}, {}, {}, {}
        for n, (t, q_ref, q_half, c_ref, half) in enumerate(others):
            js = list(range(max(1 - WIN, t - WIN + 1), min(1, t) + 1))
            q, cot = q_ref[pl.ds(q_half * rows, rows), here], c_ref[pl.ds(half * rows, rows), here]
            keys = stacked(window, js, rows, here)
            values = stacked(window, js, rows, there)
            probs, score_grad = scores_back(
                q, cot, levels[n, pl.ds(head, 1), :], deltas[n, pl.ds(head, 1), :], sides[n][0:8],
                keys, values, js, t, causal, scale,
            )
            probs = probs.astype(BF)
            qs[t], cots[t] = q, cot
            for m, j in enumerate(js):
                score_grads[j, t] = score_grad[m * rows : (m + 1) * rows]
                probs_at[j, t] = probs[m * rows : (m + 1) * rows]
        for j in blocks:
            ts = [t for t in qs if (j, t) in probs_at]
            keys_at[j] = keys_at[j] + nn(
                jnp.concatenate([score_grads[j, t] for t in ts], axis=1), jnp.concatenate([qs[t] for t in ts], axis=0)
            )
            values_at[j] = values_at[j] + nn(
                jnp.concatenate([probs_at[j, t] for t in ts], axis=1), jnp.concatenate([cots[t] for t in ts], axis=0)
            )
        key_grads = {j: (keys_at[j] * scale).astype(BF) for j in blocks}
        value_grads = {j: values_at[j].astype(BF) for j in blocks}
        tans = []
        for t in range(PAIR):
            place = pl.ds(t * rows, rows)
            js = list(range(t - WIN + 1, t + 1))
            keys = stacked(window, js, rows, here)
            probs = probs_in[head, t].astype(F32)
            both_keys = jnp.concatenate([keys, jnp.concatenate([key_grads[j] for j in js], axis=0)], axis=1)
            both_rows = jnp.concatenate([grads_q[place, here], q2[place, here]], axis=1)
            tan_values = jnp.concatenate([value_grads[j] for j in js], axis=0)
            score_tan = nt(both_keys, both_rows) * scale
            mean = jnp.sum(probs * score_tan, axis=0, keepdims=True)
            prob_tan = (probs * (score_tan - mean)).astype(BF)
            tan = tn(prob_tan, stacked(window, js, rows, there)) + nn(probs_low_in[head, t], tan_values)
            tans.append(tan.astype(BF))
        for grads, tans_out, mine, other in ((keep, tans_keep, 0, 1), (send, tans_send, 1, 0)):
            grads[:, here] = jnp.where(core == 0, key_grads[mine], key_grads[other])
            grads[:, there] = jnp.where(core == 0, value_grads[mine], value_grads[other])
            tans_out[:, here] = jnp.where(core == 0, tans[mine], tans[other])

    each_head(heads, one, 4)


def gather_kernel(q_keep, q_got, keep, got, out_q, out_k, out_v):
    core = this_core()
    width = q_keep.shape[1]
    for owner, q, kv in ((core, q_keep, keep), (1 - core, q_got, got)):
        columns = pl.ds(pl.multiple_of(owner * width, width), width)
        out_q[:, columns] = q[...]
        out_k[:, columns] = kv[:, 0:width]
        out_v[:, columns] = kv[:, width:]


def cot_payload(size, cot, attended):
    rows, width = cot.shape
    heads = width // size
    lanes = lax.broadcasted_iota(jnp.int32, (rows, SIDE), 1)
    sums = jnp.zeros((rows, SIDE), F32)
    for head in range(heads):
        here = slice(head * size, (head + 1) * size)
        delta = jnp.sum(cot[:, here].astype(F32) * attended[:, here].astype(F32), axis=1, keepdims=True)
        sums = jnp.where(lanes == head, delta, sums)
    blank = jnp.zeros((DELTA, rows), F32)
    rest = jnp.zeros((SIDE - DELTA - 3 * heads, rows), F32)
    side = jnp.concatenate([blank, terms_of(sums.T[0:heads]), rest], axis=0)
    return jnp.concatenate([cot, side.astype(BF)], axis=1)


def in_order(core, kept, got):
    return jnp.where(
        core == 0, jnp.concatenate([kept, got], axis=1), jnp.concatenate([got, kept], axis=1)
    )


def pair_of(a, b, bit):
    return jnp.where(bit == 0, a, b), jnp.where(bit == 0, b, a)


def down_of_other(hidden, core, over, over_s):
    half = hidden.shape[1] // 2
    mine, others = pair_of(hidden[:, :half], hidden[:, half:], core)
    return nn(mine, over[...]) + nn(others, over_s[...])


def hidden_grad_kernel(cot, down, out):
    out[...] = nt(cot[0], down[...])


def middle_of(chosen, gate_pre, up_value, back, hidden, slope_up, active):
    activated, slope = silu_parts(gate_pre)
    activated = activated * chosen
    slope = slope * up_value * chosen
    hidden[...] = (activated * up_value).astype(BF)
    slope_up[...] = slope
    active[...] = activated
    return (back * slope).astype(BF), (back * activated).astype(BF)


def own_expert_kernel(keep, got, picks, back, gate, up, sum_keep, sum_got, hidden, slope_up, active):
    mine, others = columns_of(this_core(), keep.shape[1])
    rows_keep, rows_got = keep[...], got[...]

    def inner(ref):
        return nn(rows_keep, ref[mine, :]) + nn(rows_got, ref[others, :])

    gate_grad, up_grad = middle_of(picks[:, 0:1], inner(gate), inner(up), back[...], hidden, slope_up, active)
    for here, out in ((mine, sum_keep), (others, sum_got)):
        out[...] = nt(gate_grad, gate[here, :]) + nt(up_grad, up[here, :])


def stream(pairs, sems):
    copies = fetch([pltpu.make_async_copy(source, buffer, sems.at[n]) for n, (source, buffer) in enumerate(pairs)])

    def waiting(n):
        def get():
            copies[n].wait()
            return pairs[n][1][...]

        return get

    return [waiting(n) for n in range(len(pairs))]


def other_expert_kernel(
    size, keep, got, cot, picks, sum_keep, sum_got, inner, inner_s, over, over_s,
    cot_keep, cot_send, hidden, slope_up, active,
):
    core = this_core()
    mine, others = columns_of(core, keep.shape[1])
    rows_keep, rows_got = keep[...], got[...]
    cots = cot[0]
    back = jnp.concatenate(pair_of(nt(cots, over[...]), nt(cots, over_s[...]), core), axis=1)
    gate_pre, up_value = (nn(rows_keep, inner[n]) + nn(rows_got, inner_s[n]) for n in range(2))
    gate_grad, up_grad = middle_of(picks[:, 1:2], gate_pre, up_value, back, hidden, slope_up, active)
    weight = picks[:, 2:3]
    for here, attended, so_far, ref, out in (
        (others, rows_got, sum_got, inner_s, cot_send),
        (mine, rows_keep, sum_keep, inner, cot_keep),
    ):
        summed = so_far[...] + nt(gate_grad, ref[0]) + nt(up_grad, ref[1])
        attn_cot = (cot[0, :, here].astype(F32) + summed.astype(BF).astype(F32) * weight).astype(BF)
        out[...] = cot_payload(size, attn_cot, attended)


def layer_kernel(keep, got, hidden_own, hidden, picks, down, over, over_s, *rest):
    out, done = rest[-2:]
    done[...] = jnp.zeros_like(done)
    core = this_core()
    rows_in = in_order(core, keep[...], got[...]).astype(F32)
    summed = nn(hidden_own[...], down[...]) + down_of_other(hidden[...], core, over, over_s)
    out[...] = (rows_in + summed.astype(BF).astype(F32) * picks[:, 2:3]).astype(BF)


def load_kernel(*refs):
    count = (len(refs) - 3) // 2
    sources, outs, done, sems = refs[:count], refs[count + 1 : 2 * count + 1], refs[-2], refs[-1]
    copies = fetch([pltpu.make_async_copy(a, b, sems.at[n]) for n, (a, b) in enumerate(zip(sources, outs))])
    done[...] = jnp.zeros_like(done)
    ready(copies)


def tangent_kernel(
    keep, got, slope_up_own, active_own, slope_up, active, picks, gate, up, inner, inner_s, down, over, over_s, out,
):
    core = this_core()
    rows_keep, rows_got = keep[...], got[...]
    rows_in = in_order(core, rows_keep, rows_got)
    hidden = slope_up_own[...] * nn(rows_in, gate[...]) + active_own[...] * nn(rows_in, up[...])
    summed = nn(hidden.astype(BF), down[...])
    gate_tan, up_tan = (nn(rows_keep, inner[n]) + nn(rows_got, inner_s[n]) for n in range(2))
    hidden = slope_up[...] * gate_tan + active[...] * up_tan
    summed = summed + down_of_other(hidden.astype(BF), core, over, over_s)
    out[...] = (rows_in.astype(F32) + summed.astype(BF).astype(F32) * picks[:, 2:3]).astype(BF)


class PairExperts:
    def __init__(self, index, own_rows, mask, upstream, route_ids, route_weights, w_gate, w_up, w_down):
        own = lax.axis_index("exp")
        self.upstream = upstream
        mine = (route_ids == own).astype(F32)
        self.picks = jnp.concatenate([mine, 1.0 - mine, route_weights], axis=1)
        rows, wide = upstream.shape[1:]
        units = w_gate.shape[1]
        pieces = 4
        inner = call(
            inner_kernel,
            like(2, wide // 2, units),
            hbm(w_gate, w_up),
            [pltpu.VMEM((2, pieces, wide // 2 // pieces, units), BF), pltpu.SemaphoreType.DMA((2, 2 * pieces))],
            limit=60,
            spaces=HBM,
        )
        down_half, self.mates = call(
            cut_kernel,
            (like(units // 2, wide), like(rows, 3 * wide // 2 + SIDE)),
            [(mask, SMEM)] + hbm(w_down, *own_rows) + anywhere(inner),
            [
                pltpu.VMEM((pieces, units // 2 // pieces, wide), BF),
                pltpu.VMEM((3, rows, wide // 2), BF),
                pltpu.VMEM((SIDE, rows), BF),
                pltpu.SemaphoreType.DMA((2, pieces + 3)),
                pltpu.SemaphoreType.DMA(()),
            ],
            limit=60,
            spaces=(HBM, HBM),
        )
        self.inner, self.over = crossed(inner), crossed(down_half)
        self.whole = (w_gate, w_up, w_down)
        self.rows, self.wide, self.units = rows, wide, units
        self.back_own = call(
            hidden_grad_kernel, like(rows, units, kind=F32), vmem(upstream, w_down), time=1.5
        )

    def before(self):
        return [self.back_own]

    def forward(self, size, keep, got, after):
        rows, wide, units = self.rows, self.wide, self.units
        w_gate, w_up, w_down = self.whole
        half, inner = like(rows, wide // PAIR + SIDE), like(rows, units, kind=F32)
        sums = like(rows, wide // PAIR, kind=F32)
        sum_keep, sum_got, hidden_own, *own_slopes = call(
            own_expert_kernel,
            (sums, sums, like(rows, units), inner, inner),
            vmem(keep, got, self.picks, self.back_own, w_gate, w_up),
            time=0.1,
        )
        inner_o, over = tied(self.inner, keep), tied(self.over, sum_keep)
        sum_got = tied(sum_got, *after, time=14)
        self.down = (w_down, over, swapped(over))
        self.inner = (inner_o, swapped(inner_o))
        cot_keep, cot_send, hidden, *slopes = call(
            functools.partial(other_expert_kernel, size),
            (half, half, like(rows, units), inner, inner),
            vmem(keep, got, self.upstream, self.picks, sum_keep, sum_got, *self.inner, *self.down[1:]),
            time=4.5,
        )
        self.slopes = own_slopes + slopes

        def layer(*after):
            return call(
                layer_kernel,
                (like(rows, wide), like(8, SIDE, kind=F32)),
                vmem(keep, got, hidden_own, hidden, self.picks, *self.down) + anywhere(*after),
                time=3,
            )

        return cot_keep, cot_send, layer

    def prefetch(self, after):
        arrays = (*self.inner, *self.down[1:])
        *loaded, done = call(
            load_kernel,
            (*(like(*x.shape) for x in arrays), like(8, SIDE, kind=F32)),
            hbm(*arrays) + anywhere(after),
            [pltpu.SemaphoreType.DMA((len(arrays),))],
            time=2,
        )
        self.inner, self.down = tuple(loaded[:2]), (self.down[0], *loaded[2:])
        return done

    def tangent(self, keep, got):
        return call(
            tangent_kernel,
            like(self.rows, self.wide),
            vmem(keep, got, *self.slopes, self.picks, *self.whole[:2], *self.inner, *self.down),
            time=4.5,
        )


def routing_table(route_rows, experts, capacity):
    flat_ids = route_rows.reshape(-1)
    one_hot = (flat_ids[:, None] == jnp.arange(experts, dtype=jnp.int32)[None, :]).astype(jnp.int32)
    slot_rank = jnp.sum((jnp.cumsum(one_hot, axis=0) - one_hot) * one_hot, axis=1)
    target = flat_ids * capacity + slot_rank
    return (jnp.arange(experts * capacity, dtype=jnp.int32)[:, None] == target[None, :]).astype(
        jnp.bfloat16
    )


def dispatch(slot_table, row_block, routes, experts):
    pair_rows = jnp.repeat(row_block, routes, axis=0)
    sent = jnp.dot(slot_table, pair_rows, preferred_element_type=jnp.float32).astype(jnp.bfloat16)
    return sent.reshape(experts, -1, row_block.shape[1])


def combine(slot_table, returned, weights):
    rows_here, routes = weights.shape
    pair_vals = jnp.dot(
        slot_table.T, returned.reshape(-1, returned.shape[2]), preferred_element_type=jnp.float32
    )
    return jnp.sum(pair_vals.reshape(rows_here, routes, -1) * weights[:, :, None], axis=1)


def expert_forward(row_block, gate_matrix, up_matrix, down_matrix):
    gate_pre = jnp.dot(row_block, gate_matrix, preferred_element_type=jnp.float32)
    up_value = jnp.dot(row_block, up_matrix, preferred_element_type=jnp.float32)
    activated, slope_val = silu_parts(gate_pre)
    hidden = (activated * up_value).astype(jnp.bfloat16)
    return (
        jnp.dot(hidden, down_matrix, preferred_element_type=jnp.float32).astype(jnp.bfloat16),
        gate_pre,
        up_value,
    )


def expert_backward(cot_block, gate_pre, up_value, gate_matrix, up_matrix, down_matrix):
    hidden_grad = jnp.dot(cot_block, down_matrix.T, preferred_element_type=jnp.float32)
    activated, slope_val = silu_parts(gate_pre)
    gate_grad = (hidden_grad * up_value * slope_val).astype(jnp.bfloat16)
    up_grad = (hidden_grad * activated).astype(jnp.bfloat16)
    summed = jnp.dot(gate_grad, gate_matrix.T, preferred_element_type=jnp.float32) + jnp.dot(
        up_grad, up_matrix.T, preferred_element_type=jnp.float32
    )
    return summed.astype(jnp.bfloat16)


def expert_tangent(tan_block, gate_pre, up_value, gate_matrix, up_matrix, down_matrix):
    gate_tan = jnp.dot(tan_block, gate_matrix, preferred_element_type=jnp.float32)
    up_tan = jnp.dot(tan_block, up_matrix, preferred_element_type=jnp.float32)
    activated, slope_val = silu_parts(gate_pre)
    hidden_tan = (slope_val * gate_tan * up_value + activated * up_tan).astype(jnp.bfloat16)
    return jnp.dot(hidden_tan, down_matrix, preferred_element_type=jnp.float32).astype(jnp.bfloat16)


class RoutedExperts:
    def __init__(self, index, own_rows, mask, upstream, route_ids, route_weights, w_gate, w_up, w_down):
        rows, routes = route_ids.shape
        self.experts = lax.axis_size("exp")
        self.routes = routes
        capacity = min(rows, 2 * rows * routes // self.experts)
        self.core, self.upstream, self.weights = index % 2, upstream[0], route_weights
        self.matrices = (w_gate, w_up, w_down)
        self.table = routing_table(route_ids, self.experts, capacity)
        self.got_cots = self.sent(self.upstream)
        wide = self.upstream.shape[1]
        self.mates = call(
            split_kernel,
            like(rows, 3 * wide // 2 + SIDE),
            [(mask, SMEM)] + hbm(*own_rows),
            [
                pltpu.VMEM((3, rows, wide // 2), BF),
                pltpu.VMEM((SIDE, rows), BF),
                pltpu.SemaphoreType.DMA((2, 3)),
                pltpu.SemaphoreType.DMA(()),
            ],
            limit=20,
            spaces=HBM,
        )

    def before(self):
        return [self.got_cots]

    def across(self, x):
        return lax.all_to_all(x, "exp", split_axis=0, concat_axis=0, tiled=True)

    def sent(self, x):
        return self.across(dispatch(self.table, x, self.routes, self.experts))

    def returned(self, x):
        back = self.across(x.reshape(self.got_cots.shape))
        return combine(self.table, back, self.weights)

    def forward(self, size, keep, got, after):
        attended = in_order(self.core, keep, got)
        rows, wide = attended.shape
        got_rows = self.sent(attended).reshape(-1, wide)
        expert_out, self.gate_pre, self.up_value = expert_forward(got_rows, *self.matrices)
        route_grad = expert_backward(
            self.got_cots.reshape(-1, wide), self.gate_pre, self.up_value, *self.matrices
        )
        attn_cot = (self.upstream.astype(F32) + self.returned(route_grad)).astype(BF)
        layer_out = (attended.astype(F32) + self.returned(expert_out)).astype(BF)

        def kernel(cot, kept, got, cot_keep, cot_send):
            width = kept.shape[1]
            for part, attended, out in ((this_core(), kept, cot_keep), (1 - this_core(), got, cot_send)):
                here = pl.ds(pl.multiple_of(part * width, width), width)
                out[...] = cot_payload(size, cot[:, here], attended[...])

        half = like(rows, wide // PAIR + SIDE)
        cot_keep, cot_send = call(
            kernel, (half, half), vmem(attn_cot, keep, got)
        )
        return cot_keep, cot_send, lambda *after: (layer_out, layer_out)

    def prefetch(self, after):
        return after

    def tangent(self, keep, got):
        rows = in_order(self.core, keep, got)
        got_rows = self.sent(rows).reshape(-1, rows.shape[1])
        out = expert_tangent(got_rows, self.gate_pre, self.up_value, *self.matrices)
        return (rows.astype(F32) + self.returned(out)).astype(BF)


def neighbours(whole, even, odd):
    return (
        moved(odd, 2 * PAIR),
        moved(whole, PAIR),
        moved(whole, -PAIR),
        moved(even, -2 * PAIR),
    )


def local(query, key, value, cotangent, route_ids, route_weights, block_mask, w_gate, w_up, w_down):
    rows, wide = query.shape[1:]
    width = wide // PAIR
    size = wide // HEADS
    heads = width // size
    index = lax.axis_index("ctx")
    core = index % PAIR

    pair = lax.axis_size("exp") == 2 and route_ids.shape[2] == 1
    experts = (PairExperts if pair else RoutedExperts)(
        index, (query, key, value), block_mask, cotangent, route_ids[0], route_weights[0], w_gate[0], w_up[0], w_down[0]
    )
    half, pairs = like(rows, width), like(2 * rows, width)
    q2, own, odd, side = call(
        join_kernel,
        (pairs, like(2 * rows, wide), like(rows, wide), like(2 * rows, SIDE)),
        vmem(query, key, value) + [(block_mask, SMEM)] + vmem(swapped(experts.mates)),
    )
    near, far = moved(own, PAIR), moved(odd, 2 * PAIR)
    three = like(3 * rows, width)
    q_other = swapped(q2, 2)
    q_up, q_down = call(shift_kernel, (three, three), vmem(q2, q_other))
    side, keep, send = call(
        functools.partial(attend_kernel, size),
        (
            like(2 * rows, SIDE),
            half,
            half,
        ),
        vmem(far, near, own, q2, side) + anywhere(q_up, *experts.before()),
        [pltpu.VMEM((PAIR, heads, rows), F32)],
        time=0.1,
    )
    got = swapped(send)
    q_below, q_above = moved(q_up, 2 * PAIR), moved(q_down, -2 * PAIR)
    q_before, q_after = call(around_kernel, (three, three), vmem(q_other, q_below, q_above))

    cot_keep, cot_send, layer = experts.forward(size, keep, got, (q_below, q_above))
    payload = wide // PAIR + SIDE
    co, co_even, co_odd = call(
        cots_kernel,
        (like(2 * rows, payload), like(rows, payload), like(rows, payload)),
        vmem(cot_keep, swapped(cot_send), side),
    )
    cfb, cnb, cna, cfa = neighbours(co, co_even, co_odd)

    layer_out, layer_done = layer(co, q_before)
    layer_done = experts.prefetch(layer_done)
    sums = like((WIN + 1) * rows, width, kind=F32)
    probs, probs_low, grads_q, q_keep, q_send, key_sums, value_sums = call(
        functools.partial(own_grads_kernel, size),
        (
            like(heads, PAIR, WIN * rows, rows),
            like(heads, PAIR, rows, WIN * rows),
            pairs, half, half, sums, sums,
        ),
        vmem(far, near, own, q2, co),
        [pltpu.VMEM((2, heads, rows), F32)] * 2,
        time=7,
    )
    q_got = swapped(q_send)
    kv_half = like(rows, 2 * width)
    kv_keep, kv_send, tan_keep, tan_send = call(
        functools.partial(grads_kernel, size),
        (kv_half, kv_half, half, half),
        vmem(far, near, own, q2, q_before, q_after, cfb, cnb, cna, cfa)
        + vmem(probs, probs_low, grads_q, key_sums, value_sums)
        + anywhere(layer_done),
        [pltpu.VMEM((6, heads, rows), F32)] * 2,
        time=16,
    )
    tan_got = swapped(tan_send)
    kv_got = swapped(kv_send)
    tangent_out = experts.tangent(tan_keep, tan_got)
    out = like(rows, wide)
    outs = call(gather_kernel, (out, out, out), vmem(q_keep, q_got, kv_keep, kv_got))
    return (layer_out[None], *(x[None] for x in outs), tangent_out[None])


def solution(mesh):
    return jax.shard_map(
        local,
        mesh=mesh,
        in_specs=(
            P("exp", "ctx", None),
            P("exp", "ctx", None),
            P("exp", "ctx", None),
            P("exp", "ctx", None),
            P("exp", "ctx", None),
            P("exp", "ctx", None),
            P("exp", "ctx", None),
            P("exp", None, None),
            P("exp", None, None),
            P("exp", None, None),
        ),
        out_specs=(
            P("exp", "ctx", None),
            P("exp", "ctx", None),
            P("exp", "ctx", None),
            P("exp", "ctx", None),
            P("exp", "ctx", None),
        ),
        check_vma=False,
    )
```

```python
import functools

import jax
import jax.numpy as jnp
from jax import lax
from jax.experimental import pallas as pl
from jax.experimental.pallas import tpu as pltpu
from jax.sharding import PartitionSpec as P

HEADS = 16
WIN = 4
PAIR = 2
SIDE = 128
FAR = 1e30
BF = jnp.bfloat16
F32 = jnp.float32
VMEM = pl.BlockSpec(memory_space=pltpu.VMEM)
SMEM = pl.BlockSpec(memory_space=pltpu.SMEM)
ANY = pl.BlockSpec(memory_space=pl.ANY)
HBM = pl.BlockSpec(memory_space=pltpu.HBM)


def moved(x, by):
    devices = lax.axis_size("ctx")
    pairs = [(i, i + by) for i in range(devices) if 0 <= i + by < devices]
    return lax.ppermute(x, "ctx", pairs)


def swapped(x, bit=1):
    return lax.ppermute(x, "ctx", [(i, i ^ bit) for i in range(lax.axis_size("ctx"))])


def this_core():
    return lax.axis_index("ctx") % PAIR


def this_lane():
    return lax.axis_index("ctx") // PAIR % 2


def crossed(x):
    return lax.ppermute(x, "exp", [(0, 1), (1, 0)])


def nn(a, b):
    return lax.dot_general(a, b, (((1,), (0,)), ((), ())), preferred_element_type=F32)


def nt(a, b):
    return lax.dot_general(a, b, (((1,), (1,)), ((), ())), preferred_element_type=F32)


def tn(a, b):
    return lax.dot_general(a, b, (((0,), (0,)), ((), ())), preferred_element_type=F32)


def silu_parts(gate_pre):
    sigmoid_val = jax.nn.sigmoid(gate_pre)
    return (gate_pre * sigmoid_val, sigmoid_val * (1.0 + gate_pre * (1.0 - sigmoid_val)))


LEVEL, DELTA = 8, 32


def terms_of(x):
    first = x.astype(BF).astype(F32)
    second = (x - first).astype(BF).astype(F32)
    return jnp.concatenate([first, second, x - first - second], axis=0)


def rows_of(side, at, heads):
    return sum(side[at + n * heads : at + (n + 1) * heads].astype(F32) for n in range(3))


def hidden_by(flag):
    return (1.0 - flag) * FAR


def causal_of(rows):
    return lax.broadcasted_iota(jnp.int32, (rows, rows), 1) >= lax.broadcasted_iota(
        jnp.int32, (rows, rows), 0
    )


def like(*shape, kind=BF):
    return jax.ShapeDtypeStruct(shape, kind)


def call(kernel, outs, args, scratch=(), time=1, limit=8, alias=None, spaces=None):
    return pl.pallas_call(
        kernel,
        out_shape=outs,
        in_specs=[space for _, space in args],
        out_specs=jax.tree.map(lambda _: VMEM, outs) if spaces is None else spaces,
        input_output_aliases=alias or {},
        scratch_shapes=list(scratch),
        compiler_params=pltpu.CompilerParams(vmem_limit_bytes=limit * 1024 * 1024),
        cost_estimate=pl.CostEstimate(flops=int(time * 1.1e9), bytes_accessed=0, transcendentals=0),
    )(*(array for array, _ in args))


def vmem(*arrays):
    return [(array, VMEM) for array in arrays]


def hbm(*arrays):
    return [(array, HBM) for array in arrays]


def anywhere(*arrays):
    return [(array, ANY) for array in arrays]


def tied(x, *after, time=0.01):
    out = like(*x.shape, kind=x.dtype)
    return call(lambda *refs: None, out, anywhere(x, *after), alias={0: 0}, spaces=ANY, limit=1, time=time)


def fetch(copies):
    for copy in copies:
        copy.start()
    return copies


def ready(copies):
    for copy in copies:
        copy.wait()


def through(moves, sems):
    ins = [pltpu.make_async_copy(source, buffer, sems.at[0, n]) for n, (source, buffer, _) in enumerate(moves)]
    outs = [pltpu.make_async_copy(buffer, target, sems.at[1, n]) for n, (_, buffer, target) in enumerate(moves)]
    fetch(ins)
    for first, second in zip(ins, outs):
        first.wait()
        second.start()
    ready(outs)


def columns_of(core, width):
    return [pl.ds(pl.multiple_of(n * width, width), width) for n in (core, 1 - core)]


def join_kernel(query, key, value, mask, got, q2, kv2, odd, side):
    core = this_core()
    rows, width = got.shape[0], q2.shape[1]
    mine, _ = columns_of(core, width)
    here, there = (pl.ds(pl.multiple_of(n * rows, rows), rows) for n in (core, 1 - core))
    q2[here, :] = query[0, :, mine]
    q2[there, :] = got[:, 0:width]
    kept = jnp.concatenate([key[0, :, mine], value[0, :, mine]], axis=1)
    sent = got[:, width : 3 * width]
    kv2[here, :] = kept
    kv2[there, :] = sent
    odd[...] = jnp.where(core == 1, kept, sent)
    side[here, :] = seen_by(mask, rows)
    side[there, :] = got[:, 3 * width :]


def seen_by(mask, rows):
    at = lax.broadcasted_iota(jnp.int32, (SIDE, rows), 0)
    sees = jnp.zeros((SIDE, rows), F32)
    for w in range(1, WIN):
        flag = jnp.where((mask[0, 0, w - 1] == 1) & (lax.axis_index("ctx") >= w), 1.0, 0.0)
        sees = jnp.where(at == w - 1, flag, sees)
    return sees.astype(BF)


def shift_kernel(own, other, up, down):
    lane = this_lane()
    rows = own.shape[0] // 2

    def put(first, last):
        up[0:rows] = first[rows : 2 * rows]
        up[rows : 3 * rows] = last[...]
        down[0 : 2 * rows] = first[...]
        down[2 * rows : 3 * rows] = last[0:rows]

    pl.when(lane == 0)(lambda: put(own, other))
    pl.when(lane != 0)(lambda: put(other, own))


def around_kernel(other, below, above, before, after):
    lane = this_lane()
    rows = other.shape[0] // 2

    @pl.when(lane == 0)
    def _():
        before[...] = below[...]
        after[0 : 2 * rows] = other[...]
        after[2 * rows :] = above[0:rows]

    @pl.when(lane != 0)
    def _():
        before[0:rows] = below[2 * rows :]
        before[rows:] = other[...]
        after[...] = above[...]


def split_moves(query, key, value, blocks, sent):
    width = query.shape[2] // 2
    _, others = columns_of(this_core(), width)
    return [
        (ref.at[0, :, others], blocks.at[n], sent.at[:, pl.ds(n * width, width)])
        for n, ref in enumerate((query, key, value))
    ]


def split_kernel(mask, query, key, value, sent, blocks, seen, sems, seen_sem):
    through(split_moves(query, key, value, blocks, sent), sems)
    send_seen(mask, seen, sent, seen_sem)


def send_seen(mask, seen, sent, sem):
    rows = seen.shape[1]
    seen[...] = seen_by(mask, rows)
    copy = pltpu.make_async_copy(seen, sent.at[:, pl.ds(sent.shape[1] - rows, rows)], sem)
    copy.start()
    copy.wait()


def half_moves(matrix, buffers, out):
    pieces, size = buffers.shape[:2]
    start = this_core() * pieces * size
    return [
        (matrix.at[pl.ds(start + n * size, size)], buffers.at[n], out.at[pl.ds(n * size, size)]) for n in range(pieces)
    ]


def inner_kernel(gate, up, inner, parts, sems):
    through([move for n, x in enumerate((gate, up)) for move in half_moves(x, parts.at[n], inner.at[n])], sems)


def cut_kernel(mask, down, query, key, value, after, down_half, sent, down_parts, blocks, seen, sems, seen_sem):
    moves = split_moves(query, key, value, blocks, sent) + half_moves(down, down_parts, down_half)
    through(moves, sems)
    send_seen(mask, seen, sent, seen_sem)


def cots_kernel(keep, got, side, whole, even, odd):
    core = this_core()
    rows, width = keep.shape[0], keep.shape[1] - SIDE
    for ref, block in ((keep, core), (got, 1 - core)):
        here = pl.ds(pl.multiple_of(block * rows, rows), rows)
        filled = (ref[:, width:].astype(F32) + side[here, :].astype(F32)).astype(BF)
        whole[here, 0:width] = ref[:, 0:width]
        whole[here, width:] = filled

        @pl.when(block == 0)
        def _():
            even[:, 0:width] = ref[:, 0:width]
            even[:, width:] = filled

        @pl.when(block == 1)
        def _():
            odd[:, 0:width] = ref[:, 0:width]
            odd[:, width:] = filled


def window_refs(far, near, own, rows):
    return {-3: (far, 0), -2: (near, 0), -1: (near, rows), 0: (own, 0), 1: (own, rows)}


def stacked(window, js, rows, here):
    return jnp.concatenate([window[j][0][pl.ds(window[j][1], rows), here] for j in js], axis=0)


def each_head(heads, one, step=2):
    def some(n, carry):
        for at in range(step):
            one(step * n + at)
        return carry

    lax.fori_loop(0, heads // step, some, 0)


def attend_kernel(size, far, near, own, q2, flags, *rest):
    side, keep, send, levels = rest[-4:]
    rows, width = far.shape[0], far.shape[1] // 2
    heads = width // size
    scale = size ** (-0.5)
    core = this_core()
    window = window_refs(far, near, own, rows)
    causal = causal_of(rows)
    seen = [flags[block * rows : (block + 1) * rows, :].astype(F32)[:LEVEL] for block in range(PAIR)]

    def one(head):
        here = pl.ds(pl.multiple_of(head * size, size), size)
        there = pl.ds(pl.multiple_of(width + head * size, size), size)
        outs = []
        for block in range(PAIR):
            js = list(range(block - WIN + 1, block + 1))
            q = q2[pl.ds(block * rows, rows), here]
            scores = nt(stacked(window, js, rows, here), q) * scale
            parts = [
                scores[n * rows : (n + 1) * rows] - hidden_by(seen[block][block - j - 1 : block - j])
                if j < block
                else jnp.where(causal, scores[n * rows : (n + 1) * rows], -FAR)
                for n, j in enumerate(js)
            ]
            scores = jnp.concatenate(parts, axis=0)
            top = jnp.max(scores, axis=0, keepdims=True)
            weights = jnp.exp(scores - top)
            total = jnp.sum(weights, axis=0, keepdims=True)
            probs = weights * (1.0 / total)
            levels[block, pl.ds(head, 1), :] = top + jnp.log(total)
            outs.append(tn(probs.astype(BF), stacked(window, js, rows, there)).astype(BF))
        keep[:, here] = jnp.where(core == 0, outs[0], outs[1])
        send[:, here] = jnp.where(core == 0, outs[1], outs[0])

    each_head(heads, one)
    for block in range(PAIR):
        filled = jnp.concatenate(
            [seen[block], terms_of(levels[block]), jnp.zeros((SIDE - LEVEL - 3 * heads, rows), F32)], axis=0
        )
        side[block * rows : (block + 1) * rows, :] = filled.astype(BF)


def scores_back(q, cot, level, delta, seen, keys, values, js, t, causal, scale):
    rows = q.shape[0]
    scores = nt(keys, q) * scale
    parts = []
    for n, j in enumerate(js):
        part = scores[n * rows : (n + 1) * rows]
        if j < t:
            part = part - (level + hidden_by(seen[t - j - 1 : t - j]))
        else:
            part = jnp.where(causal, part - level, -FAR)
        parts.append(part)
    probs = jnp.exp(jnp.concatenate(parts, axis=0))
    return probs, (probs * (nt(values, cot) - delta)).astype(BF)


def add_blocks(sums, js, terms, rows):
    for n, j in enumerate(js):
        term = terms[n * rows : (n + 1) * rows]
        sums[j] = sums[j] + term if j in sums else term


def own_grads_kernel(
    size, far, near, own, q2, co, probs_out, probs_low_out, grads_q, q_keep, q_send, key_sums, value_sums, levels, deltas,
):
    rows, width = far.shape[0], far.shape[1] // 2
    heads = width // size
    scale = size ** (-0.5)
    core = this_core()
    window = window_refs(far, near, own, rows)
    causal = causal_of(rows)
    sides = [co[t * rows : (t + 1) * rows, width:].astype(F32) for t in range(PAIR)]
    for t in range(PAIR):
        levels[t] = rows_of(sides[t], LEVEL, heads)
        deltas[t] = rows_of(sides[t], DELTA, heads)

    def one(head):
        here = pl.ds(pl.multiple_of(head * size, size), size)
        there = pl.ds(pl.multiple_of(width + head * size, size), size)
        keys_at, values_at, grads = {}, {}, []
        for t in range(PAIR):
            place = pl.ds(t * rows, rows)
            js = list(range(t - WIN + 1, t + 1))
            q, cot = q2[place, here], co[place, here]
            keys = stacked(window, js, rows, here)
            probs, score_grad = scores_back(
                q, cot, levels[t, pl.ds(head, 1), :], deltas[t, pl.ds(head, 1), :], sides[t][0:LEVEL],
                keys, stacked(window, js, rows, there), js, t, causal, scale,
            )
            probs_low = probs.astype(BF)
            probs_out[head, t] = probs_low
            probs_low_out[head, t] = probs_low.T
            add_blocks(keys_at, js, nn(score_grad, q), rows)
            add_blocks(values_at, js, nn(probs_low, cot), rows)
            grads.append((tn(score_grad, keys) * scale).astype(BF))
            grads_q[place, here] = grads[t]
        q_keep[:, here] = jnp.where(core == 0, grads[0], grads[1])
        q_send[:, here] = jnp.where(core == 0, grads[1], grads[0])
        for j in keys_at:
            place = pl.ds((j + WIN - 1) * rows, rows)
            key_sums[place, here] = keys_at[j]
            value_sums[place, here] = values_at[j]

    each_head(heads, one)


def grads_kernel(
    size, far, near, own, q2, q_before, q_after, cfb, cnb, cna, cfa, probs_in, probs_low_in, grads_q,
    key_sums, value_sums, after, keep, send, tans_keep, tans_send, levels, deltas,
):
    rows, width = far.shape[0], far.shape[1] // 2
    heads = width // size
    scale = size ** (-0.5)
    core = this_core()
    window = window_refs(far, near, own, rows)
    causal = causal_of(rows)
    others = (
        (-3, q_before, 0, cfb, 0), (-2, q_before, 1, cnb, 0), (-1, q_before, 2, cnb, 1),
        (2, q_after, 0, cna, 0), (3, q_after, 1, cna, 1), (4, q_after, 2, cfa, 0),
    )
    sides = [c_ref[half * rows : (half + 1) * rows, width:].astype(F32) for _, _, _, c_ref, half in others]
    for n, side in enumerate(sides):
        levels[n] = rows_of(side, LEVEL, heads)
        deltas[n] = rows_of(side, DELTA, heads)

    def one(head):
        at = pl.multiple_of(head * size, size)
        here = pl.ds(at, size)
        there = pl.ds(pl.multiple_of(width + at, size), size)
        blocks = range(1 - WIN, PAIR)
        keys_at = {j: key_sums[pl.ds((j + WIN - 1) * rows, rows), here] for j in blocks}
        values_at = {j: value_sums[pl.ds((j + WIN - 1) * rows, rows), here] for j in blocks}
        score_grads, probs_at, qs, cots = {}, {}, {}, {}
        for n, (t, q_ref, q_half, c_ref, half) in enumerate(others):
            js = list(range(max(1 - WIN, t - WIN + 1), min(1, t) + 1))
            q, cot = q_ref[pl.ds(q_half * rows, rows), here], c_ref[pl.ds(half * rows, rows), here]
            keys = stacked(window, js, rows, here)
            values = stacked(window, js, rows, there)
            probs, score_grad = scores_back(
                q, cot, levels[n, pl.ds(head, 1), :], deltas[n, pl.ds(head, 1), :], sides[n][0:8],
                keys, values, js, t, causal, scale,
            )
            probs = probs.astype(BF)
            qs[t], cots[t] = q, cot
            for m, j in enumerate(js):
                score_grads[j, t] = score_grad[m * rows : (m + 1) * rows]
                probs_at[j, t] = probs[m * rows : (m + 1) * rows]
        for j in blocks:
            ts = [t for t in qs if (j, t) in probs_at]
            keys_at[j] = keys_at[j] + nn(
                jnp.concatenate([score_grads[j, t] for t in ts], axis=1), jnp.concatenate([qs[t] for t in ts], axis=0)
            )
            values_at[j] = values_at[j] + nn(
                jnp.concatenate([probs_at[j, t] for t in ts], axis=1), jnp.concatenate([cots[t] for t in ts], axis=0)
            )
        key_grads = {j: (keys_at[j] * scale).astype(BF) for j in blocks}
        value_grads = {j: values_at[j].astype(BF) for j in blocks}
        tans = []
        for t in range(PAIR):
            place = pl.ds(t * rows, rows)
            js = list(range(t - WIN + 1, t + 1))
            keys = stacked(window, js, rows, here)
            probs = probs_in[head, t].astype(F32)
            both_keys = jnp.concatenate([keys, jnp.concatenate([key_grads[j] for j in js], axis=0)], axis=1)
            both_rows = jnp.concatenate([grads_q[place, here], q2[place, here]], axis=1)
            tan_values = jnp.concatenate([value_grads[j] for j in js], axis=0)
            score_tan = nt(both_keys, both_rows) * scale
            mean = jnp.sum(probs * score_tan, axis=0, keepdims=True)
            prob_tan = (probs * (score_tan - mean)).astype(BF)
            tan = tn(prob_tan, stacked(window, js, rows, there)) + nn(probs_low_in[head, t], tan_values)
            tans.append(tan.astype(BF))
        for grads, tans_out, mine, other in ((keep, tans_keep, 0, 1), (send, tans_send, 1, 0)):
            grads[:, here] = jnp.where(core == 0, key_grads[mine], key_grads[other])
            grads[:, there] = jnp.where(core == 0, value_grads[mine], value_grads[other])
            tans_out[:, here] = jnp.where(core == 0, tans[mine], tans[other])

    each_head(heads, one, 4)


def gather_kernel(q_keep, q_got, keep, got, out_q, out_k, out_v):
    core = this_core()
    width = q_keep.shape[1]
    for owner, q, kv in ((core, q_keep, keep), (1 - core, q_got, got)):
        columns = pl.ds(pl.multiple_of(owner * width, width), width)
        out_q[:, columns] = q[...]
        out_k[:, columns] = kv[:, 0:width]
        out_v[:, columns] = kv[:, width:]


def cot_payload(size, cot, attended):
    rows, width = cot.shape
    heads = width // size
    lanes = lax.broadcasted_iota(jnp.int32, (rows, SIDE), 1)
    sums = jnp.zeros((rows, SIDE), F32)
    for head in range(heads):
        here = slice(head * size, (head + 1) * size)
        delta = jnp.sum(cot[:, here].astype(F32) * attended[:, here].astype(F32), axis=1, keepdims=True)
        sums = jnp.where(lanes == head, delta, sums)
    blank = jnp.zeros((DELTA, rows), F32)
    rest = jnp.zeros((SIDE - DELTA - 3 * heads, rows), F32)
    side = jnp.concatenate([blank, terms_of(sums.T[0:heads]), rest], axis=0)
    return jnp.concatenate([cot, side.astype(BF)], axis=1)


def in_order(core, kept, got):
    return jnp.where(
        core == 0, jnp.concatenate([kept, got], axis=1), jnp.concatenate([got, kept], axis=1)
    )


def pair_of(a, b, bit):
    return jnp.where(bit == 0, a, b), jnp.where(bit == 0, b, a)


def down_of_other(hidden, core, over, over_s):
    half = hidden.shape[1] // 2
    mine, others = pair_of(hidden[:, :half], hidden[:, half:], core)
    return nn(mine, over[...]) + nn(others, over_s[...])


def hidden_grad_kernel(cot, down, out):
    out[...] = nt(cot[0], down[...])


def middle_of(chosen, gate_pre, up_value, back, hidden, slope_up, active):
    activated, slope = silu_parts(gate_pre)
    activated = activated * chosen
    slope = slope * up_value * chosen
    hidden[...] = (activated * up_value).astype(BF)
    slope_up[...] = slope
    active[...] = activated
    return (back * slope).astype(BF), (back * activated).astype(BF)


def own_expert_kernel(keep, got, picks, back, gate, up, sum_keep, sum_got, hidden, slope_up, active):
    mine, others = columns_of(this_core(), keep.shape[1])
    rows_keep, rows_got = keep[...], got[...]

    def inner(ref):
        return nn(rows_keep, ref[mine, :]) + nn(rows_got, ref[others, :])

    gate_grad, up_grad = middle_of(picks[:, 0:1], inner(gate), inner(up), back[...], hidden, slope_up, active)
    for here, out in ((mine, sum_keep), (others, sum_got)):
        out[...] = nt(gate_grad, gate[here, :]) + nt(up_grad, up[here, :])


def stream(pairs, sems):
    copies = fetch([pltpu.make_async_copy(source, buffer, sems.at[n]) for n, (source, buffer) in enumerate(pairs)])

    def waiting(n):
        def get():
            copies[n].wait()
            return pairs[n][1][...]

        return get

    return [waiting(n) for n in range(len(pairs))]


def other_expert_kernel(
    size, keep, got, cot, picks, sum_keep, sum_got, inner, inner_s, over, over_s,
    cot_keep, cot_send, hidden, slope_up, active,
):
    core = this_core()
    mine, others = columns_of(core, keep.shape[1])
    rows_keep, rows_got = keep[...], got[...]
    cots = cot[0]
    back = jnp.concatenate(pair_of(nt(cots, over[...]), nt(cots, over_s[...]), core), axis=1)
    gate_pre, up_value = (nn(rows_keep, inner[n]) + nn(rows_got, inner_s[n]) for n in range(2))
    gate_grad, up_grad = middle_of(picks[:, 1:2], gate_pre, up_value, back, hidden, slope_up, active)
    weight = picks[:, 2:3]
    for here, attended, so_far, ref, out in (
        (others, rows_got, sum_got, inner_s, cot_send),
        (mine, rows_keep, sum_keep, inner, cot_keep),
    ):
        summed = so_far[...] + nt(gate_grad, ref[0]) + nt(up_grad, ref[1])
        attn_cot = (cot[0, :, here].astype(F32) + summed.astype(BF).astype(F32) * weight).astype(BF)
        out[...] = cot_payload(size, attn_cot, attended)


def layer_kernel(keep, got, hidden_own, hidden, picks, down, over, over_s, *rest):
    out, done = rest[-2:]
    done[...] = jnp.zeros_like(done)
    core = this_core()
    rows_in = in_order(core, keep[...], got[...]).astype(F32)
    summed = nn(hidden_own[...], down[...]) + down_of_other(hidden[...], core, over, over_s)
    out[...] = (rows_in + summed.astype(BF).astype(F32) * picks[:, 2:3]).astype(BF)


def load_kernel(*refs):
    count = (len(refs) - 3) // 2
    sources, outs, done, sems = refs[:count], refs[count + 1 : 2 * count + 1], refs[-2], refs[-1]
    copies = fetch([pltpu.make_async_copy(a, b, sems.at[n]) for n, (a, b) in enumerate(zip(sources, outs))])
    done[...] = jnp.zeros_like(done)
    ready(copies)


def tangent_kernel(
    keep, got, slope_up_own, active_own, slope_up, active, picks, gate, up, inner, inner_s, down, over, over_s, out,
):
    core = this_core()
    rows_keep, rows_got = keep[...], got[...]
    rows_in = in_order(core, rows_keep, rows_got)
    hidden = slope_up_own[...] * nn(rows_in, gate[...]) + active_own[...] * nn(rows_in, up[...])
    summed = nn(hidden.astype(BF), down[...])
    gate_tan, up_tan = (nn(rows_keep, inner[n]) + nn(rows_got, inner_s[n]) for n in range(2))
    hidden = slope_up[...] * gate_tan + active[...] * up_tan
    summed = summed + down_of_other(hidden.astype(BF), core, over, over_s)
    out[...] = (rows_in.astype(F32) + summed.astype(BF).astype(F32) * picks[:, 2:3]).astype(BF)


class PairExperts:
    def __init__(self, index, own_rows, mask, upstream, route_ids, route_weights, w_gate, w_up, w_down):
        own = lax.axis_index("exp")
        self.upstream = upstream
        mine = (route_ids == own).astype(F32)
        self.picks = jnp.concatenate([mine, 1.0 - mine, route_weights], axis=1)
        rows, wide = upstream.shape[1:]
        units = w_gate.shape[1]
        pieces = 4
        inner = call(
            inner_kernel,
            like(2, wide // 2, units),
            hbm(w_gate, w_up),
            [pltpu.VMEM((2, pieces, wide // 2 // pieces, units), BF), pltpu.SemaphoreType.DMA((2, 2 * pieces))],
            limit=60,
            spaces=HBM,
        )
        down_half, self.mates = call(
            cut_kernel,
            (like(units // 2, wide), like(rows, 3 * wide // 2 + SIDE)),
            [(mask, SMEM)] + hbm(w_down, *own_rows) + anywhere(inner),
            [
                pltpu.VMEM((pieces, units // 2 // pieces, wide), BF),
                pltpu.VMEM((3, rows, wide // 2), BF),
                pltpu.VMEM((SIDE, rows), BF),
                pltpu.SemaphoreType.DMA((2, pieces + 3)),
                pltpu.SemaphoreType.DMA(()),
            ],
            limit=60,
            spaces=(HBM, HBM),
        )
        self.inner, self.over = crossed(inner), crossed(down_half)
        self.whole = (w_gate, w_up, w_down)
        self.rows, self.wide, self.units = rows, wide, units
        self.back_own = call(
            hidden_grad_kernel, like(rows, units, kind=F32), vmem(upstream, w_down), time=1.5
        )

    def before(self):
        return [self.back_own]

    def forward(self, size, keep, got, after):
        rows, wide, units = self.rows, self.wide, self.units
        w_gate, w_up, w_down = self.whole
        half, inner = like(rows, wide // PAIR + SIDE), like(rows, units, kind=F32)
        sums = like(rows, wide // PAIR, kind=F32)
        sum_keep, sum_got, hidden_own, *own_slopes = call(
            own_expert_kernel,
            (sums, sums, like(rows, units), inner, inner),
            vmem(keep, got, self.picks, self.back_own, w_gate, w_up),
            time=0.1,
        )
        inner_o, over = tied(self.inner, keep), tied(self.over, sum_keep)
        sum_got = tied(sum_got, *after, time=14)
        self.down = (w_down, over, swapped(over))
        self.inner = (inner_o, swapped(inner_o))
        cot_keep, cot_send, hidden, *slopes = call(
            functools.partial(other_expert_kernel, size),
            (half, half, like(rows, units), inner, inner),
            vmem(keep, got, self.upstream, self.picks, sum_keep, sum_got, *self.inner, *self.down[1:]),
            time=4.5,
        )
        self.slopes = own_slopes + slopes

        def layer(*after):
            return call(
                layer_kernel,
                (like(rows, wide), like(8, SIDE, kind=F32)),
                vmem(keep, got, hidden_own, hidden, self.picks, *self.down) + anywhere(*after),
                time=3,
            )

        return cot_keep, cot_send, layer

    def prefetch(self, after):
        arrays = (*self.inner, *self.down[1:])
        *loaded, done = call(
            load_kernel,
            (*(like(*x.shape) for x in arrays), like(8, SIDE, kind=F32)),
            hbm(*arrays) + anywhere(after),
            [pltpu.SemaphoreType.DMA((len(arrays),))],
            time=2,
        )
        self.inner, self.down = tuple(loaded[:2]), (self.down[0], *loaded[2:])
        return done

    def tangent(self, keep, got):
        return call(
            tangent_kernel,
            like(self.rows, self.wide),
            vmem(keep, got, *self.slopes, self.picks, *self.whole[:2], *self.inner, *self.down),
            time=4.5,
        )


def routing_table(route_rows, experts, capacity):
    flat_ids = route_rows.reshape(-1)
    one_hot = (flat_ids[:, None] == jnp.arange(experts, dtype=jnp.int32)[None, :]).astype(jnp.int32)
    slot_rank = jnp.sum((jnp.cumsum(one_hot, axis=0) - one_hot) * one_hot, axis=1)
    target = flat_ids * capacity + slot_rank
    return (jnp.arange(experts * capacity, dtype=jnp.int32)[:, None] == target[None, :]).astype(
        jnp.bfloat16
    )


def dispatch(slot_table, row_block, routes, experts):
    pair_rows = jnp.repeat(row_block, routes, axis=0)
    sent = jnp.dot(slot_table, pair_rows, preferred_element_type=jnp.float32).astype(jnp.bfloat16)
    return sent.reshape(experts, -1, row_block.shape[1])


def combine(slot_table, returned, weights):
    rows_here, routes = weights.shape
    pair_vals = jnp.dot(
        slot_table.T, returned.reshape(-1, returned.shape[2]), preferred_element_type=jnp.float32
    )
    return jnp.sum(pair_vals.reshape(rows_here, routes, -1) * weights[:, :, None], axis=1)


def expert_forward(row_block, gate_matrix, up_matrix, down_matrix):
    gate_pre = jnp.dot(row_block, gate_matrix, preferred_element_type=jnp.float32)
    up_value = jnp.dot(row_block, up_matrix, preferred_element_type=jnp.float32)
    activated, slope_val = silu_parts(gate_pre)
    hidden = (activated * up_value).astype(jnp.bfloat16)
    return (
        jnp.dot(hidden, down_matrix, preferred_element_type=jnp.float32).astype(jnp.bfloat16),
        gate_pre,
        up_value,
    )


def expert_backward(cot_block, gate_pre, up_value, gate_matrix, up_matrix, down_matrix):
    hidden_grad = jnp.dot(cot_block, down_matrix.T, preferred_element_type=jnp.float32)
    activated, slope_val = silu_parts(gate_pre)
    gate_grad = (hidden_grad * up_value * slope_val).astype(jnp.bfloat16)
    up_grad = (hidden_grad * activated).astype(jnp.bfloat16)
    summed = jnp.dot(gate_grad, gate_matrix.T, preferred_element_type=jnp.float32) + jnp.dot(
        up_grad, up_matrix.T, preferred_element_type=jnp.float32
    )
    return summed.astype(jnp.bfloat16)


def expert_tangent(tan_block, gate_pre, up_value, gate_matrix, up_matrix, down_matrix):
    gate_tan = jnp.dot(tan_block, gate_matrix, preferred_element_type=jnp.float32)
    up_tan = jnp.dot(tan_block, up_matrix, preferred_element_type=jnp.float32)
    activated, slope_val = silu_parts(gate_pre)
    hidden_tan = (slope_val * gate_tan * up_value + activated * up_tan).astype(jnp.bfloat16)
    return jnp.dot(hidden_tan, down_matrix, preferred_element_type=jnp.float32).astype(jnp.bfloat16)


class RoutedExperts:
    def __init__(self, index, own_rows, mask, upstream, route_ids, route_weights, w_gate, w_up, w_down):
        rows, routes = route_ids.shape
        self.experts = lax.axis_size("exp")
        self.routes = routes
        capacity = min(rows, 2 * rows * routes // self.experts)
        self.core, self.upstream, self.weights = index % 2, upstream[0], route_weights
        self.matrices = (w_gate, w_up, w_down)
        self.table = routing_table(route_ids, self.experts, capacity)
        self.got_cots = self.sent(self.upstream)
        wide = self.upstream.shape[1]
        self.mates = call(
            split_kernel,
            like(rows, 3 * wide // 2 + SIDE),
            [(mask, SMEM)] + hbm(*own_rows),
            [
                pltpu.VMEM((3, rows, wide // 2), BF),
                pltpu.VMEM((SIDE, rows), BF),
                pltpu.SemaphoreType.DMA((2, 3)),
                pltpu.SemaphoreType.DMA(()),
            ],
            limit=20,
            spaces=HBM,
        )

    def before(self):
        return [self.got_cots]

    def across(self, x):
        return lax.all_to_all(x, "exp", split_axis=0, concat_axis=0, tiled=True)

    def sent(self, x):
        return self.across(dispatch(self.table, x, self.routes, self.experts))

    def returned(self, x):
        back = self.across(x.reshape(self.got_cots.shape))
        return combine(self.table, back, self.weights)

    def forward(self, size, keep, got, after):
        attended = in_order(self.core, keep, got)
        rows, wide = attended.shape
        got_rows = self.sent(attended).reshape(-1, wide)
        expert_out, self.gate_pre, self.up_value = expert_forward(got_rows, *self.matrices)
        route_grad = expert_backward(
            self.got_cots.reshape(-1, wide), self.gate_pre, self.up_value, *self.matrices
        )
        attn_cot = (self.upstream.astype(F32) + self.returned(route_grad)).astype(BF)
        layer_out = (attended.astype(F32) + self.returned(expert_out)).astype(BF)

        def kernel(cot, kept, got, cot_keep, cot_send):
            width = kept.shape[1]
            for part, attended, out in ((this_core(), kept, cot_keep), (1 - this_core(), got, cot_send)):
                here = pl.ds(pl.multiple_of(part * width, width), width)
                out[...] = cot_payload(size, cot[:, here], attended[...])

        half = like(rows, wide // PAIR + SIDE)
        cot_keep, cot_send = call(
            kernel, (half, half), vmem(attn_cot, keep, got)
        )
        return cot_keep, cot_send, lambda *after: (layer_out, layer_out)

    def prefetch(self, after):
        return after

    def tangent(self, keep, got):
        rows = in_order(self.core, keep, got)
        got_rows = self.sent(rows).reshape(-1, rows.shape[1])
        out = expert_tangent(got_rows, self.gate_pre, self.up_value, *self.matrices)
        return (rows.astype(F32) + self.returned(out)).astype(BF)


def neighbours(whole, even, odd):
    return (
        moved(odd, 2 * PAIR),
        moved(whole, PAIR),
        moved(whole, -PAIR),
        moved(even, -2 * PAIR),
    )


def local(query, key, value, cotangent, route_ids, route_weights, block_mask, w_gate, w_up, w_down):
    rows, wide = query.shape[1:]
    width = wide // PAIR
    size = wide // HEADS
    heads = width // size
    index = lax.axis_index("ctx")
    core = index % PAIR

    pair = lax.axis_size("exp") == 2 and route_ids.shape[2] == 1
    experts = (PairExperts if pair else RoutedExperts)(
        index, (query, key, value), block_mask, cotangent, route_ids[0], route_weights[0], w_gate[0], w_up[0], w_down[0]
    )
    half, pairs = like(rows, width), like(2 * rows, width)
    q2, own, odd, side = call(
        join_kernel,
        (pairs, like(2 * rows, wide), like(rows, wide), like(2 * rows, SIDE)),
        vmem(query, key, value) + [(block_mask, SMEM)] + vmem(swapped(experts.mates)),
    )
    near, far = moved(own, PAIR), moved(odd, 2 * PAIR)
    three = like(3 * rows, width)
    q_other = swapped(q2, 2)
    q_up, q_down = call(shift_kernel, (three, three), vmem(q2, q_other))
    side, keep, send = call(
        functools.partial(attend_kernel, size),
        (
            like(2 * rows, SIDE),
            half,
            half,
        ),
        vmem(far, near, own, q2, side) + anywhere(q_up, *experts.before()),
        [pltpu.VMEM((PAIR, heads, rows), F32)],
        time=0.1,
    )
    got = swapped(send)
    q_below, q_above = moved(q_up, 2 * PAIR), moved(q_down, -2 * PAIR)
    q_before, q_after = call(around_kernel, (three, three), vmem(q_other, q_below, q_above))

    cot_keep, cot_send, layer = experts.forward(size, keep, got, (q_below, q_above))
    payload = wide // PAIR + SIDE
    co, co_even, co_odd = call(
        cots_kernel,
        (like(2 * rows, payload), like(rows, payload), like(rows, payload)),
        vmem(cot_keep, swapped(cot_send), side),
    )
    cfb, cnb, cna, cfa = neighbours(co, co_even, co_odd)

    layer_out, layer_done = layer(co, q_before)
    layer_done = experts.prefetch(layer_done)
    sums = like((WIN + 1) * rows, width, kind=F32)
    probs, probs_low, grads_q, q_keep, q_send, key_sums, value_sums = call(
        functools.partial(own_grads_kernel, size),
        (
            like(heads, PAIR, WIN * rows, rows),
            like(heads, PAIR, rows, WIN * rows),
            pairs, half, half, sums, sums,
        ),
        vmem(far, near, own, q2, co),
        [pltpu.VMEM((2, heads, rows), F32)] * 2,
        time=7,
    )
    q_got = swapped(q_send)
    kv_half = like(rows, 2 * width)
    kv_keep, kv_send, tan_keep, tan_send = call(
        functools.partial(grads_kernel, size),
        (kv_half, kv_half, half, half),
        vmem(far, near, own, q2, q_before, q_after, cfb, cnb, cna, cfa)
        + vmem(probs, probs_low, grads_q, key_sums, value_sums)
        + anywhere(layer_done),
        [pltpu.VMEM((6, heads, rows), F32)] * 2,
        time=16,
    )
    tan_got = swapped(tan_send)
    kv_got = swapped(kv_send)
    tangent_out = experts.tangent(tan_keep, tan_got)
    out = like(rows, wide)
    outs = call(gather_kernel, (out, out, out), vmem(q_keep, q_got, kv_keep, kv_got))
    return (layer_out[None], *(x[None] for x in outs), tangent_out[None])


def solution(mesh):
    return jax.shard_map(
        local,
        mesh=mesh,
        in_specs=(
            P("exp", "ctx", None),
            P("exp", "ctx", None),
            P("exp", "ctx", None),
            P("exp", "ctx", None),
            P("exp", "ctx", None),
            P("exp", "ctx", None),
            P("exp", "ctx", None),
            P("exp", None, None),
            P("exp", None, None),
            P("exp", None, None),
        ),
        out_specs=(
            P("exp", "ctx", None),
            P("exp", "ctx", None),
            P("exp", "ctx", None),
            P("exp", "ctx", None),
            P("exp", "ctx", None),
        ),
        check_vma=False,
    )
```
